128 devices in a mesh: gx: 8 (over x, y_lo), gy: 16 (over y_hi, z, core).
Axes of the slice: x: 4, y: 4 (y_hi: 2, y_lo: 2; y = y_hi * 2 + y_lo), z: 4, core: 2. Of those that a mesh axis runs over, the one named last changes fastest.
Arguments:
- fields: float32 [4, 128, 128, 2048], P(None, None, 'gx', 'gy'), may hold values from -6 to 6
- courant: float32 [2, 128, 128, 2048], P(None, None, 'gx', 'gy'), may hold values from -0.3 to 0.3
- sun_columns: int32 [8, 16, 2048], P('gx', 'gy'), may hold values from -1 to 2047, as said below
- rad_w1: bfloat16 [512, 1024], replicated, may hold values from -0.25 to 0.25
- rad_b1: float32 [1024], replicated, may hold values from -3 to 3
- rad_w2: bfloat16 [1024, 1024], replicated, may hold values from -0.1875 to 0.1875
- rad_b2: float32 [1024], replicated, may hold values from -3 to 3
- rad_w3: bfloat16 [1024, 512], replicated, may hold values from -0.1875 to 0.1875
- segment_route: int32 [2, 8, 16, 1024], P(None, 'gx', 'gy'), may hold values from 0 to 1023, as said below
- regrid_weights: bfloat16 [8, 16, 16, 128, 128], P('gx', 'gy'), may hold values from 0 to 1, as said below
- chem_w1: bfloat16 [256, 1024], replicated, may hold values from -0.375 to 0.375
- chem_b1: float32 [1024], replicated, may hold values from -3 to 3
- chem_w2: bfloat16 [1024, 256], replicated, may hold values from -0.1875 to 0.1875
Outputs:
- fields_out: float32 [4, 128, 128, 2048], P(None, None, 'gx', 'gy')
- chem_tendency: bfloat16 [8, 16, 2048, 256], P('gx', 'gy')
The draws below stay inside these ranges and needn't reach their ends.
Inputs may be any that keep to these rules, and one draw needn't show every extreme that they name: `sun_columns`: in each tile the live entries come first and are distinct columns of the tile; the rest are -1. Counting a tile's sunlit blocks as its live entries divided by 128, rounded up, a tile and the tile with the same first index and second index 8 further (modulo 16) have exactly 16 sunlit blocks together. `segment_route`: entry 0 is the receiving tile, entry 1 the slot there. Every tile receives exactly 1024 segments, one in each slot; no tile receives more than 16 segments from one tile, and some tile receives exactly 16 from one tile. `regrid_weights`: entries are nonnegative and each row sums to one up to rounding.
All inputs are finite; a program needn't handle non-finite values.
Results may differ from the reference program's by a relative error of at most 0.0075.
Values may be sent and summed in bfloat16 or wider, within the bound.
No kernel may reach another device: no remote copies, remote signals or barrier semaphores. Data moves between devices by JAX's collectives and lax.ppermute only.
A program may use at most 128 MiB of HBM per device.

```python
import jax
import jax.numpy as jnp
from jax import lax

LEV = 128
NF = 4
RAD_HID = 1024
CHEM_HID = 1024
BLOCK = 128
SEG = 2
STEPS = 2
RAD_IN = 512
CHEM_IN = 256
COLS = 2048
BLOCKS = 16
NSEG = 1024
TX = 8
TY = 16
CAP = 16
NLAT = 128
NLON = 2048


def draw_sun_columns(key, part):
    half_tiles = TY // 2
    key_low = jax.random.fold_in(key, 101)
    key_spare = jax.random.fold_in(key, 102)
    key_order = jax.random.fold_in(key, 103)
    low_blocks = jax.random.randint(key_low, (TX, half_tiles), 0, BLOCKS + 1)
    low_blocks = low_blocks.at[0, 0].set(BLOCKS)
    block_counts = jnp.concatenate([low_blocks, BLOCKS - low_blocks], axis=1)
    spare = jax.random.randint(key_spare, (TX, TY), 0, BLOCK)
    lit_count = jnp.where(block_counts > 0, block_counts * BLOCK - spare, 0)
    order_keys = jax.random.split(key_order, TX * TY)
    orders = jax.vmap(jax.random.permutation, in_axes=(0, None))(order_keys, COLS).reshape(TX, TY, COLS)
    slot_index = jnp.arange(COLS)
    return jnp.where(slot_index[None, None, :] < lit_count[:, :, None], orders, -1).astype(jnp.int32)


def draw_segment_route(key, part):
    tile_count = TX * TY
    multiset = jnp.arange(tile_count * CAP, dtype=jnp.int32) // CAP
    remaining = jax.random.permutation(jax.random.fold_in(key, 201), multiset[CAP:])
    offsets = jnp.concatenate([multiset[:CAP], remaining])[:NSEG]
    offsets = (offsets + jax.random.randint(jax.random.fold_in(key, 202), (), 0, tile_count)) % tile_count
    first_perm = jax.random.permutation(jax.random.fold_in(key, 203), tile_count)
    second_perm = jax.random.permutation(jax.random.fold_in(key, 204), tile_count)
    segment_perm = jax.random.permutation(jax.random.fold_in(key, 205), NSEG)
    slot_perm = jax.random.permutation(jax.random.fold_in(key, 206), NSEG)
    source_turn = jax.random.randint(jax.random.fold_in(key, 207), (tile_count,), 0, NSEG)
    target_turn = jax.random.randint(jax.random.fold_in(key, 208), (tile_count,), 0, NSEG)
    segment_index = jnp.arange(NSEG)
    inverse = jnp.argsort(segment_perm)
    which = inverse[(segment_index[None, :] - source_turn[:, None]) % NSEG]
    destination = second_perm[(first_perm[:, None] + offsets[which]) % tile_count]
    arrival = (slot_perm[which] + target_turn[destination]) % NSEG
    return jnp.stack([destination, arrival]).reshape(2, TX, TY, NSEG).astype(jnp.int32)


def draw_regrid_weights(key, part):
    shape = (TX, TY, BLOCKS, BLOCK, BLOCK)
    raw_weights = jax.random.uniform(key, shape, jnp.float32, 0.0, 1.0)
    raw_weights = raw_weights + 0.5 * BLOCK * jnp.eye(BLOCK, dtype=jnp.float32)
    return (raw_weights / jnp.sum(raw_weights, axis=-1, keepdims=True)).astype(jnp.bfloat16)


def block_levels(own_key, dims, shards, low, high):
    factor_of, own = 1.0, jax.random.fold_in(own_key, 6)
    for axis_at, parts in shards:
        heights = jnp.exp(jax.random.uniform(jax.random.fold_in(own, axis_at), (parts,), jnp.float32, low / len(shards), high / len(shards)))
        factor_of = factor_of * jnp.repeat(heights, dims[axis_at] // parts).reshape([-1 if axis == axis_at else 1 for axis in range(len(dims))])
    return factor_of


def scatter_about(own_key, extent, scale, bound, cuts=(), kind=jnp.bfloat16):
    entries = scale * jax.random.normal(own_key, extent, jnp.float32)
    if cuts:
        entries = entries * block_levels(own_key, extent, cuts, -0.22, 0.18)
    return jnp.clip(entries, -bound, bound).astype(kind)


def setup_inputs(seed: int = 0) -> dict:
    key_list = jax.random.split(jax.random.key(seed), 14)
    fields = scatter_about(key_list[0], (NF, LEV, NLAT, NLON), 1.0, 6.0, ((2, 8), (3, 16)), jnp.float32)
    courant = jnp.clip(jax.random.uniform(key_list[1], (2, LEV, NLAT, NLON), jnp.float32, -0.3, 0.3) * block_levels(key_list[1], (2, LEV, NLAT, NLON), ((2, 8), (3, 16)), -0.4, 0.0), -0.3, 0.3)
    sun_columns = draw_sun_columns(jax.random.fold_in(key_list[13], 71), 0)
    rad_w1 = scatter_about(key_list[3], (RAD_IN, RAD_HID), RAD_IN ** -0.5, 0.25)
    rad_b1 = scatter_about(key_list[4], (RAD_HID,), 0.5, 3.0, (), jnp.float32)
    rad_w2 = scatter_about(key_list[5], (RAD_HID, RAD_HID), RAD_HID ** -0.5, 0.1875)
    rad_b2 = scatter_about(key_list[6], (RAD_HID,), 0.5, 3.0, (), jnp.float32)
    rad_w3 = scatter_about(key_list[7], (RAD_HID, RAD_IN), RAD_HID ** -0.5, 0.1875)
    segment_route = draw_segment_route(jax.random.fold_in(key_list[13], 71), 0)
    regrid_weights = draw_regrid_weights(jax.random.fold_in(key_list[13], 71), 0)
    chem_w1 = scatter_about(key_list[10], (CHEM_IN, CHEM_HID), CHEM_IN ** -0.5, 0.375)
    chem_b1 = scatter_about(key_list[11], (CHEM_HID,), 0.5, 3.0, (), jnp.float32)
    chem_w2 = scatter_about(key_list[12], (CHEM_HID, CHEM_IN), CHEM_HID ** -0.5, 0.1875)
    return {"fields": fields, "courant": courant, "sun_columns": sun_columns, "rad_w1": rad_w1, "rad_b1": rad_b1, "rad_w2": rad_w2, "rad_b2": rad_b2, "rad_w3": rad_w3, "segment_route": segment_route, "regrid_weights": regrid_weights, "chem_w1": chem_w1, "chem_b1": chem_b1, "chem_w2": chem_w2}


def advect(fields, courant):
    lat_count = fields.shape[2]
    cells_lat = jnp.pad(fields, ((0, 0), (0, 0), (1, 1), (0, 0)))
    speed_lat = jnp.pad(courant[0], ((0, 0), (1, 1), (0, 0)))
    lower_row = jnp.arange(lat_count + 1) - 1
    valid_face = ((lower_row >= 0) & (lower_row <= lat_count - 2)).astype(jnp.float32)
    face_lat = 0.5 * (speed_lat[:, :-1] + speed_lat[:, 1:]) * valid_face[None, :, None]
    flux_lat = jnp.maximum(face_lat, 0.0) * cells_lat[:, :, :-1] + jnp.minimum(face_lat, 0.0) * cells_lat[:, :, 1:]
    cells_lon = jnp.pad(fields, ((0, 0), (0, 0), (0, 0), (1, 1)), mode="wrap")
    speed_lon = jnp.pad(courant[1], ((0, 0), (0, 0), (1, 1)), mode="wrap")
    face_lon = 0.5 * (speed_lon[:, :, :-1] + speed_lon[:, :, 1:])
    flux_lon = jnp.maximum(face_lon, 0.0) * cells_lon[..., :-1] + jnp.minimum(face_lon, 0.0) * cells_lon[..., 1:]
    return fields - (flux_lat[:, :, 1:] - flux_lat[:, :, :-1]) - (flux_lon[..., 1:] - flux_lon[..., :-1])


def radiation_net(features, rad_w1, rad_b1, rad_w2, rad_b2, rad_w3):
    contract = (((0,), (0,)), ((), ()))
    layer_one = jax.nn.silu(lax.dot_general(rad_w1, features, contract, preferred_element_type=jnp.float32) + rad_b1[:, None]).astype(jnp.bfloat16)
    layer_two = jax.nn.silu(lax.dot_general(rad_w2, layer_one, contract, preferred_element_type=jnp.float32) + rad_b2[:, None]).astype(jnp.bfloat16)
    return lax.dot_general(rad_w3, layer_two, contract, preferred_element_type=jnp.float32)


def radiate(fields, sun_columns, rad_w1, rad_b1, rad_w2, rad_b2, rad_w3):
    field_count, levels, lat_count, lon_count = fields.shape
    tile_rows = lat_count // TX
    tile_cols = lon_count // TY
    tiled = fields.reshape(field_count * levels, TX, tile_rows, TY, tile_cols)
    tiled = tiled.transpose(1, 3, 0, 2, 4).reshape(TX * TY, field_count * levels, tile_rows * tile_cols)

    def one_tile(tile_pair):
        tile_fields, slot_list = tile_pair
        lit_mask = slot_list >= 0
        safe_index = jnp.where(lit_mask, slot_list, 0).astype(jnp.int32)
        features = (jnp.take(tile_fields, safe_index, axis=1) * lit_mask[None, :]).astype(jnp.bfloat16)
        heating = radiation_net(features, rad_w1, rad_b1, rad_w2, rad_b2, rad_w3)
        return jnp.zeros_like(tile_fields).at[:, safe_index].add(jnp.where(lit_mask[None, :], heating, 0.0))

    tendency = lax.map(one_tile, (tiled, sun_columns.reshape(TX * TY, -1)))
    tendency = tendency.reshape(TX, TY, field_count * levels, tile_rows, tile_cols).transpose(2, 0, 3, 1, 4)
    return fields + tendency.reshape(fields.shape)


def chemistry(fields, segment_route, regrid_weights, chem_w1, chem_b1, chem_w2):
    levels = fields.shape[1]
    tile_rows = fields.shape[2] // TX
    tile_cols = fields.shape[3] // TY
    source = fields[2:4].astype(jnp.bfloat16)
    tiled = source.reshape(2 * levels, TX, tile_rows, TY, tile_cols).transpose(1, 3, 2, 4, 0)
    tiled = tiled.reshape(TX * TY * NSEG, SEG, 2 * levels)
    placed = jnp.zeros((TX * TY, NSEG, SEG, 2 * levels), jnp.bfloat16)
    placed = placed.at[segment_route[0].reshape(-1).astype(jnp.int32), segment_route[1].reshape(-1).astype(jnp.int32)].set(tiled)
    chem_cells = placed.reshape(TX * TY, BLOCKS, BLOCK, 2 * levels)
    mixing = regrid_weights.reshape(TX * TY, BLOCKS, BLOCK, BLOCK)
    regridded = jnp.einsum("tjab,tjbf->tjaf", mixing.astype(jnp.float32), chem_cells.astype(jnp.float32)).astype(jnp.bfloat16)
    flat_cells = regridded.reshape(-1, 2 * levels)
    chem_hidden = jax.nn.silu(jnp.dot(flat_cells, chem_w1, preferred_element_type=jnp.float32) + chem_b1).astype(jnp.bfloat16)
    output = jnp.dot(chem_hidden, chem_w2, preferred_element_type=jnp.float32).astype(jnp.bfloat16)
    return output.reshape(TX, TY, tile_rows * tile_cols, 2 * levels)


def reference(fields, courant, sun_columns, rad_w1, rad_b1, rad_w2, rad_b2, rad_w3, segment_route, regrid_weights, chem_w1, chem_b1, chem_w2):
    current = fields
    for repeat in range(STEPS):
        current = advect(current, courant)
        current = radiate(current, sun_columns, rad_w1, rad_b1, rad_w2, rad_b2, rad_w3)
    chem_output = chemistry(current, segment_route, regrid_weights, chem_w1, chem_b1, chem_w2)
    return current, chem_output
```

```python
import jax
import jax.numpy as jnp
from jax import lax
from jax.experimental import pallas as pl
from jax.experimental.pallas import tpu as pltpu
from jax.sharding import PartitionSpec as P

F32 = jnp.float32
BF16 = jnp.bfloat16
LANES = 128
FIELDS = 4
ROWS = 16
COLS = 128
FEAT = FIELDS * LANES
CELLS = ROWS * COLS
SEGS = CELLS // 2
EDGE = 8
INNER = COLS - 2 * EDGE
GROUP = 2
RIM = 2 * COLS + (ROWS - 2) * 2 * EDGE
VMEM_LIMIT = 20 * 1024 * 1024

VMEM = pl.BlockSpec(memory_space=pltpu.VMEM)
SMEM = pl.BlockSpec(memory_space=pltpu.SMEM)
ANY = pl.BlockSpec(memory_space=pl.ANY)


def vmem_out(shape, dtype):
    return pltpu.VMEM(shape, dtype)


def params():
    return pltpu.CompilerParams(vmem_limit_bytes=VMEM_LIMIT)


def cost(flops, bytes_accessed=0):
    return pl.CostEstimate(flops=flops, bytes_accessed=bytes_accessed, transcendentals=0)


def dot(a, b):
    return jnp.dot(a, b, preferred_element_type=F32)


def dot_nt(a, b):
    return lax.dot_general(a, b, (((1,), (1,)), ((), ())), preferred_element_type=F32)


def silu(u):
    half = 0.5 * u
    return half + half * jnp.tanh(half)


def iota(shape, dim):
    return lax.broadcasted_iota(jnp.int32, shape, dim)


def turn_kernel(f_ref, c_ref, t_ref, cc_ref, row_lo_ref, row_hi_ref, col_lo_ref, col_hi_ref):
    step = pl.program_id(0)

    @pl.when(step < FIELDS)
    def _():
        for r in range(ROWS):
            block = f_ref[pl.ds(r, LANES, stride=ROWS), :].T
            t_ref[0, r] = block
            if r == 0:
                row_lo_ref[...] = block.astype(BF16)
            if r == ROWS - 1:
                row_hi_ref[...] = block.astype(BF16)
        col_lo_ref[...] = t_ref[0, :, 0, :].astype(BF16)
        col_hi_ref[...] = t_ref[0, :, COLS - 1, :].astype(BF16)

    @pl.when(step >= FIELDS)
    def _():
        for r in range(ROWS):
            cc_ref[0, r] = c_ref[pl.ds(r, LANES, stride=ROWS), :].T

    @pl.when(step == FIELDS)
    def _():
        row_lo_ref[...] = cc_ref[0, 0].astype(BF16)
        row_hi_ref[...] = cc_ref[0, ROWS - 1].astype(BF16)

    @pl.when(step == FIELDS + 1)
    def _():
        col_lo_ref[...] = cc_ref[0, :, 0, :].astype(BF16)
        col_hi_ref[...] = cc_ref[0, :, COLS - 1, :].astype(BF16)


def turn(fields, courant):
    flat_f = fields.reshape(FIELDS * LANES * ROWS, COLS)
    flat_c = courant.reshape(2 * LANES * ROWS, COLS)
    field_at = lambda i: jnp.minimum(i, FIELDS - 1)
    speed_at = lambda i: jnp.maximum(i - FIELDS, 0)
    halo_at = lambda i: jnp.minimum(i, FIELDS)
    return pl.pallas_call(
        turn_kernel,
        grid=(FIELDS + 2,),
        in_specs=[
            pl.BlockSpec((LANES * ROWS, COLS), lambda i: (field_at(i), 0)),
            pl.BlockSpec((LANES * ROWS, COLS), lambda i: (speed_at(i), 0)),
        ],
        out_specs=[
            pl.BlockSpec((1, ROWS, COLS, LANES), lambda i: (field_at(i), 0, 0, 0)),
            pl.BlockSpec((1, ROWS, COLS, LANES), lambda i: (speed_at(i), 0, 0, 0)),
            pl.BlockSpec((COLS, LANES), lambda i: (0, halo_at(i))),
            pl.BlockSpec((COLS, LANES), lambda i: (0, halo_at(i))),
            pl.BlockSpec((ROWS, LANES), lambda i: (0, halo_at(i))),
            pl.BlockSpec((ROWS, LANES), lambda i: (0, halo_at(i))),
        ],
        out_shape=[
            jax.ShapeDtypeStruct((FIELDS, ROWS, COLS, LANES), F32),
            jax.ShapeDtypeStruct((2, ROWS, COLS, LANES), F32),
            jax.ShapeDtypeStruct((COLS, FEAT + LANES), BF16),
            jax.ShapeDtypeStruct((COLS, FEAT + LANES), BF16),
            jax.ShapeDtypeStruct((ROWS, FEAT + LANES), BF16),
            jax.ShapeDtypeStruct((ROWS, FEAT + LANES), BF16),
        ],
        compiler_params=params(),
        cost_estimate=cost(20_000_000, 12 << 20),
        name="turn",
    )(flat_f, flat_c)


def plan_kernel(sun_ref, route_ref, regrid_ref, mask_ref, place_ref, tags_ref, mix_ref):
    slots = sun_ref[...]
    low = (iota((COLS, CELLS), 0) == (slots & (COLS - 1))).astype(F32).astype(BF16)
    high = (iota((LANES, CELLS), 0) == (slots >> 7)).astype(F32).astype(BF16)
    lit = dot_nt(low, high)
    for r in range(ROWS):
        mask_ref[r] = jnp.broadcast_to(lit[:, r : r + 1], (COLS, LANES))

    target = route_ref[0:1, :]
    arrival = route_ref[1:2, :] + 1
    before = (iota((LANES, LANES), 0) < iota((LANES, LANES), 1)).astype(F32).astype(BF16)
    ones = jnp.ones((LANES, LANES), BF16)
    carry = jnp.zeros((LANES, LANES), F32)
    ranks = []
    for b in range(SEGS // LANES):
        goes = (iota((LANES, LANES), 0) == target[:, b * LANES : (b + 1) * LANES]).astype(F32)
        goes16 = goes.astype(BF16)
        ranks.append(jnp.sum(goes * (dot(goes16, before) + carry), axis=0, keepdims=True))
        carry = carry + dot(goes16, ones)
    rank = jnp.concatenate(ranks, axis=1).astype(jnp.int32)
    row = target * 16 + rank
    index = iota((LANES, SEGS), 0)
    coarse = (arrival >> 5).astype(F32)
    fine = (arrival & 31).astype(F32)
    tag_rows = [
        jnp.where(index == 2 * q, coarse, jnp.where(index == 2 * q + 1, fine, 0.0)).astype(BF16)
        for q in range(2)
    ]
    for b in range(SEGS // LANES):
        tags = jnp.zeros((LANES, LANES), F32)
        for q in range(2):
            want = 2 * (iota((LANES, SEGS), 0) + b * LANES) + q
            chosen = (row == want).astype(F32).astype(BF16)
            place_ref[q, b * LANES : (b + 1) * LANES, :] = chosen
            tags = tags + dot_nt(chosen, tag_rows[q])
        tags_ref[b * LANES : (b + 1) * LANES, :] = tags.astype(BF16)

    from_cell = iota((LANES, LANES), 0)
    to_lane = iota((LANES, LANES), 1)
    source_cell = jnp.where(to_lane < 64, 2 * to_lane, 2 * (to_lane - 64) + 1)
    split = (from_cell == source_cell).astype(F32).astype(BF16)
    mix_ref[...] = dot(regrid_ref[...], split).astype(BF16)


def plan(sun_columns, segment_route, regrid_weights):
    return pl.pallas_call(
        plan_kernel,
        in_specs=[VMEM] * 3,
        out_specs=[VMEM] * 4,
        out_shape=[
            vmem_out((ROWS, COLS, LANES), F32),
            vmem_out((2, SEGS, SEGS), BF16),
            vmem_out((SEGS, LANES), BF16),
            vmem_out((CELLS, LANES), BF16),
        ],
        compiler_params=params(),
        cost_estimate=cost(3_000_000_000, 1 << 20),
        name="plan",
    )(
        sun_columns.reshape(1, CELLS),
        segment_route.reshape(2, SEGS),
        regrid_weights.reshape(CELLS, LANES),
    )


def weights_of(lo0, mid0, hi0, left1, mid1, right1, valid_lo=None, valid_hi=None):
    f_lo = 0.5 * (lo0 + mid0)
    f_hi = 0.5 * (mid0 + hi0)
    if valid_lo is not None:
        f_lo = f_lo * valid_lo
    if valid_hi is not None:
        f_hi = f_hi * valid_hi
    g_lo = 0.5 * (left1 + mid1)
    g_hi = 0.5 * (mid1 + right1)
    keep = (
        1.0
        - jnp.maximum(f_hi, 0.0)
        + jnp.minimum(f_lo, 0.0)
        - jnp.maximum(g_hi, 0.0)
        + jnp.minimum(g_lo, 0.0)
    )
    return (
        keep,
        jnp.maximum(f_lo, 0.0),
        -jnp.minimum(f_hi, 0.0),
        jnp.maximum(g_lo, 0.0),
        -jnp.minimum(g_hi, 0.0),
    )


def combine(k, mid, lo, hi, left, right):
    return k[0] * mid + k[1] * lo + k[2] * hi + k[3] * left + k[4] * right


def net(x_ref, h1_ref, h2_ref, w1_ref, b1_ref, w2_ref, b2_ref, w3_ref, emit):
    hidden = w2_ref.shape[0]
    wide = 256
    x = x_ref[...]
    for n in range(0, hidden, wide):
        u = dot(x, w1_ref[:, n : n + wide]) + b1_ref[:, n : n + wide]
        h1_ref[:, n : n + wide] = silu(u).astype(BF16)
    h1 = h1_ref[...]
    for n in range(0, hidden, wide):
        u = dot(h1, w2_ref[:, n : n + wide]) + b2_ref[:, n : n + wide]
        h2_ref[:, n : n + wide] = silu(u).astype(BF16)
    h2 = h2_ref[...]
    for n in range(0, FEAT, wide):
        emit(n, dot(h2, w3_ref[:, n : n + wide]))


def inner_kernel(
    t_ref, c_ref, mask_ref, w1_ref, b1_ref, w2_ref, b2_ref, w3_ref,
    out_ref, x_ref, adv_ref, h1_ref, h2_ref,
):
    mid = slice(EDGE, EDGE + INNER)
    left = slice(EDGE - 1, EDGE + INNER - 1)
    right = slice(EDGE + 1, EDGE + INNER + 1)

    def body(i, carry):
        first = 1 + i * GROUP
        for j in range(GROUP):
            r = first + j
            k = weights_of(
                c_ref[0, r - 1, mid, :], c_ref[0, r, mid, :], c_ref[0, r + 1, mid, :],
                c_ref[1, r, left, :], c_ref[1, r, mid, :], c_ref[1, r, right, :],
            )
            for f in range(FIELDS):
                at = slice(f * LANES, (f + 1) * LANES)
                moved = combine(
                    k, t_ref[f, r, mid, :], t_ref[f, r - 1, mid, :], t_ref[f, r + 1, mid, :],
                    t_ref[f, r, left, :], t_ref[f, r, right, :],
                )
                adv_ref[j * INNER : (j + 1) * INNER, at] = moved
                x_ref[j * INNER : (j + 1) * INNER, at] = moved.astype(BF16)

        def emit(n, heat):
            for j in range(GROUP):
                for m in range(0, heat.shape[1], LANES):
                    at = slice(n + m, n + m + LANES)
                    here = slice(j * INNER, (j + 1) * INNER)
                    out_ref[(n + m) // LANES, first + j, mid, :] = (
                        adv_ref[here, at] + mask_ref[first + j, mid, :] * heat[here, m : m + LANES]
                    )

        net(x_ref, h1_ref, h2_ref, w1_ref, b1_ref, w2_ref, b2_ref, w3_ref, emit)
        return carry

    lax.fori_loop(0, (ROWS - 2) // GROUP, body, 0)


def inner(state, speeds, mask, weights):
    many = GROUP * INNER
    hidden = weights[2].shape[0]
    return pl.pallas_call(
        inner_kernel,
        in_specs=[VMEM] * 8,
        out_specs=VMEM,
        out_shape=vmem_out((FIELDS, ROWS, COLS, LANES), F32),
        scratch_shapes=[
            pltpu.VMEM((many, FEAT), BF16),
            pltpu.VMEM((many, FEAT), F32),
            pltpu.VMEM((many, hidden), BF16),
            pltpu.VMEM((many, hidden), BF16),
        ],
        compiler_params=params(),
        cost_estimate=cost(7_500_000_000, 4 << 20),
        name="inner",
    )(state, speeds, mask, *weights)


def rim_kernel(
    last,
    valid_ref, t_ref, c_ref, mask_ref,
    row_lo_ref, row_hi_ref, col_lo_ref, col_hi_ref,
    crow_lo_ref, crow_hi_ref, ccol_lo_ref, ccol_hi_ref,
    w1_ref, b1_ref, w2_ref, b2_ref, w3_ref, *rest,
):
    if last:
        (place_ref, tags_ref, _, out_ref, pack_ref,
         x_ref, adv_ref, h1_ref, h2_ref, cols_ref, ccols_ref) = rest
    else:
        (_, out_ref, srow_lo_ref, srow_hi_ref, scol_lo_ref, scol_hi_ref,
         x_ref, adv_ref, h1_ref, h2_ref, cols_ref, ccols_ref) = rest
    lat = slice(0, LANES)
    speed_at = slice(FEAT, FEAT + LANES)
    for side, col, ccol in ((0, col_lo_ref, ccol_lo_ref), (1, col_hi_ref, ccol_hi_ref)):
        col = col[:, :FEAT].astype(F32)
        ccol = ccol[:, speed_at].astype(F32)
        for r in range(ROWS):
            cols_ref[side, r] = jnp.broadcast_to(col[r : r + 1, :], (EDGE, FEAT))
            ccols_ref[side, r] = jnp.broadcast_to(ccol[r : r + 1, :], (EDGE, LANES))

    def from_left(whole, edge):
        return jnp.where(iota(whole.shape, 0) == 0, edge, pltpu.roll(whole, 1, 0))

    def from_right(whole, edge):
        count = whole.shape[0]
        return jnp.where(iota(whole.shape, 0) == count - 1, edge, pltpu.roll(whole, count - 1, 0))

    for at_row, side in ((0, 0), (ROWS - 1, 1)):
        low_row = lambda ref, f, halo, at: halo[:, at].astype(F32) if side == 0 else ref[f, at_row - 1]
        high_row = lambda ref, f, halo, at: ref[f, at_row + 1] if side == 0 else halo[:, at].astype(F32)
        crow = crow_lo_ref if side == 0 else crow_hi_ref
        vrow = row_lo_ref if side == 0 else row_hi_ref
        mid1 = c_ref[1, at_row]
        k = weights_of(
            low_row(c_ref, 0, crow, speed_at), c_ref[0, at_row], high_row(c_ref, 0, crow, speed_at),
            from_left(mid1, ccols_ref[0, at_row, 0:1, :]), mid1,
            from_right(mid1, ccols_ref[1, at_row, 0:1, :]),
            valid_ref[0] if side == 0 else None,
            valid_ref[1] if side == 1 else None,
        )
        for f in range(FIELDS):
            at = slice(f * LANES, (f + 1) * LANES)
            v = t_ref[f, at_row]
            moved = combine(
                k, v, low_row(t_ref, f, vrow, at), high_row(t_ref, f, vrow, at),
                from_left(v, cols_ref[0, at_row, 0:1, at]),
                from_right(v, cols_ref[1, at_row, 0:1, at]),
            )
            adv_ref[side * COLS : (side + 1) * COLS, at] = moved
            x_ref[side * COLS : (side + 1) * COLS, at] = moved.astype(BF16)

    def edges(ref, f, r, cols, at):
        lo = ref[f, r, 0:EDGE, :]
        hi = ref[f, r, COLS - EDGE : COLS, :]
        left = jnp.concatenate(
            [from_left(lo, cols[0, r, :, at]), ref[f, r, COLS - EDGE - 1 : COLS - 1, :]], axis=0
        )
        right = jnp.concatenate(
            [ref[f, r, 1 : EDGE + 1, :], from_right(hi, cols[1, r, :, at])], axis=0
        )
        return jnp.concatenate([lo, hi], axis=0), left, right

    def both(ref, f, r):
        return jnp.concatenate([ref[f, r, 0:EDGE, :], ref[f, r, COLS - EDGE : COLS, :]], axis=0)

    def edge_row(i, carry):
        r = i + 1
        spot = pl.multiple_of(2 * COLS + i * 2 * EDGE, 2 * EDGE)
        mid1, left1, right1 = edges(c_ref, 1, r, ccols_ref, lat)
        k = weights_of(
            both(c_ref, 0, r - 1), both(c_ref, 0, r), both(c_ref, 0, r + 1), left1, mid1, right1
        )
        for f in range(FIELDS):
            at = slice(f * LANES, (f + 1) * LANES)
            v, left, right = edges(t_ref, f, r, cols_ref, at)
            moved = combine(k, v, both(t_ref, f, r - 1), both(t_ref, f, r + 1), left, right)
            adv_ref[pl.ds(spot, 2 * EDGE), at] = moved
            x_ref[pl.ds(spot, 2 * EDGE), at] = moved.astype(BF16)
        return carry

    lax.fori_loop(0, ROWS - 2, edge_row, 0)

    def emit(n, heat):
        for m in range(0, heat.shape[1], LANES):
            at = slice(n + m, n + m + LANES)
            part = heat[:, m : m + LANES]
            f = (n + m) // LANES
            for side, at_row in ((0, 0), (1, ROWS - 1)):
                here = slice(side * COLS, (side + 1) * COLS)
                out_ref[f, at_row] = adv_ref[here, at] + mask_ref[at_row] * part[here]
            for r in range(1, ROWS - 1):
                spot = 2 * COLS + (r - 1) * 2 * EDGE
                lo = slice(spot, spot + EDGE)
                hi = slice(spot + EDGE, spot + 2 * EDGE)
                out_ref[f, r, 0:EDGE, :] = adv_ref[lo, at] + mask_ref[r, 0:EDGE, :] * part[lo]
                out_ref[f, r, COLS - EDGE : COLS, :] = (
                    adv_ref[hi, at] + mask_ref[r, COLS - EDGE : COLS, :] * part[hi]
                )

    net(x_ref, h1_ref, h2_ref, w1_ref, b1_ref, w2_ref, b2_ref, w3_ref, emit)

    if not last:
        for f in range(FIELDS):
            at = slice(f * LANES, (f + 1) * LANES)
            srow_lo_ref[:, at] = out_ref[f, 0].astype(BF16)
            srow_hi_ref[:, at] = out_ref[f, ROWS - 1].astype(BF16)
            scol_lo_ref[:, at] = out_ref[f, :, 0].astype(BF16)
            scol_hi_ref[:, at] = out_ref[f, :, COLS - 1].astype(BF16)
        return
    flat = out_ref.reshape(FIELDS * CELLS, LANES)
    half = FEAT // 2
    for c in range(2):
        columns = jnp.concatenate(
            [
                flat[pl.ds(f * CELLS + c, SEGS, stride=2), :]
                for f in (2, 3)
            ],
            axis=1,
        ).astype(BF16)
        for q in range(2):
            for b in range(0, SEGS, 256):
                pack_ref[b : b + 256, q * FEAT + c * half : q * FEAT + (c + 1) * half] = dot(
                    place_ref[q, b : b + 256, :], columns
                ).astype(BF16)
    pack_ref[:, 2 * FEAT :] = tags_ref[...]


def rim(last, valid, state, speeds, mask, halo, speed_halo, weights, extra, partial):
    hidden = weights[2].shape[0]
    operands = (valid, state, speeds, mask, *halo, *speed_halo, *weights, *extra, partial)
    outs = [vmem_out((FIELDS, ROWS, COLS, LANES), F32)]
    if last:
        outs += [vmem_out((SEGS, 2 * FEAT + LANES), BF16)]
    else:
        outs += [vmem_out((COLS, FEAT), BF16)] * 2 + [vmem_out((ROWS, FEAT), BF16)] * 2
    return pl.pallas_call(
        lambda *refs: rim_kernel(last, *refs),
        in_specs=[SMEM] + [VMEM] * (len(operands) - 1),
        out_specs=[VMEM] * len(outs),
        out_shape=outs,
        input_output_aliases={len(operands) - 1: 0},
        scratch_shapes=[
            pltpu.VMEM((RIM, FEAT), BF16),
            pltpu.VMEM((RIM, FEAT), F32),
            pltpu.VMEM((RIM, hidden), BF16),
            pltpu.VMEM((RIM, hidden), BF16),
            pltpu.VMEM((2, ROWS, EDGE, FEAT), F32),
            pltpu.VMEM((2, ROWS, EDGE, LANES), F32),
        ],
        compiler_params=params(),
        cost_estimate=cost(4_000_000_000, 4 << 20),
        name="rim_last" if last else "rim",
    )(*operands)


def unturn_kernel(t_ref, out_ref, stage_ref, sems):
    size = LANES * ROWS
    for f in range(FIELDS):
        for r in range(ROWS):
            stage_ref[f, pl.ds(r, LANES, stride=ROWS), :] = t_ref[f, r].T
        pltpu.make_async_copy(
            stage_ref.at[f], out_ref.at[pl.ds(f * size, size)], sems.at[f]
        ).start()
    for f in range(FIELDS):
        pltpu.make_async_copy(
            stage_ref.at[f], out_ref.at[pl.ds(f * size, size)], sems.at[f]
        ).wait()


def unturn(state):
    return pl.pallas_call(
        unturn_kernel,
        in_specs=[VMEM],
        out_specs=ANY,
        out_shape=jax.ShapeDtypeStruct((FIELDS * LANES * ROWS, COLS), F32),
        scratch_shapes=[
            pltpu.VMEM((FIELDS, LANES * ROWS, COLS), F32),
            pltpu.SemaphoreType.DMA((FIELDS,)),
        ],
        compiler_params=params(),
        cost_estimate=cost(1_000_000_000, 8 << 20),
        name="unturn",
    )(state)


def chem_kernel(arr_ref, mix_ref, w1_ref, b1_ref, w2_ref, out_ref, want_ref, x_ref, h_ref):
    lane = iota((8, LANES), 1)
    which = iota((8, LANES), 0)
    pick = jnp.where(
        lane == 2 * which, 32.0, jnp.where(lane == 2 * which + 1, 1.0, 0.0)
    )
    pick = jnp.where(which < 2, pick, 0.0).astype(BF16)
    want_ref[...] = dot_nt(pick, arr_ref[:, 2 * FEAT :]).astype(jnp.int32) - 1
    span = 256
    half = FEAT // 2

    def body(i, carry):
        start = i * span
        placed = jnp.zeros((span, FEAT), F32)
        for q in range(2):
            chosen = (iota((span, SEGS), 0) + start == want_ref[q : q + 1, :]).astype(F32).astype(BF16)
            placed = placed + dot(chosen, arr_ref[:, q * FEAT : (q + 1) * FEAT])
        placed = placed.astype(BF16)
        for b in range(span // 64):
            cells = jnp.concatenate(
                [placed[b * 64 : (b + 1) * 64, :half], placed[b * 64 : (b + 1) * 64, half:]], axis=0
            )
            spot = pl.multiple_of(2 * start + b * LANES, LANES)
            x_ref[b * LANES : (b + 1) * LANES, :] = dot(mix_ref[pl.ds(spot, LANES), :], cells).astype(BF16)
        x = x_ref[...]
        for n in range(0, w1_ref.shape[1], 256):
            u = dot(x, w1_ref[:, n : n + 256]) + b1_ref[:, n : n + 256]
            h_ref[:, n : n + 256] = silu(u).astype(BF16)
        out_ref[pl.ds(pl.multiple_of(2 * start, 2 * span), 2 * span), :] = dot(h_ref[...], w2_ref[...]).astype(BF16)
        return carry

    lax.fori_loop(0, SEGS // span, body, 0)


def chem(arrived, mix, w1, b1, w2):
    return pl.pallas_call(
        chem_kernel,
        in_specs=[VMEM] * 5,
        out_specs=VMEM,
        out_shape=jax.ShapeDtypeStruct((CELLS, w2.shape[1]), BF16),
        scratch_shapes=[
            pltpu.VMEM((8, SEGS), jnp.int32),
            pltpu.VMEM((512, FEAT // 2), BF16),
            pltpu.VMEM((512, w1.shape[1]), BF16),
        ],
        compiler_params=params(),
        cost_estimate=cost(4_400_000_000, 4 << 20),
        name="chem",
    )(arrived, mix, w1, b1, w2)


def swap(low, high):
    rows, columns = lax.axis_size("gx"), lax.axis_size("gy")
    up = [(i, i + 1) for i in range(rows - 1)]
    down = [(i + 1, i) for i in range(rows - 1)]
    right = [(i, (i + 1) % columns) for i in range(columns)]
    left = [((i + 1) % columns, i) for i in range(columns)]
    row_lo, col_lo = low
    row_hi, col_hi = high
    return (
        lax.ppermute(row_hi, "gx", up),
        lax.ppermute(row_lo, "gx", down),
        lax.ppermute(col_hi, "gy", right),
        lax.ppermute(col_lo, "gy", left),
    )


def local(
    fields, courant, sun_columns, rad_w1, rad_b1, rad_w2, rad_b2, rad_w3,
    segment_route, regrid_weights, chem_w1, chem_b1, chem_w2,
):
    place_at = lax.axis_index("gx")
    valid = jnp.stack([place_at > 0, place_at < lax.axis_size("gx") - 1]).astype(F32)
    weights = (rad_w1, rad_b1.reshape(1, -1), rad_w2, rad_b2.reshape(1, -1), rad_w3)
    weights = tuple(pltpu.with_memory_space_constraint(w, pltpu.VMEM) for w in weights)

    state, speeds, row_lo, row_hi, col_lo, col_hi = turn(fields, courant)
    state = pltpu.with_memory_space_constraint(state, pltpu.VMEM)
    speeds = pltpu.with_memory_space_constraint(speeds, pltpu.VMEM)
    speed_halo = swap((row_lo, col_lo), (row_hi, col_hi))
    mask, place, tags, mix = plan(sun_columns, segment_route, regrid_weights)
    partial = inner(state, speeds, mask, weights)
    state, row_lo, row_hi, col_lo, col_hi = rim(
        False, valid, state, speeds, mask, speed_halo, speed_halo, weights, (), partial
    )
    halo = swap((row_lo, col_lo), (row_hi, col_hi))
    partial = inner(state, speeds, mask, weights)
    state, packed = rim(
        True, valid, state, speeds, mask, halo, speed_halo, weights, (place, tags), partial
    )
    tiles = lax.axis_size("gx") * lax.axis_size("gy")
    packed = packed.reshape(tiles, SEGS // tiles, packed.shape[1])
    arrived = lax.all_to_all(packed, ("gx", "gy"), split_axis=0, concat_axis=0, tiled=True)
    fields_out = unturn(state).reshape(fields.shape)
    output = chem(
        arrived.reshape(SEGS, arrived.shape[2]), mix, chem_w1, chem_b1.reshape(1, -1), chem_w2
    )
    return fields_out, output.reshape(1, 1, CELLS, -1)


def solution(mesh):
    return jax.shard_map(
        local,
        mesh=mesh,
        in_specs=(
            P(None, None, "gx", "gy"),
            P(None, None, "gx", "gy"),
            P("gx", "gy", None),
            P(),
            P(),
            P(),
            P(),
            P(),
            P(None, "gx", "gy", None),
            P("gx", "gy", None, None, None),
            P(),
            P(),
            P(),
        ),
        out_specs=(P(None, None, "gx", "gy"), P("gx", "gy", None, None)),
        check_vma=False,
    )
```

```python
import jax
import jax.numpy as jnp
from jax import lax
from jax.experimental import pallas as pl
from jax.experimental.pallas import tpu as pltpu
from jax.sharding import PartitionSpec as P

F32 = jnp.float32
BF16 = jnp.bfloat16
LANES = 128
FIELDS = 4
ROWS = 16
COLS = 128
FEAT = FIELDS * LANES
CELLS = ROWS * COLS
SEGS = CELLS // 2
EDGE = 8
INNER = COLS - 2 * EDGE
GROUP = 7
RIM = 2 * COLS + (ROWS - 2) * 2 * EDGE
VMEM_LIMIT = 40 * 1024 * 1024

VMEM = pl.BlockSpec(memory_space=pltpu.VMEM)
SMEM = pl.BlockSpec(memory_space=pltpu.SMEM)
ANY = pl.BlockSpec(memory_space=pl.ANY)


HBM = pl.BlockSpec(memory_space=pltpu.HBM)


def hbm_out(shape, dtype):
    return pltpu.HBM(shape, dtype)


def in_vmem(x):
    return pltpu.with_memory_space_constraint(x, pltpu.VMEM)


def in_hbm(x):
    return pltpu.with_memory_space_constraint(x, pltpu.HBM)


def params():
    return pltpu.CompilerParams(vmem_limit_bytes=VMEM_LIMIT)


def cost(flops, bytes_accessed=0):
    return pl.CostEstimate(flops=flops, bytes_accessed=bytes_accessed, transcendentals=0)


def dot(a, b):
    return jnp.dot(a, b, preferred_element_type=F32)


def dot_nt(a, b):
    return lax.dot_general(a, b, (((1,), (1,)), ((), ())), preferred_element_type=F32)


def silu(u):
    half = 0.5 * u
    return half + half * jnp.tanh(half)


def iota(shape, dim):
    return lax.broadcasted_iota(jnp.int32, shape, dim)


def turn_kernel(f_ref, c_ref, t_ref, cc_ref, row_lo_ref, row_hi_ref, col_lo_ref, col_hi_ref):
    step = pl.program_id(0)

    @pl.when(step < FIELDS)
    def _():
        for r in range(ROWS):
            block = f_ref[pl.ds(r, LANES, stride=ROWS), :].T
            t_ref[0, r] = block
            if r == 0:
                row_lo_ref[...] = block.astype(BF16)
            if r == ROWS - 1:
                row_hi_ref[...] = block.astype(BF16)
        col_lo_ref[...] = t_ref[0, :, 0, :].astype(BF16)
        col_hi_ref[...] = t_ref[0, :, COLS - 1, :].astype(BF16)

    @pl.when(step >= FIELDS)
    def _():
        for r in range(ROWS):
            cc_ref[0, r] = c_ref[pl.ds(r, LANES, stride=ROWS), :].T

    @pl.when(step == FIELDS)
    def _():
        row_lo_ref[...] = cc_ref[0, 0].astype(BF16)
        row_hi_ref[...] = cc_ref[0, ROWS - 1].astype(BF16)

    @pl.when(step == FIELDS + 1)
    def _():
        col_lo_ref[...] = cc_ref[0, :, 0, :].astype(BF16)
        col_hi_ref[...] = cc_ref[0, :, COLS - 1, :].astype(BF16)


def turn(fields, courant):
    flat_f = in_hbm(fields.reshape(FIELDS * LANES * ROWS, COLS))
    flat_c = in_hbm(courant.reshape(2 * LANES * ROWS, COLS))
    field_at = lambda i: jnp.minimum(i, FIELDS - 1)
    speed_at = lambda i: jnp.maximum(i - FIELDS, 0)
    halo_at = lambda i: jnp.minimum(i, FIELDS)
    return pl.pallas_call(
        turn_kernel,
        grid=(FIELDS + 2,),
        in_specs=[
            pl.BlockSpec((LANES * ROWS, COLS), lambda i: (field_at(i), 0)),
            pl.BlockSpec((LANES * ROWS, COLS), lambda i: (speed_at(i), 0)),
        ],
        out_specs=[
            pl.BlockSpec((1, ROWS, COLS, LANES), lambda i: (field_at(i), 0, 0, 0)),
            pl.BlockSpec((1, ROWS, COLS, LANES), lambda i: (speed_at(i), 0, 0, 0)),
            pl.BlockSpec((COLS, LANES), lambda i: (0, halo_at(i))),
            pl.BlockSpec((COLS, LANES), lambda i: (0, halo_at(i))),
            pl.BlockSpec((ROWS, LANES), lambda i: (0, halo_at(i))),
            pl.BlockSpec((ROWS, LANES), lambda i: (0, halo_at(i))),
        ],
        out_shape=[
            hbm_out((FIELDS, ROWS, COLS, LANES), F32),
            jax.ShapeDtypeStruct((2, ROWS, COLS, LANES), F32),
            jax.ShapeDtypeStruct((COLS, FEAT + LANES), BF16),
            jax.ShapeDtypeStruct((COLS, FEAT + LANES), BF16),
            jax.ShapeDtypeStruct((ROWS, FEAT + LANES), BF16),
            jax.ShapeDtypeStruct((ROWS, FEAT + LANES), BF16),
        ],
        compiler_params=params(),
        cost_estimate=cost(20_000_000, 12 << 20),
        name="turn",
    )(flat_f, flat_c)


def plan_kernel(sun_ref, route_ref, mask_ref, place_ref, tags_ref, stage_ref, sems):
    slots = sun_ref[...]
    low = (iota((COLS, CELLS), 0) == (slots & (COLS - 1))).astype(F32).astype(BF16)
    high = (iota((LANES, CELLS), 0) == (slots >> 7)).astype(F32).astype(BF16)
    lit = dot_nt(low, high)
    mask_ref[...] = lit

    target = route_ref[0:1, :]
    arrival = route_ref[1:2, :] + 1
    before = (iota((LANES, LANES), 0) < iota((LANES, LANES), 1)).astype(F32).astype(BF16)
    ones = jnp.ones((LANES, LANES), BF16)
    carry = jnp.zeros((LANES, LANES), F32)
    ranks = []
    for b in range(SEGS // LANES):
        goes = (iota((LANES, LANES), 0) == target[:, b * LANES : (b + 1) * LANES]).astype(F32)
        goes16 = goes.astype(BF16)
        ranks.append(jnp.sum(goes * (dot(goes16, before) + carry), axis=0, keepdims=True))
        carry = carry + dot(goes16, ones)
    rank = jnp.concatenate(ranks, axis=1).astype(jnp.int32)
    row = target * 16 + rank
    index = iota((LANES, SEGS), 0)
    coarse = (arrival >> 5).astype(F32)
    fine = (arrival & 31).astype(F32)
    tag_rows = [
        jnp.where(index == 2 * q, coarse, jnp.where(index == 2 * q + 1, fine, 0.0)).astype(BF16)
        for q in range(2)
    ]
    for b in range(SEGS // LANES):
        tags = jnp.zeros((LANES, LANES), F32)
        for q in range(2):
            want = 2 * (iota((LANES, SEGS), 0) + b * LANES) + q
            chosen = (row == want).astype(F32).astype(BF16)
            at = (q, slice(b * LANES, (b + 1) * LANES))
            stage_ref[at] = chosen
            pltpu.make_async_copy(stage_ref.at[at], place_ref.at[at], sems.at[q, b]).start()
            tags = tags + dot_nt(chosen, tag_rows[q])
        tags_ref[b * LANES : (b + 1) * LANES, :] = tags.astype(BF16)
    for b in range(SEGS // LANES):
        for q in range(2):
            at = (q, slice(b * LANES, (b + 1) * LANES))
            pltpu.make_async_copy(stage_ref.at[at], place_ref.at[at], sems.at[q, b]).wait()


def plan(sun_columns, segment_route):
    return pl.pallas_call(
        plan_kernel,
        in_specs=[VMEM] * 2,
        out_specs=[VMEM, HBM, VMEM],
        out_shape=[
            jax.ShapeDtypeStruct((COLS, LANES), F32),
            hbm_out((2, SEGS, SEGS), BF16),
            jax.ShapeDtypeStruct((SEGS, LANES), BF16),
        ],
        scratch_shapes=[
            pltpu.VMEM((2, SEGS, SEGS), BF16),
            pltpu.SemaphoreType.DMA((2, SEGS // LANES)),
        ],
        compiler_params=params(),
        cost_estimate=cost(3_000_000_000, 1 << 20),
        name="plan",
    )(sun_columns.reshape(1, CELLS), segment_route.reshape(2, SEGS))


def weights_of(lo0, mid0, hi0, left1, mid1, right1, valid_lo=None, valid_hi=None):
    f_lo = 0.5 * (lo0 + mid0)
    f_hi = 0.5 * (mid0 + hi0)
    if valid_lo is not None:
        f_lo = f_lo * valid_lo
    if valid_hi is not None:
        f_hi = f_hi * valid_hi
    g_lo = 0.5 * (left1 + mid1)
    g_hi = 0.5 * (mid1 + right1)
    keep = (
        1.0
        - jnp.maximum(f_hi, 0.0)
        + jnp.minimum(f_lo, 0.0)
        - jnp.maximum(g_hi, 0.0)
        + jnp.minimum(g_lo, 0.0)
    )
    return (
        keep,
        jnp.maximum(f_lo, 0.0),
        -jnp.minimum(f_hi, 0.0),
        jnp.maximum(g_lo, 0.0),
        -jnp.minimum(g_hi, 0.0),
    )


def combine(k, mid, lo, hi, left, right):
    return k[0] * mid + k[1] * lo + k[2] * hi + k[3] * left + k[4] * right


def net(x, h1_ref, h2_ref, w1_ref, b1_ref, w2_ref, b2_ref, w3_ref, emit, beside=(), ready=None):
    hidden = w2_ref.shape[0]
    wide = 256
    beside = list(beside)
    for n in range(0, hidden, wide):
        u = dot(x, w1_ref[:, n : n + wide]) + b1_ref[:, n : n + wide]
        h1_ref[:, n : n + wide] = silu(u).astype(BF16)
    if ready is not None:
        ready(1)
    h1 = h1_ref[...]
    for n in range(0, hidden, wide):
        u = dot(h1, w2_ref[:, n : n + wide]) + b2_ref[:, n : n + wide]
        h2_ref[:, n : n + wide] = silu(u).astype(BF16)
        if beside:
            beside.pop(0)()
    if ready is not None:
        ready(2)
    h2 = h2_ref[...]
    for n in range(0, FEAT, wide):
        emit(n, dot(h2, w3_ref[:, n : n + wide]))


def weight_copies(sources, held, sems):
    return [pltpu.make_async_copy(a, b, sems.at[i]) for i, (a, b) in enumerate(zip(sources, held))]


def inner_kernel(
    mask_ref, c_ref, w1_ref, b1_ref, w2_ref, b2_ref, w3_ref, t_hbm, out_hbm,
    t_ref, out_ref, lit_ref, x_ref, adv_ref, h1_ref, h2_ref, t_sems, out_sems,
):
    groups = (ROWS - 2) // GROUP

    def load(g, first, count):
        at = pl.ds(first, count)
        return pltpu.make_async_copy(t_hbm.at[:, at], t_ref.at[:, at], t_sems.at[g])

    def store(g):
        return pltpu.make_async_copy(
            out_ref.at[:, pl.ds(g * GROUP, GROUP)],
            out_hbm.at[:, pl.ds(1 + g * GROUP, GROUP), pl.ds(EDGE, INNER)],
            out_sems.at[g],
        )

    load(0, 0, 2).start()
    for g in range(groups):
        load(g + 1, GROUP * g + 2, GROUP).start()
    for r in range(ROWS):
        lit_ref[r] = jnp.broadcast_to(mask_ref[:, r : r + 1], (COLS, LANES))
    load(0, 0, 2).wait()

    mid = slice(EDGE, EDGE + INNER)
    left = slice(EDGE - 1, EDGE + INNER - 1)
    right = slice(EDGE + 1, EDGE + INNER + 1)

    def body(g, carry):
        load(g + 1, GROUP * g + 2, GROUP).wait()
        for j in range(GROUP):
            r = 1 + g * GROUP + j
            k = weights_of(
                c_ref[0, r - 1, mid, :], c_ref[0, r, mid, :], c_ref[0, r + 1, mid, :],
                c_ref[1, r, left, :], c_ref[1, r, mid, :], c_ref[1, r, right, :],
            )
            for f in range(FIELDS):
                at = slice(f * LANES, (f + 1) * LANES)
                moved = combine(
                    k, t_ref[f, r, mid, :], t_ref[f, r - 1, mid, :], t_ref[f, r + 1, mid, :],
                    t_ref[f, r, left, :], t_ref[f, r, right, :],
                )
                adv_ref[j * INNER : (j + 1) * INNER, at] = moved
                x_ref[j * INNER : (j + 1) * INNER, at] = moved.astype(BF16)

        def emit(n, heat):
            for j in range(GROUP):
                r = 1 + g * GROUP + j
                lit = lit_ref[r, mid, :]
                for m in range(0, heat.shape[1], LANES):
                    here = slice(j * INNER, (j + 1) * INNER)
                    out_ref[(n + m) // LANES, r - 1] = (
                        adv_ref[here, n + m : n + m + LANES] + lit * heat[here, m : m + LANES]
                    )

        net(x_ref[...], h1_ref, h2_ref, w1_ref, b1_ref, w2_ref, b2_ref, w3_ref, emit)
        store(g).start()
        return carry

    lax.fori_loop(0, groups, body, 0)
    for g in range(groups):
        store(g).wait()


def inner(state, speeds, mask, weights):
    many = GROUP * INNER
    hidden = weights[2].shape[0]
    groups = (ROWS - 2) // GROUP
    return pl.pallas_call(
        inner_kernel,
        in_specs=[VMEM] * 7 + [HBM],
        out_specs=HBM,
        out_shape=hbm_out((FIELDS, ROWS, COLS, LANES), F32),
        scratch_shapes=[
            pltpu.VMEM((FIELDS, ROWS, COLS, LANES), F32),
            pltpu.VMEM((FIELDS, ROWS - 2, INNER, LANES), F32),
            pltpu.VMEM((ROWS, COLS, LANES), F32),
            pltpu.VMEM((many, FEAT), BF16),
            pltpu.VMEM((many, FEAT), F32),
            pltpu.VMEM((many, hidden), BF16),
            pltpu.VMEM((many, hidden), BF16),
            pltpu.SemaphoreType.DMA((groups + 1,)),
            pltpu.SemaphoreType.DMA((groups,)),
        ],
        compiler_params=params(),
        cost_estimate=cost(7_500_000_000, 4 << 20),
        name="inner",
    )(
        mask,
        in_vmem(speeds),
        *(in_vmem(w) if w.dtype == BF16 else w for w in weights),
        in_hbm(state),
    )


def rim_kernel(
    last,
    valid_ref, mask_ref,
    row_lo_ref, row_hi_ref, col_lo_ref, col_hi_ref,
    crow_lo_ref, crow_hi_ref, ccol_lo_ref, ccol_hi_ref,
    b1_ref, b2_ref, *rest,
):
    if last:
        tags_ref, rest = rest[0], rest[1:]
        t_hbm, c_hbm, w1_hbm, w2_hbm, w3_hbm, place_hbm, part_hbm, out_hbm, pack_hbm = rest[:9]
        rest = rest[9:]
    else:
        t_hbm, c_hbm, w1_hbm, w2_hbm, w3_hbm, part_hbm, out_hbm = rest[:7]
        srow_lo_ref, srow_hi_ref, scol_lo_ref, scol_hi_ref = rest[7:11]
        rest = rest[11:]
    (
        trow_ref, tlo_ref, thi_ref, crow_ref, clo_ref, chi_ref,
        w1_ref, w2_ref, w3_ref, out_ref, x_ref, adv_ref, h1_ref, h2_ref, cols_ref, ccols_ref,
        t_sems, w_sems, out_sems,
    ) = rest[:19]
    if last:
        place_ref, pack_ref, place_sems, pack_sems = rest[19:]
    loads = []
    for hbm, row, lo, hi in ((t_hbm, trow_ref, tlo_ref, thi_ref), (c_hbm, crow_ref, clo_ref, chi_ref)):
        loads += [
            (hbm.at[:, pl.ds(0, 2)], row.at[:, pl.ds(0, 2)]),
            (hbm.at[:, pl.ds(ROWS - 2, 2)], row.at[:, pl.ds(2, 2)]),
            (hbm.at[:, :, pl.ds(0, 2 * EDGE)], lo),
            (hbm.at[:, :, pl.ds(COLS - 2 * EDGE, 2 * EDGE)], hi),
        ]
    loads = [pltpu.make_async_copy(x, y, t_sems.at[i]) for i, (x, y) in enumerate(loads)]
    weight_loads = weight_copies((w1_hbm, w2_hbm, w3_hbm), (w1_ref, w2_ref, w3_ref), w_sems)
    for copy in loads + weight_loads:
        copy.start()
    if last:
        centre = (pl.ds(1, ROWS - 2), pl.ds(EDGE, INNER))
        centre_load = pltpu.make_async_copy(
            part_hbm.at[pl.ds(2, 2), *centre], out_ref.at[pl.ds(2, 2), *centre], place_sems.at[2]
        )
        centre_load.start()
        place_loads = weight_copies((place_hbm.at[0], place_hbm.at[1]), (place_ref.at[0], place_ref.at[1]), place_sems)
        for copy in place_loads:
            copy.start()
    speed_at = slice(FEAT, FEAT + LANES)
    for side, col, ccol in ((0, col_lo_ref, ccol_lo_ref), (1, col_hi_ref, ccol_hi_ref)):
        col = col[:, :FEAT].astype(F32)
        ccol = ccol[:, speed_at].astype(F32)
        for r in range(ROWS):
            cols_ref[side, r] = jnp.broadcast_to(col[r : r + 1, :], (EDGE, FEAT))
            ccols_ref[side, r] = jnp.broadcast_to(ccol[r : r + 1, :], (EDGE, LANES))

    lat = slice(0, LANES)
    for copy in loads:
        copy.wait()

    def from_left(whole, edge):
        return jnp.where(iota(whole.shape, 0) == 0, edge, pltpu.roll(whole, 1, 0))

    def from_right(whole, edge):
        count = whole.shape[0]
        return jnp.where(iota(whole.shape, 0) == count - 1, edge, pltpu.roll(whole, count - 1, 0))

    for at_row, side in ((0, 0), (ROWS - 1, 1)):
        low_row = lambda ref, f, halo, at: halo[:, at].astype(F32) if side == 0 else ref[f, 2]
        high_row = lambda ref, f, halo, at: ref[f, 1] if side == 0 else halo[:, at].astype(F32)
        crow = crow_lo_ref if side == 0 else crow_hi_ref
        vrow = row_lo_ref if side == 0 else row_hi_ref
        held = 0 if side == 0 else 3
        mid1 = crow_ref[1, held]
        k = weights_of(
            low_row(crow_ref, 0, crow, speed_at), crow_ref[0, held], high_row(crow_ref, 0, crow, speed_at),
            from_left(mid1, ccols_ref[0, at_row, 0:1, :]), mid1,
            from_right(mid1, ccols_ref[1, at_row, 0:1, :]),
            valid_ref[0] if side == 0 else None,
            valid_ref[1] if side == 1 else None,
        )
        for f in range(FIELDS):
            at = slice(f * LANES, (f + 1) * LANES)
            v = trow_ref[f, held]
            moved = combine(
                k, v, low_row(trow_ref, f, vrow, at), high_row(trow_ref, f, vrow, at),
                from_left(v, cols_ref[0, at_row, 0:1, at]),
                from_right(v, cols_ref[1, at_row, 0:1, at]),
            )
            adv_ref[side * COLS : (side + 1) * COLS, at] = moved
            x_ref[side * COLS : (side + 1) * COLS, at] = moved.astype(BF16)

    def edges(lo_ref, hi_ref, f, r, cols, at):
        lo = lo_ref[f, r, 0:EDGE, :]
        hi = hi_ref[f, r, EDGE : 2 * EDGE, :]
        left = jnp.concatenate(
            [from_left(lo, cols[0, r, :, at]), hi_ref[f, r, EDGE - 1 : 2 * EDGE - 1, :]], axis=0
        )
        right = jnp.concatenate(
            [lo_ref[f, r, 1 : EDGE + 1, :], from_right(hi, cols[1, r, :, at])], axis=0
        )
        return jnp.concatenate([lo, hi], axis=0), left, right

    def both(lo_ref, hi_ref, f, r):
        return jnp.concatenate([lo_ref[f, r, 0:EDGE, :], hi_ref[f, r, EDGE : 2 * EDGE, :]], axis=0)

    def edge_row(i, carry):
        r = i + 1
        spot = pl.multiple_of(2 * COLS + i * 2 * EDGE, 2 * EDGE)
        mid1, left1, right1 = edges(clo_ref, chi_ref, 1, r, ccols_ref, lat)
        k = weights_of(
            both(clo_ref, chi_ref, 0, r - 1), both(clo_ref, chi_ref, 0, r), both(clo_ref, chi_ref, 0, r + 1), left1, mid1, right1
        )
        for f in range(FIELDS):
            at = slice(f * LANES, (f + 1) * LANES)
            v, left, right = edges(tlo_ref, thi_ref, f, r, cols_ref, at)
            moved = combine(k, v, both(tlo_ref, thi_ref, f, r - 1), both(tlo_ref, thi_ref, f, r + 1), left, right)
            adv_ref[pl.ds(spot, 2 * EDGE), at] = moved
            x_ref[pl.ds(spot, 2 * EDGE), at] = moved.astype(BF16)
        return carry

    lax.fori_loop(0, ROWS - 2, edge_row, 0)

    def emit(n, heat):
        for m in range(0, heat.shape[1], LANES):
            at = slice(n + m, n + m + LANES)
            part = heat[:, m : m + LANES]
            f = (n + m) // LANES
            for side, at_row in ((0, 0), (1, ROWS - 1)):
                here = slice(side * COLS, (side + 1) * COLS)
                out_ref[f, at_row] = adv_ref[here, at] + mask_ref[:, at_row : at_row + 1] * part[here]
            for r in range(1, ROWS - 1):
                spot = 2 * COLS + (r - 1) * 2 * EDGE
                lo = slice(spot, spot + EDGE)
                hi = slice(spot + EDGE, spot + 2 * EDGE)
                out_ref[f, r, 0:EDGE, :] = adv_ref[lo, at] + mask_ref[0:EDGE, r : r + 1] * part[lo]
                out_ref[f, r, COLS - EDGE : COLS, :] = (
                    adv_ref[hi, at] + mask_ref[COLS - EDGE : COLS, r : r + 1] * part[hi]
                )

    weight_loads[0].wait()
    net(
        x_ref[...], h1_ref, h2_ref, w1_ref, b1_ref, w2_ref, b2_ref, w3_ref, emit, (),
        lambda n: weight_loads[n].wait(),
    )
    stores = []
    for i, at in enumerate((
        (slice(None), 0),
        (slice(None), ROWS - 1),
        (slice(None), pl.ds(1, ROWS - 2), pl.ds(0, EDGE)),
        (slice(None), pl.ds(1, ROWS - 2), pl.ds(COLS - EDGE, EDGE)),
    )):
        stores.append(pltpu.make_async_copy(out_ref.at[at], out_hbm.at[at], out_sems.at[i]))
        stores[-1].start()

    if not last:
        for f in range(FIELDS):
            at = slice(f * LANES, (f + 1) * LANES)
            srow_lo_ref[:, at] = out_ref[f, 0].astype(BF16)
            srow_hi_ref[:, at] = out_ref[f, ROWS - 1].astype(BF16)
            scol_lo_ref[:, at] = out_ref[f, :, 0].astype(BF16)
            scol_hi_ref[:, at] = out_ref[f, :, COLS - 1].astype(BF16)
        for store in stores:
            store.wait()
        return
    centre_load.wait()
    for copy in place_loads:
        copy.wait()
    flat = out_ref.reshape(FIELDS * CELLS, LANES)
    half = FEAT // 2
    columns = [
        jnp.concatenate(
            [flat[pl.ds(f * CELLS + c, SEGS, stride=2), :] for f in (2, 3)], axis=1
        ).astype(BF16)
        for c in range(2)
    ]
    pack_ref[:, 2 * FEAT :] = tags_ref[...]
    for i, b in enumerate(range(0, SEGS, 256)):
        for q in range(2):
            for c in range(2):
                pack_ref[b : b + 256, q * FEAT + c * half : q * FEAT + (c + 1) * half] = dot(
                    place_ref[q, b : b + 256, :], columns[c]
                ).astype(BF16)
        at = pl.ds(b, 256)
        stores.append(pltpu.make_async_copy(pack_ref.at[at], pack_hbm.at[at], pack_sems.at[i]))
        stores[-1].start()
    for store in stores:
        store.wait()


def rim(last, valid, state, speeds, mask, halo, speed_halo, weights, extra, partial):
    w1, b1, w2, b2, w3 = weights
    hidden = w2.shape[0]
    near = (valid, mask, *halo, *speed_halo, b1, b2)
    far = (in_hbm(state), in_hbm(speeds), in_hbm(w1), in_hbm(w2), in_hbm(w3))
    if last:
        place, tags = extra
        near += (tags,)
        far += (in_hbm(place),)
    far += (in_hbm(partial),)
    outs = [hbm_out((FIELDS, ROWS, COLS, LANES), F32)]
    scratch = [
        pltpu.VMEM((FIELDS, 4, COLS, LANES), F32),
        pltpu.VMEM((FIELDS, ROWS, 2 * EDGE, LANES), F32),
        pltpu.VMEM((FIELDS, ROWS, 2 * EDGE, LANES), F32),
        pltpu.VMEM((2, 4, COLS, LANES), F32),
        pltpu.VMEM((2, ROWS, 2 * EDGE, LANES), F32),
        pltpu.VMEM((2, ROWS, 2 * EDGE, LANES), F32),
        pltpu.VMEM(w1.shape, BF16),
        pltpu.VMEM(w2.shape, BF16),
        pltpu.VMEM(w3.shape, BF16),
        pltpu.VMEM((FIELDS, ROWS, COLS, LANES), F32),
        pltpu.VMEM((RIM, FEAT), BF16),
        pltpu.VMEM((RIM, FEAT), F32),
        pltpu.VMEM((RIM, hidden), BF16),
        pltpu.VMEM((RIM, hidden), BF16),
        pltpu.VMEM((2, ROWS, EDGE, FEAT), F32),
        pltpu.VMEM((2, ROWS, EDGE, LANES), F32),
        pltpu.SemaphoreType.DMA((8,)),
        pltpu.SemaphoreType.DMA((3,)),
        pltpu.SemaphoreType.DMA((4,)),
    ]
    if last:
        outs += [hbm_out((SEGS, 2 * FEAT + LANES), BF16)]
        out_specs = [HBM] * 2
        scratch += [
            pltpu.VMEM((2, SEGS, SEGS), BF16),
            pltpu.VMEM((SEGS, 2 * FEAT + LANES), BF16),
            pltpu.SemaphoreType.DMA((3,)),
            pltpu.SemaphoreType.DMA((SEGS // 256,)),
        ]
    else:
        outs += [jax.ShapeDtypeStruct((COLS, FEAT), BF16)] * 2
        outs += [jax.ShapeDtypeStruct((ROWS, FEAT), BF16)] * 2
        out_specs = [HBM] + [VMEM] * 4
    operands = near + far
    return pl.pallas_call(
        lambda *refs: rim_kernel(last, *refs),
        in_specs=[SMEM] + [VMEM] * (len(near) - 1) + [HBM] * len(far),
        out_specs=out_specs,
        out_shape=outs,
        input_output_aliases={len(operands) - 1: 0},
        scratch_shapes=scratch,
        compiler_params=params(),
        cost_estimate=cost(4_000_000_000, 4 << 20),
        name="rim_last" if last else "rim",
    )(*operands)


def unturn_kernel(t_hbm, out_ref, t_ref, stage_ref, in_sems, sems):
    size = LANES * ROWS
    loads = [pltpu.make_async_copy(t_hbm.at[f], t_ref.at[f], in_sems.at[f]) for f in range(FIELDS)]
    stores = [
        pltpu.make_async_copy(stage_ref.at[f], out_ref.at[pl.ds(f * size, size)], sems.at[f])
        for f in range(FIELDS)
    ]
    for load in loads:
        load.start()
    for f in range(FIELDS):
        loads[f].wait()
        for r in range(ROWS):
            stage_ref[f, pl.ds(r, LANES, stride=ROWS), :] = t_ref[f, r].T
        stores[f].start()
    for store in stores:
        store.wait()


def unturn(state):
    return pl.pallas_call(
        unturn_kernel,
        in_specs=[HBM],
        out_specs=HBM,
        out_shape=hbm_out((FIELDS * LANES * ROWS, COLS), F32),
        scratch_shapes=[
            pltpu.VMEM((FIELDS, ROWS, COLS, LANES), F32),
            pltpu.VMEM((FIELDS, LANES * ROWS, COLS), F32),
            pltpu.SemaphoreType.DMA((FIELDS,)),
            pltpu.SemaphoreType.DMA((FIELDS,)),
        ],
        compiler_params=params(),
        cost_estimate=cost(1_000_000_000, 8 << 20),
        name="unturn",
    )(in_hbm(state))


def chem_kernel(
    arr_ref, regrid_ref, w1_ref, b1_ref, w2_ref, out_hbm, want_ref, mix_ref, x_ref, h_ref, out_ref, sems
):
    from_cell = iota((LANES, LANES), 0)
    to_lane = iota((LANES, LANES), 1)
    source_cell = jnp.where(to_lane < 64, 2 * to_lane, 2 * (to_lane - 64) + 1)
    split = (from_cell == source_cell).astype(F32).astype(BF16)
    mix_ref[...] = dot(regrid_ref[...], split).astype(BF16)
    lane = iota((8, LANES), 1)
    which = iota((8, LANES), 0)
    pick = jnp.where(lane == 2 * which, 32.0, jnp.where(lane == 2 * which + 1, 1.0, 0.0))
    pick = jnp.where(which < 2, pick, 0.0).astype(BF16)
    want_ref[...] = dot_nt(pick, arr_ref[:, 2 * FEAT :]).astype(jnp.int32) - 1
    span = 256
    half = FEAT // 2
    stores = []
    for i in range(SEGS // span):
        start = i * span
        placed = []
        for q in range(2):
            chosen = (iota((span, SEGS), 0) + start == want_ref[q : q + 1, :]).astype(F32).astype(BF16)
            placed.append(dot(chosen, arr_ref[:, q * FEAT : (q + 1) * FEAT]))
        placed = (placed[0] + placed[1]).astype(BF16)
        for b in range(span // 64):
            cells = jnp.concatenate(
                [placed[b * 64 : (b + 1) * 64, :half], placed[b * 64 : (b + 1) * 64, half:]], axis=0
            )
            spot = 2 * start + b * LANES
            x_ref[i % 2, b * LANES : (b + 1) * LANES, :] = dot(
                mix_ref[spot : spot + LANES, :], cells
            ).astype(BF16)
        x = x_ref[i % 2]
        for n in range(0, w1_ref.shape[1], 256):
            u = dot(x, w1_ref[:, n : n + 256]) + b1_ref[:, n : n + 256]
            h_ref[i % 2, :, n : n + 256] = silu(u).astype(BF16)
        rows = slice(2 * start, 2 * (start + span))
        out_ref[rows, :] = dot(h_ref[i % 2], w2_ref[...]).astype(BF16)
        at = pl.ds(2 * start, 2 * span)
        stores.append(pltpu.make_async_copy(out_ref.at[at], out_hbm.at[at], sems.at[i]))
        stores[-1].start()
    for store in stores:
        store.wait()


def chem(arrived, regrid_weights, w1, b1, w2):
    return pl.pallas_call(
        chem_kernel,
        in_specs=[VMEM] * 5,
        out_specs=HBM,
        out_shape=hbm_out((CELLS, w2.shape[1]), BF16),
        scratch_shapes=[
            pltpu.VMEM((8, SEGS), jnp.int32),
            pltpu.VMEM((CELLS, LANES), BF16),
            pltpu.VMEM((2, 512, FEAT // 2), BF16),
            pltpu.VMEM((2, 512, w1.shape[1]), BF16),
            pltpu.VMEM((CELLS, w2.shape[1]), BF16),
            pltpu.SemaphoreType.DMA((SEGS // 256,)),
        ],
        compiler_params=params(),
        cost_estimate=cost(4_400_000_000, 4 << 20),
        name="chem",
    )(
        in_vmem(arrived),
        in_vmem(regrid_weights.reshape(CELLS, LANES)),
        in_vmem(w1),
        b1,
        in_vmem(w2),
    )


def swap(low, high):
    rows, columns = lax.axis_size("gx"), lax.axis_size("gy")
    up = [(i, i + 1) for i in range(rows - 1)]
    down = [(i + 1, i) for i in range(rows - 1)]
    right = [(i, (i + 1) % columns) for i in range(columns)]
    left = [((i + 1) % columns, i) for i in range(columns)]
    row_lo, col_lo = low
    row_hi, col_hi = high
    return (
        lax.ppermute(row_hi, "gx", up),
        lax.ppermute(row_lo, "gx", down),
        lax.ppermute(col_hi, "gy", right),
        lax.ppermute(col_lo, "gy", left),
    )


def local(
    fields, courant, sun_columns, rad_w1, rad_b1, rad_w2, rad_b2, rad_w3,
    segment_route, regrid_weights, chem_w1, chem_b1, chem_w2,
):
    place_at = lax.axis_index("gx")
    valid = jnp.stack([place_at > 0, place_at < lax.axis_size("gx") - 1]).astype(F32)
    weights = (rad_w1, rad_b1.reshape(1, -1), rad_w2, rad_b2.reshape(1, -1), rad_w3)

    state, speeds, row_lo, row_hi, col_lo, col_hi = turn(fields, courant)
    speed_halo = swap((row_lo, col_lo), (row_hi, col_hi))
    mask, place, tags = plan(sun_columns, segment_route)
    partial = inner(state, speeds, mask, weights)
    state, row_lo, row_hi, col_lo, col_hi = rim(
        False, valid, state, speeds, mask, speed_halo, speed_halo, weights, (), partial
    )
    halo = swap((row_lo, col_lo), (row_hi, col_hi))
    partial = inner(state, speeds, mask, weights)
    state, packed = rim(
        True, valid, state, speeds, mask, halo, speed_halo, weights, (place, tags), partial
    )
    tiles = lax.axis_size("gx") * lax.axis_size("gy")
    packed = packed.reshape(tiles, SEGS // tiles, packed.shape[1])
    arrived = lax.all_to_all(packed, ("gx", "gy"), split_axis=0, concat_axis=0, tiled=True)
    fields_out = unturn(state).reshape(fields.shape)
    output = chem(
        arrived.reshape(SEGS, arrived.shape[2]), regrid_weights, chem_w1, chem_b1.reshape(1, -1), chem_w2
    )
    return fields_out, output.reshape(1, 1, CELLS, -1)


def solution(mesh):
    return jax.shard_map(
        local,
        mesh=mesh,
        in_specs=(
            P(None, None, "gx", "gy"),
            P(None, None, "gx", "gy"),
            P("gx", "gy", None),
            P(),
            P(),
            P(),
            P(),
            P(),
            P(None, "gx", "gy", None),
            P("gx", "gy", None, None, None),
            P(),
            P(),
            P(),
        ),
        out_specs=(P(None, None, "gx", "gy"), P("gx", "gy", None, None)),
        check_vma=False,
    )
```

```python
import jax
import jax.numpy as jnp
from jax import lax
from jax.experimental import pallas as pl
from jax.experimental.pallas import tpu as pltpu
from jax.sharding import PartitionSpec as P

F32 = jnp.float32
BF16 = jnp.bfloat16
LANES = 128
FIELDS = 4
ROWS = 16
COLS = 128
FEAT = FIELDS * LANES
CELLS = ROWS * COLS
SEGS = CELLS // 2
EDGE = 8
GROUP = 4
MIB = 1024 * 1024

VMEM = pl.BlockSpec(memory_space=pltpu.VMEM)
SMEM = pl.BlockSpec(memory_space=pltpu.SMEM)
ANY = pl.BlockSpec(memory_space=pl.ANY)


HBM = pl.BlockSpec(memory_space=pltpu.HBM)


def hbm_out(shape, dtype):
    return pltpu.HBM(shape, dtype)


def in_vmem(x):
    return pltpu.with_memory_space_constraint(x, pltpu.VMEM)


def in_hbm(x):
    return pltpu.with_memory_space_constraint(x, pltpu.HBM)


def params(mib):
    return pltpu.CompilerParams(vmem_limit_bytes=mib * MIB)


def cost(flops, bytes_accessed=0):
    return pl.CostEstimate(flops=flops, bytes_accessed=bytes_accessed, transcendentals=0)


def dot(a, b):
    return jnp.dot(a, b, preferred_element_type=F32)


def dot_nt(a, b):
    return lax.dot_general(a, b, (((1,), (1,)), ((), ())), preferred_element_type=F32)


def silu(u):
    half = 0.5 * u
    return half + half * jnp.tanh(half)


def iota(shape, dim):
    return lax.broadcasted_iota(jnp.int32, shape, dim)


def turn_kernel(f_ref, c_ref, t_ref, cc_ref, row_lo_ref, row_hi_ref, col_lo_ref, col_hi_ref):
    step = pl.program_id(0)

    @pl.when(step < FIELDS)
    def _():
        for r in range(ROWS):
            block = f_ref[pl.ds(r, LANES, stride=ROWS), :].T
            t_ref[0, r] = block
            if r == 0:
                row_lo_ref[...] = block.astype(BF16)
            if r == ROWS - 1:
                row_hi_ref[...] = block.astype(BF16)
        col_lo_ref[...] = t_ref[0, :, 0, :].astype(BF16)
        col_hi_ref[...] = t_ref[0, :, COLS - 1, :].astype(BF16)

    @pl.when(step >= FIELDS)
    def _():
        for r in range(ROWS):
            cc_ref[0, r] = c_ref[pl.ds(r, LANES, stride=ROWS), :].T

    @pl.when(step == FIELDS)
    def _():
        row_lo_ref[...] = cc_ref[0, 0].astype(BF16)
        row_hi_ref[...] = cc_ref[0, ROWS - 1].astype(BF16)

    @pl.when(step == FIELDS + 1)
    def _():
        col_lo_ref[...] = cc_ref[0, :, 0, :].astype(BF16)
        col_hi_ref[...] = cc_ref[0, :, COLS - 1, :].astype(BF16)


def turn(fields, courant):
    flat_f = in_hbm(fields.reshape(FIELDS * LANES * ROWS, COLS))
    flat_c = in_hbm(courant.reshape(2 * LANES * ROWS, COLS))
    field_at = lambda i: jnp.minimum(i, FIELDS - 1)
    speed_at = lambda i: jnp.maximum(i - FIELDS, 0)
    halo_at = lambda i: jnp.minimum(i, FIELDS)
    return pl.pallas_call(
        turn_kernel,
        grid=(FIELDS + 2,),
        in_specs=[
            pl.BlockSpec((LANES * ROWS, COLS), lambda i: (field_at(i), 0)),
            pl.BlockSpec((LANES * ROWS, COLS), lambda i: (speed_at(i), 0)),
        ],
        out_specs=[
            pl.BlockSpec((1, ROWS, COLS, LANES), lambda i: (field_at(i), 0, 0, 0)),
            pl.BlockSpec((1, ROWS, COLS, LANES), lambda i: (speed_at(i), 0, 0, 0)),
            pl.BlockSpec((COLS, LANES), lambda i: (0, halo_at(i))),
            pl.BlockSpec((COLS, LANES), lambda i: (0, halo_at(i))),
            pl.BlockSpec((ROWS, LANES), lambda i: (0, halo_at(i))),
            pl.BlockSpec((ROWS, LANES), lambda i: (0, halo_at(i))),
        ],
        out_shape=[
            jax.ShapeDtypeStruct((FIELDS, ROWS, COLS, LANES), F32),
            jax.ShapeDtypeStruct((2, ROWS, COLS, LANES), F32),
            jax.ShapeDtypeStruct((COLS, FEAT + LANES), BF16),
            jax.ShapeDtypeStruct((COLS, FEAT + LANES), BF16),
            jax.ShapeDtypeStruct((ROWS, FEAT + LANES), BF16),
            jax.ShapeDtypeStruct((ROWS, FEAT + LANES), BF16),
        ],
        compiler_params=params(14),
        cost_estimate=cost(20_000_000, 12 << 20),
        name="turn",
    )(flat_f, flat_c)


def plan_kernel(sun_ref, route_ref, mask_ref, place_ref, tags_ref, stage_ref, sems):
    slots = sun_ref[...]
    low = (iota((COLS, CELLS), 0) == (slots & (COLS - 1))).astype(F32).astype(BF16)
    high = (iota((LANES, CELLS), 0) == (slots >> 7)).astype(F32).astype(BF16)
    lit = dot_nt(low, high)
    mask_ref[...] = lit

    target = route_ref[0, 0]
    arrival = route_ref[1, 0] + 1
    before = (iota((LANES, LANES), 0) < iota((LANES, LANES), 1)).astype(F32).astype(BF16)
    ones = jnp.ones((LANES, LANES), BF16)
    carry = jnp.zeros((LANES, LANES), F32)
    ranks = []
    for b in range(SEGS // LANES):
        goes = (iota((LANES, LANES), 0) == target[:, b * LANES : (b + 1) * LANES]).astype(F32)
        goes16 = goes.astype(BF16)
        ranks.append(jnp.sum(goes * (dot(goes16, before) + carry), axis=0, keepdims=True))
        carry = carry + dot(goes16, ones)
    rank = jnp.concatenate(ranks, axis=1).astype(jnp.int32)
    row = target * 16 + rank
    index = iota((LANES, SEGS), 0)
    coarse = (arrival >> 5).astype(F32)
    fine = (arrival & 31).astype(F32)
    tag_rows = [
        jnp.where(index == 2 * q, coarse, jnp.where(index == 2 * q + 1, fine, 0.0)).astype(BF16)
        for q in range(2)
    ]
    for b in range(SEGS // LANES):
        tags = jnp.zeros((LANES, LANES), F32)
        for q in range(2):
            want = 2 * (iota((LANES, SEGS), 0) + b * LANES) + q
            chosen = (row == want).astype(F32).astype(BF16)
            at = (q, slice(b * LANES, (b + 1) * LANES))
            stage_ref[at] = chosen
            pltpu.make_async_copy(stage_ref.at[at], place_ref.at[at], sems.at[q, b]).start()
            tags = tags + dot_nt(chosen, tag_rows[q])
        tags_ref[b * LANES : (b + 1) * LANES, :] = tags.astype(BF16)
    for b in range(SEGS // LANES):
        for q in range(2):
            at = (q, slice(b * LANES, (b + 1) * LANES))
            pltpu.make_async_copy(stage_ref.at[at], place_ref.at[at], sems.at[q, b]).wait()


def plan(sun_columns, segment_route):
    return pl.pallas_call(
        plan_kernel,
        in_specs=[VMEM] * 2,
        out_specs=[VMEM, ANY, VMEM],
        out_shape=[
            jax.ShapeDtypeStruct((COLS, LANES), F32),
            jax.ShapeDtypeStruct((2, SEGS, SEGS), BF16),
            jax.ShapeDtypeStruct((SEGS, LANES), BF16),
        ],
        scratch_shapes=[
            pltpu.VMEM((2, SEGS, SEGS), BF16),
            pltpu.SemaphoreType.DMA((2, SEGS // LANES)),
        ],
        compiler_params=params(10),
        cost_estimate=cost(3_000_000_000, 1 << 20),
        name="plan",
    )(sun_columns.reshape(1, CELLS), segment_route)


def weights_of(lo0, mid0, hi0, left1, mid1, right1):
    f_lo = 0.5 * (lo0 + mid0)
    f_hi = 0.5 * (mid0 + hi0)
    g_lo = 0.5 * (left1 + mid1)
    g_hi = 0.5 * (mid1 + right1)
    keep = (
        1.0
        - jnp.maximum(f_hi, 0.0)
        + jnp.minimum(f_lo, 0.0)
        - jnp.maximum(g_hi, 0.0)
        + jnp.minimum(g_lo, 0.0)
    )
    return (
        keep,
        jnp.maximum(f_lo, 0.0),
        -jnp.minimum(f_hi, 0.0),
        jnp.maximum(g_lo, 0.0),
        -jnp.minimum(g_hi, 0.0),
    )


def combine(k, mid, lo, hi, left, right):
    return k[0] * mid + k[1] * lo + k[2] * hi + k[3] * left + k[4] * right


def net(x, h1_ref, h2_ref, w1_ref, b1_ref, w2_ref, b2_ref, w3_ref, emit):
    hidden = w2_ref.shape[0]
    wide = 256
    for n in range(0, hidden, wide):
        u = dot(x, w1_ref[:, n : n + wide]) + b1_ref[:, n : n + wide]
        h1_ref[:, n : n + wide] = silu(u).astype(BF16)
    h1 = h1_ref[...]
    for n in range(0, hidden, wide):
        u = dot(h1, w2_ref[:, n : n + wide]) + b2_ref[:, n : n + wide]
        h2_ref[:, n : n + wide] = silu(u).astype(BF16)
    h2 = h2_ref[...]
    for n in range(0, FEAT, wide):
        emit(n, dot(h2, w3_ref[:, n : n + wide]))


def step_kernel(
    last,
    mask_ref,
    row_lo_ref, row_hi_ref, col_lo_ref, col_hi_ref,
    crow_lo_ref, crow_hi_ref, ccol_lo_ref, ccol_hi_ref,
    w1_ref, b1_ref, w2_ref, b2_ref, w3_ref, *rest,
):
    if last:
        tags_ref, t_any, c_any, place_any, out_any, pack_any = rest[:6]
        rest = rest[6:]
    else:
        t_any, c_any, out_any, srow_lo_ref, srow_hi_ref, scol_lo_ref, scol_hi_ref = rest[:7]
        rest = rest[7:]
    v_ref, c_ref, lit_ref, out_ref, x_ref, adv_ref, h1_ref, h2_ref, t_sems, c_sems, out_sems = rest[:11]
    if last:
        place_ref, pack_ref, place_sem, pack_sems = rest[11:]
    mid = slice(EDGE, EDGE + COLS)
    left = slice(EDGE - 1, EDGE + COLS - 1)
    right = slice(EDGE + 1, EDGE + COLS + 1)
    inside = pl.ds(EDGE, COLS)

    def load(r):
        return (
            pltpu.make_async_copy(t_any.at[:, r], v_ref.at[:, r + 1, inside], t_sems.at[r]),
            pltpu.make_async_copy(c_any.at[:, r], c_ref.at[:, r + 1, inside], c_sems.at[r]),
        )

    def store(g):
        rows = pl.ds(g * GROUP, GROUP)
        return pltpu.make_async_copy(out_ref.at[:, rows], out_any.at[:, rows], out_sems.at[g])

    first, final = 0, ROWS - 1
    order = [first, final] + list(range(1, ROWS - 1))
    for r in order:
        for copy in load(r):
            copy.start()
    if last:
        place_load = pltpu.make_async_copy(place_any, place_ref, place_sem.at[0])
        place_load.start()

    speed_at = slice(FEAT, FEAT + LANES)
    for f in range(FIELDS):
        at = slice(f * LANES, (f + 1) * LANES)
        v_ref[f, 0, mid, :] = row_lo_ref[:, at].astype(F32)
        v_ref[f, ROWS + 1, mid, :] = row_hi_ref[:, at].astype(F32)
        low = col_lo_ref[:, at].astype(F32)
        high = col_hi_ref[:, at].astype(F32)
        for r in range(ROWS):
            v_ref[f, r + 1, EDGE - 1 : EDGE, :] = low[r : r + 1, :]
            v_ref[f, r + 1, EDGE + COLS : EDGE + COLS + 1, :] = high[r : r + 1, :]
    low = ccol_lo_ref[:, speed_at].astype(F32)
    high = ccol_hi_ref[:, speed_at].astype(F32)
    for r in range(ROWS):
        c_ref[1, r + 1, EDGE - 1 : EDGE, :] = low[r : r + 1, :]
        c_ref[1, r + 1, EDGE + COLS : EDGE + COLS + 1, :] = high[r : r + 1, :]
        lit_ref[r] = jnp.broadcast_to(mask_ref[:, r : r + 1], (COLS, LANES))
    for r in (first, final):
        for copy in load(r):
            copy.wait()
    for spot, held, halo_ref, flag in (
        (0, 1, crow_lo_ref, lax.axis_index("gx") > 0),
        (ROWS + 1, ROWS, crow_hi_ref, lax.axis_index("gx") < lax.axis_size("gx") - 1),
    ):
        halo = halo_ref[:, speed_at].astype(F32)
        c_ref[0, spot, mid, :] = jnp.where(flag, halo, -c_ref[0, held, mid, :])

    def body(g, carry):
        for j in range(GROUP):
            r = g * GROUP + 1 + j

            def arrive():
                for copy in load(r):
                    copy.wait()

            if j < GROUP - 2:
                arrive()
            else:
                pl.when(r < final)(arrive)
        for j in range(GROUP):
            r = g * GROUP + j + 1
            k = weights_of(
                c_ref[0, r - 1, mid, :], c_ref[0, r, mid, :], c_ref[0, r + 1, mid, :],
                c_ref[1, r, left, :], c_ref[1, r, mid, :], c_ref[1, r, right, :],
            )
            for f in range(FIELDS):
                at = slice(f * LANES, (f + 1) * LANES)
                moved = combine(
                    k, v_ref[f, r, mid, :], v_ref[f, r - 1, mid, :], v_ref[f, r + 1, mid, :],
                    v_ref[f, r, left, :], v_ref[f, r, right, :],
                )
                adv_ref[j * COLS : (j + 1) * COLS, at] = moved
                x_ref[j * COLS : (j + 1) * COLS, at] = moved.astype(BF16)

        def emit(n, heat):
            for j in range(GROUP):
                r = g * GROUP + j
                for m in range(0, heat.shape[1], LANES):
                    here = slice(j * COLS, (j + 1) * COLS)
                    out_ref[(n + m) // LANES, r] = (
                        adv_ref[here, n + m : n + m + LANES] + lit_ref[r] * heat[here, m : m + LANES]
                    )

        net(x_ref[...], h1_ref, h2_ref, w1_ref, b1_ref, w2_ref, b2_ref, w3_ref, emit)
        store(g).start()
        return carry

    lax.fori_loop(0, ROWS // GROUP, body, 0)
    stores = [store(g) for g in range(ROWS // GROUP)]

    if not last:
        for f in range(FIELDS):
            at = slice(f * LANES, (f + 1) * LANES)
            srow_lo_ref[:, at] = out_ref[f, 0].astype(BF16)
            srow_hi_ref[:, at] = out_ref[f, ROWS - 1].astype(BF16)
            scol_lo_ref[:, at] = out_ref[f, :, 0].astype(BF16)
            scol_hi_ref[:, at] = out_ref[f, :, COLS - 1].astype(BF16)
        for copy in stores:
            copy.wait()
        return
    place_load.wait()
    flat = out_ref.reshape(FIELDS * CELLS, LANES)
    half = FEAT // 2
    columns = [
        jnp.concatenate(
            [flat[pl.ds(f * CELLS + c, SEGS, stride=2), :] for f in (2, 3)], axis=1
        ).astype(BF16)
        for c in range(2)
    ]
    pack_ref[:, 2 * FEAT :] = tags_ref[...]
    for i, b in enumerate(range(0, SEGS, 256)):
        for q in range(2):
            for c in range(2):
                pack_ref[b : b + 256, q * FEAT + c * half : q * FEAT + (c + 1) * half] = dot(
                    place_ref[q, b : b + 256, :], columns[c]
                ).astype(BF16)
        at = pl.ds(b, 256)
        stores.append(pltpu.make_async_copy(pack_ref.at[at], pack_any.at[at], pack_sems.at[i]))
        stores[-1].start()
    for copy in stores:
        copy.wait()


def step(last, state, speeds, mask, halo, speed_halo, weights, extra):
    w1, b1, w2, b2, w3 = weights
    hidden = w2.shape[0]
    many = GROUP * COLS
    near = (mask, *halo, *speed_halo, in_vmem(w1), b1, in_vmem(w2), b2, in_vmem(w3))
    far = (state, speeds)
    outs = [jax.ShapeDtypeStruct((FIELDS, ROWS, COLS, LANES), F32)]
    scratch = [
        pltpu.VMEM((FIELDS, ROWS + 2, COLS + 2 * EDGE, LANES), F32),
        pltpu.VMEM((2, ROWS + 2, COLS + 2 * EDGE, LANES), F32),
        pltpu.VMEM((ROWS, COLS, LANES), F32),
        pltpu.VMEM((FIELDS, ROWS, COLS, LANES), F32),
        pltpu.VMEM((many, FEAT), BF16),
        pltpu.VMEM((many, FEAT), F32),
        pltpu.VMEM((many, hidden), BF16),
        pltpu.VMEM((many, hidden), BF16),
        pltpu.SemaphoreType.DMA((ROWS,)),
        pltpu.SemaphoreType.DMA((ROWS,)),
        pltpu.SemaphoreType.DMA((ROWS // GROUP,)),
    ]
    if last:
        place, tags = extra
        near += (tags,)
        far += (place,)
        outs = [hbm_out((FIELDS, ROWS, COLS, LANES), F32)]
        outs += [jax.ShapeDtypeStruct((SEGS, 2 * FEAT + LANES), BF16)]
        out_specs = [HBM, ANY]
        scratch += [
            pltpu.VMEM((2, SEGS, SEGS), BF16),
            pltpu.VMEM((SEGS, 2 * FEAT + LANES), BF16),
            pltpu.SemaphoreType.DMA((1,)),
            pltpu.SemaphoreType.DMA((SEGS // 256,)),
        ]
    else:
        outs += [jax.ShapeDtypeStruct((COLS, FEAT), BF16)] * 2
        outs += [jax.ShapeDtypeStruct((ROWS, FEAT), BF16)] * 2
        out_specs = [ANY] + [VMEM] * 4
    return pl.pallas_call(
        lambda *refs: step_kernel(last, *refs),
        in_specs=[VMEM] * len(near) + [ANY] * len(far),
        out_specs=out_specs,
        out_shape=outs,
        scratch_shapes=scratch,
        compiler_params=params(30 if last else 22),
        cost_estimate=cost(10_000_000_000, 4 << 20),
        name="step_last" if last else "step",
    )(*near, *far)


def unturn_kernel(t_hbm, out_ref, t_ref, stage_ref, in_sems, sems):
    size = LANES * ROWS
    loads = [pltpu.make_async_copy(t_hbm.at[f], t_ref.at[f], in_sems.at[f]) for f in range(FIELDS)]
    stores = [
        pltpu.make_async_copy(stage_ref.at[f], out_ref.at[pl.ds(f * size, size)], sems.at[f])
        for f in range(FIELDS)
    ]
    for load in loads:
        load.start()
    for f in range(FIELDS):
        loads[f].wait()
        for r in range(ROWS):
            stage_ref[f, pl.ds(r, LANES, stride=ROWS), :] = t_ref[f, r].T
        stores[f].start()
    for store in stores:
        store.wait()


def unturn(state):
    return pl.pallas_call(
        unturn_kernel,
        in_specs=[HBM],
        out_specs=HBM,
        out_shape=hbm_out((FIELDS * LANES * ROWS, COLS), F32),
        scratch_shapes=[
            pltpu.VMEM((FIELDS, ROWS, COLS, LANES), F32),
            pltpu.VMEM((FIELDS, LANES * ROWS, COLS), F32),
            pltpu.SemaphoreType.DMA((FIELDS,)),
            pltpu.SemaphoreType.DMA((FIELDS,)),
        ],
        compiler_params=params(12),
        cost_estimate=cost(1_000_000_000, 8 << 20),
        name="unturn",
    )(in_hbm(state))


def chem_kernel(
    arr_ref, regrid_ref, w1_ref, b1_ref, w2_hbm, out_hbm,
    want_ref, mix_ref, x_ref, h_ref, out_ref, w2_ref, sems, w_sem,
):
    w2_load = pltpu.make_async_copy(w2_hbm, w2_ref, w_sem.at[0])
    w2_load.start()
    from_cell = iota((LANES, LANES), 0)
    to_lane = iota((LANES, LANES), 1)
    source_cell = jnp.where(to_lane < 64, 2 * to_lane, 2 * (to_lane - 64) + 1)
    split = (from_cell == source_cell).astype(F32).astype(BF16)
    mix_ref[...] = dot(regrid_ref[...], split).astype(BF16)
    lane = iota((8, LANES), 1)
    which = iota((8, LANES), 0)
    pick = jnp.where(lane == 2 * which, 32.0, jnp.where(lane == 2 * which + 1, 1.0, 0.0))
    pick = jnp.where(which < 2, pick, 0.0).astype(BF16)
    want_ref[...] = dot_nt(pick, arr_ref[:, 2 * FEAT :]).astype(jnp.int32) - 1
    span = 256
    half = FEAT // 2
    stores = []
    for i in range(SEGS // span):
        start = i * span
        placed = []
        for q in range(2):
            chosen = (iota((span, SEGS), 0) + start == want_ref[q : q + 1, :]).astype(F32).astype(BF16)
            placed.append(dot(chosen, arr_ref[:, q * FEAT : (q + 1) * FEAT]))
        placed = (placed[0] + placed[1]).astype(BF16)
        for b in range(span // 64):
            cells = jnp.concatenate(
                [placed[b * 64 : (b + 1) * 64, :half], placed[b * 64 : (b + 1) * 64, half:]], axis=0
            )
            spot = 2 * start + b * LANES
            x_ref[i % 2, b * LANES : (b + 1) * LANES, :] = dot(
                mix_ref[spot : spot + LANES, :], cells
            ).astype(BF16)
        x = x_ref[i % 2]
        for n in range(0, w1_ref.shape[1], 256):
            u = dot(x, w1_ref[:, n : n + 256]) + b1_ref[:, n : n + 256]
            h_ref[i % 2, :, n : n + 256] = silu(u).astype(BF16)
        if i == 0:
            w2_load.wait()
        rows = slice(2 * start, 2 * (start + span))
        out_ref[rows, :] = dot(h_ref[i % 2], w2_ref[...]).astype(BF16)
        at = pl.ds(2 * start, 2 * span)
        stores.append(pltpu.make_async_copy(out_ref.at[at], out_hbm.at[at], sems.at[i]))
        stores[-1].start()
    for store in stores:
        store.wait()


def chem(arrived, regrid_weights, w1, b1, w2):
    return pl.pallas_call(
        chem_kernel,
        in_specs=[VMEM] * 4 + [HBM],
        out_specs=HBM,
        out_shape=hbm_out((CELLS, w2.shape[1]), BF16),
        scratch_shapes=[
            pltpu.VMEM((8, SEGS), jnp.int32),
            pltpu.VMEM((CELLS, LANES), BF16),
            pltpu.VMEM((2, 512, FEAT // 2), BF16),
            pltpu.VMEM((2, 512, w1.shape[1]), BF16),
            pltpu.VMEM((CELLS, w2.shape[1]), BF16),
            pltpu.VMEM(w2.shape, BF16),
            pltpu.SemaphoreType.DMA((SEGS // 256,)),
            pltpu.SemaphoreType.DMA((1,)),
        ],
        compiler_params=params(14),
        cost_estimate=cost(4_400_000_000, 4 << 20),
        name="chem",
    )(
        in_vmem(arrived),
        in_vmem(regrid_weights.reshape(CELLS, LANES)),
        in_vmem(w1),
        b1,
        in_hbm(w2),
    )


def swap(low, high):
    rows, columns = lax.axis_size("gx"), lax.axis_size("gy")
    up = [(i, i + 1) for i in range(rows - 1)]
    down = [(i + 1, i) for i in range(rows - 1)]
    right = [(i, (i + 1) % columns) for i in range(columns)]
    left = [((i + 1) % columns, i) for i in range(columns)]
    row_lo, col_lo = low
    row_hi, col_hi = high
    return (
        lax.ppermute(row_hi, "gx", up),
        lax.ppermute(row_lo, "gx", down),
        lax.ppermute(col_hi, "gy", right),
        lax.ppermute(col_lo, "gy", left),
    )


def local(
    fields, courant, sun_columns, rad_w1, rad_b1, rad_w2, rad_b2, rad_w3,
    segment_route, regrid_weights, chem_w1, chem_b1, chem_w2,
):
    weights = (rad_w1, rad_b1.reshape(1, -1), rad_w2, rad_b2.reshape(1, -1), rad_w3)

    state, speeds, row_lo, row_hi, col_lo, col_hi = turn(fields, courant)
    speed_halo = swap((row_lo, col_lo), (row_hi, col_hi))
    mask, place, tags = plan(sun_columns, segment_route)
    state, row_lo, row_hi, col_lo, col_hi = step(
        False, state, speeds, mask, speed_halo, speed_halo, weights, ()
    )
    halo = swap((row_lo, col_lo), (row_hi, col_hi))
    state, packed = step(
        True, state, speeds, mask, halo, speed_halo, weights, (place, tags)
    )
    tiles = lax.axis_size("gx") * lax.axis_size("gy")
    packed = packed.reshape(tiles, SEGS // tiles, packed.shape[1])
    arrived = lax.all_to_all(packed, ("gx", "gy"), split_axis=0, concat_axis=0, tiled=True)
    fields_out = unturn(state).reshape(fields.shape)
    output = chem(
        arrived.reshape(SEGS, arrived.shape[2]), regrid_weights, chem_w1, chem_b1.reshape(1, -1), chem_w2
    )
    return fields_out, output.reshape(1, 1, CELLS, -1)


def solution(mesh):
    return jax.shard_map(
        local,
        mesh=mesh,
        in_specs=(
            P(None, None, "gx", "gy"),
            P(None, None, "gx", "gy"),
            P("gx", "gy", None),
            P(),
            P(),
            P(),
            P(),
            P(),
            P(None, "gx", "gy", None),
            P("gx", "gy", None, None, None),
            P(),
            P(),
            P(),
        ),
        out_specs=(P(None, None, "gx", "gy"), P("gx", "gy", None, None)),
        check_vma=False,
    )
```

```python
import jax
import jax.numpy as jnp
from jax import lax
from jax.experimental import pallas as pl
from jax.experimental.pallas import tpu as pltpu
from jax.sharding import PartitionSpec as P

F32 = jnp.float32
BF16 = jnp.bfloat16
LANES = 128
FIELDS = 4
ROWS = 16
COLS = 128
FEAT = FIELDS * LANES
CELLS = ROWS * COLS
SEGS = CELLS // 2
EDGE = 8
GROUP = 4
PIECES = ((1, 4), (5, 4), (9, 3), (12, 3))
INNER = COLS - 2 * EDGE
RIM = 2 * COLS + (ROWS - 2) * 2 * EDGE
MARGIN = (ROWS + 2, COLS + 2 * EDGE, LANES)
MIB = 1024 * 1024

VMEM = pl.BlockSpec(memory_space=pltpu.VMEM)
SMEM = pl.BlockSpec(memory_space=pltpu.SMEM)
ANY = pl.BlockSpec(memory_space=pl.ANY)


HBM = pl.BlockSpec(memory_space=pltpu.HBM)


def vmem_out(shape, dtype):
    return pltpu.VMEM(shape, dtype)


def hbm_out(shape, dtype):
    return pltpu.HBM(shape, dtype)


def in_vmem(x):
    return pltpu.with_memory_space_constraint(x, pltpu.VMEM)


def in_hbm(x):
    return pltpu.with_memory_space_constraint(x, pltpu.HBM)


def params(mib):
    return pltpu.CompilerParams(vmem_limit_bytes=mib * MIB)


def cost(flops, bytes_accessed=0):
    return pl.CostEstimate(flops=flops, bytes_accessed=bytes_accessed, transcendentals=0)


def dot(a, b):
    return jnp.dot(a, b, preferred_element_type=F32)


def dot_nt(a, b):
    return lax.dot_general(a, b, (((1,), (1,)), ((), ())), preferred_element_type=F32)


def silu(u):
    half = 0.5 * u
    return half + half * jnp.tanh(half)


def iota(shape, dim):
    return lax.broadcasted_iota(jnp.int32, shape, dim)


def turn_kernel(f_hbm, c_hbm, t_ref, cc_ref, row_lo_ref, row_hi_ref, col_lo_ref, col_hi_ref, f_ref, c_ref, sems):
    size = LANES * ROWS
    inside = slice(EDGE, EDGE + COLS)
    loads = [
        pltpu.make_async_copy(f_hbm.at[pl.ds(i * size, size)], f_ref.at[i], sems.at[i])
        for i in range(FIELDS)
    ]
    loads += [
        pltpu.make_async_copy(c_hbm.at[pl.ds(i * size, size)], c_ref.at[i], sems.at[FIELDS + i])
        for i in range(2)
    ]
    for load in loads:
        load.start()

    def plane(source, i, target):
        for r in range(ROWS):
            target[i, r + 1, inside, :] = source[i, pl.ds(r, LANES, stride=ROWS), :].T

    for i in range(FIELDS):
        loads[i].wait()
        plane(f_ref, i, t_ref)
        at = slice(i * LANES, (i + 1) * LANES)
        row_lo_ref[:, at] = t_ref[i, 1, inside, :].astype(BF16)
        row_hi_ref[:, at] = t_ref[i, ROWS, inside, :].astype(BF16)
        col_lo_ref[:, at] = t_ref[i, 1 : ROWS + 1, EDGE].astype(BF16)
        col_hi_ref[:, at] = t_ref[i, 1 : ROWS + 1, EDGE + COLS - 1].astype(BF16)
    at = slice(FEAT, FEAT + LANES)
    for i in range(2):
        loads[FIELDS + i].wait()
        plane(c_ref, i, cc_ref)
    row_lo_ref[:, at] = cc_ref[0, 1, inside, :].astype(BF16)
    row_hi_ref[:, at] = cc_ref[0, ROWS, inside, :].astype(BF16)
    col_lo_ref[:, at] = cc_ref[1, 1 : ROWS + 1, EDGE].astype(BF16)
    col_hi_ref[:, at] = cc_ref[1, 1 : ROWS + 1, EDGE + COLS - 1].astype(BF16)


def turn(fields, courant):
    flat_f = in_hbm(fields.reshape(FIELDS * LANES * ROWS, COLS))
    flat_c = in_hbm(courant.reshape(2 * LANES * ROWS, COLS))
    return pl.pallas_call(
        turn_kernel,
        in_specs=[HBM] * 2,
        out_specs=[VMEM] * 6,
        out_shape=[
            vmem_out((FIELDS, *MARGIN), F32),
            vmem_out((2, *MARGIN), F32),
            jax.ShapeDtypeStruct((COLS, FEAT + LANES), BF16),
            jax.ShapeDtypeStruct((COLS, FEAT + LANES), BF16),
            jax.ShapeDtypeStruct((ROWS, FEAT + LANES), BF16),
            jax.ShapeDtypeStruct((ROWS, FEAT + LANES), BF16),
        ],
        scratch_shapes=[
            pltpu.VMEM((FIELDS, LANES * ROWS, COLS), F32),
            pltpu.VMEM((2, LANES * ROWS, COLS), F32),
            pltpu.SemaphoreType.DMA((FIELDS + 2,)),
        ],
        compiler_params=params(14),
        cost_estimate=cost(4_000_000_000, 12 << 20),
        name="turn",
    )(flat_f, flat_c)


def plan_kernel(sun_ref, route_ref, mask_ref, place_ref, tags_ref):
    slots = sun_ref[...]
    low = (iota((COLS, CELLS), 0) == (slots & (COLS - 1))).astype(F32).astype(BF16)
    high = (iota((LANES, CELLS), 0) == (slots >> 7)).astype(F32).astype(BF16)
    lit = dot_nt(low, high)
    for r in range(ROWS):
        mask_ref[r] = jnp.broadcast_to(lit[:, r : r + 1], (COLS, LANES))

    target = route_ref[0, 0]
    arrival = route_ref[1, 0] + 1
    before = (iota((LANES, LANES), 0) < iota((LANES, LANES), 1)).astype(F32).astype(BF16)
    ones = jnp.ones((LANES, LANES), BF16)
    carry = jnp.zeros((LANES, LANES), F32)
    ranks = []
    for b in range(SEGS // LANES):
        goes = (iota((LANES, LANES), 0) == target[:, b * LANES : (b + 1) * LANES]).astype(F32)
        goes16 = goes.astype(BF16)
        ranks.append(jnp.sum(goes * (dot(goes16, before) + carry), axis=0, keepdims=True))
        carry = carry + dot(goes16, ones)
    rank = jnp.concatenate(ranks, axis=1).astype(jnp.int32)
    row = target * 16 + rank
    index = iota((LANES, SEGS), 0)
    coarse = (arrival >> 5).astype(F32)
    fine = (arrival & 31).astype(F32)
    tag_rows = [
        jnp.where(index == 2 * q, coarse, jnp.where(index == 2 * q + 1, fine, 0.0)).astype(BF16)
        for q in range(2)
    ]
    for b in range(SEGS // LANES):
        tags = jnp.zeros((LANES, LANES), F32)
        for q in range(2):
            want = 2 * (iota((LANES, SEGS), 0) + b * LANES) + q
            chosen = (row == want).astype(F32).astype(BF16)
            place_ref[q, b * LANES : (b + 1) * LANES, :] = chosen
            tags = tags + dot_nt(chosen, tag_rows[q])
        tags_ref[b * LANES : (b + 1) * LANES, :] = tags.astype(BF16)


def plan(sun_columns, segment_route):
    return pl.pallas_call(
        plan_kernel,
        in_specs=[VMEM] * 2,
        out_specs=[VMEM] * 3,
        out_shape=[
            vmem_out((ROWS, COLS, LANES), F32),
            vmem_out((2, SEGS, SEGS), BF16),
            vmem_out((SEGS, LANES), BF16),
        ],
        compiler_params=params(10),
        cost_estimate=cost(3_000_000_000, 1 << 20),
        name="plan",
    )(sun_columns.reshape(1, CELLS), segment_route)


def weights_of(lo0, mid0, hi0, left1, mid1, right1):
    f_lo = 0.5 * (lo0 + mid0)
    f_hi = 0.5 * (mid0 + hi0)
    g_lo = 0.5 * (left1 + mid1)
    g_hi = 0.5 * (mid1 + right1)
    keep = (
        1.0
        - jnp.maximum(f_hi, 0.0)
        + jnp.minimum(f_lo, 0.0)
        - jnp.maximum(g_hi, 0.0)
        + jnp.minimum(g_lo, 0.0)
    )
    return (
        keep,
        jnp.maximum(f_lo, 0.0),
        -jnp.minimum(f_hi, 0.0),
        jnp.maximum(g_lo, 0.0),
        -jnp.minimum(g_hi, 0.0),
    )


def combine(k, mid, lo, hi, left, right):
    return k[0] * mid + k[1] * lo + k[2] * hi + k[3] * left + k[4] * right


def net(x, h1_ref, h2_ref, w1_ref, b1_ref, w2_ref, b2_ref, w3_ref, emit):
    hidden = w2_ref.shape[0]
    wide = 256
    for n in range(0, hidden, wide):
        u = dot(x, w1_ref[:, n : n + wide]) + b1_ref[:, n : n + wide]
        h1_ref[:, n : n + wide] = silu(u).astype(BF16)
    h1 = h1_ref[...]
    for n in range(0, hidden, wide):
        u = dot(h1, w2_ref[:, n : n + wide]) + b2_ref[:, n : n + wide]
        h2_ref[:, n : n + wide] = silu(u).astype(BF16)
    h2 = h2_ref[...]
    for n in range(0, FEAT, wide):
        emit(n, dot(h2, w3_ref[:, n : n + wide]))


def sides(first, count):
    return (
        slice(first, first + count), slice(first - 1, first + count - 1), slice(first + 1, first + count + 1)
    )


def fill_halo(v_ref, row_lo_ref, row_hi_ref, col_lo_ref, col_hi_ref):
    inside = slice(EDGE, EDGE + COLS)
    for f in range(FIELDS):
        at = slice(f * LANES, (f + 1) * LANES)
        v_ref[f, 0, inside, :] = row_lo_ref[:, at].astype(F32)
        v_ref[f, ROWS + 1, inside, :] = row_hi_ref[:, at].astype(F32)
        low = col_lo_ref[:, at].astype(F32)
        high = col_hi_ref[:, at].astype(F32)
        for r in range(ROWS):
            v_ref[f, r + 1, EDGE - 1 : EDGE, :] = low[r : r + 1, :]
            v_ref[f, r + 1, EDGE + COLS : EDGE + COLS + 1, :] = high[r : r + 1, :]


def fill_speed_halo(c_ref, row_lo_ref, row_hi_ref, col_lo_ref, col_hi_ref):
    inside = slice(EDGE, EDGE + COLS)
    at = slice(FEAT, FEAT + LANES)
    low = col_lo_ref[:, at].astype(F32)
    high = col_hi_ref[:, at].astype(F32)
    for r in range(ROWS):
        c_ref[1, r + 1, EDGE - 1 : EDGE, :] = low[r : r + 1, :]
        c_ref[1, r + 1, EDGE + COLS : EDGE + COLS + 1, :] = high[r : r + 1, :]
    for spot, held, halo_ref, flag in (
        (0, 1, row_lo_ref, lax.axis_index("gx") > 0),
        (ROWS + 1, ROWS, row_hi_ref, lax.axis_index("gx") < lax.axis_size("gx") - 1),
    ):
        halo = halo_ref[:, at].astype(F32)
        c_ref[0, spot, inside, :] = jnp.where(flag, halo, -c_ref[0, held, inside, :])


def advect_into(v_ref, c_ref, r, pick, x_ref, adv_ref, here):
    def read(ref, f, row, which):
        parts = [ref[f, row, at, :] for at in pick[which]]
        return parts[0] if len(parts) == 1 else jnp.concatenate(parts, axis=0)

    k = weights_of(
        read(c_ref, 0, r - 1, 0), read(c_ref, 0, r, 0), read(c_ref, 0, r + 1, 0),
        read(c_ref, 1, r, 1), read(c_ref, 1, r, 0), read(c_ref, 1, r, 2),
    )
    for f in range(FIELDS):
        at = slice(f * LANES, (f + 1) * LANES)
        moved = combine(
            k, read(v_ref, f, r, 0), read(v_ref, f, r - 1, 0), read(v_ref, f, r + 1, 0),
            read(v_ref, f, r, 1), read(v_ref, f, r, 2),
        )
        adv_ref[here, at] = moved
        x_ref[here, at] = moved.astype(BF16)


def rim_kernel(
    mask_ref, row_lo_ref, row_hi_ref, col_lo_ref, col_hi_ref,
    w1_ref, b1_ref, w2_ref, b2_ref, w3_ref, _v, _c,
    v_ref, c_ref, out_ref, send_ref, x_ref, adv_ref, h1_ref, h2_ref,
):
    halo = (row_lo_ref, row_hi_ref, col_lo_ref, col_hi_ref)
    fill_halo(v_ref, *halo)
    fill_speed_halo(c_ref, *halo)
    whole = [[at] for at in sides(EDGE, COLS)]
    edge = [list(pair) for pair in zip(sides(EDGE, EDGE), sides(COLS, EDGE))]
    places = []
    for r, spot in ((1, 0), (ROWS, COLS)):
        advect_into(v_ref, c_ref, r, whole, x_ref, adv_ref, slice(spot, spot + COLS))
        places.append((r, slice(EDGE, EDGE + COLS), slice(spot, spot + COLS)))

    def edge_row(i, carry):
        spot = pl.multiple_of(2 * COLS + i * 2 * EDGE, 2 * EDGE)
        advect_into(v_ref, c_ref, i + 2, edge, x_ref, adv_ref, pl.ds(spot, 2 * EDGE))
        return carry

    lax.fori_loop(0, ROWS - 2, edge_row, 0)
    for r in range(2, ROWS):
        spot = 2 * COLS + (r - 2) * 2 * EDGE
        places.append((r, slice(EDGE, 2 * EDGE), slice(spot, spot + EDGE)))
        places.append((r, slice(COLS, COLS + EDGE), slice(spot + EDGE, spot + 2 * EDGE)))

    def emit(n, heat):
        for m in range(0, heat.shape[1], LANES):
            at = slice(n + m, n + m + LANES)
            for r, columns, here in places:
                lit = mask_ref[r - 1, columns.start - EDGE : columns.stop - EDGE, :]
                out_ref[(n + m) // LANES, r, columns, :] = (
                    adv_ref[here, at] + lit * heat[here, m : m + LANES]
                )

    net(x_ref[...], h1_ref, h2_ref, w1_ref, b1_ref, w2_ref, b2_ref, w3_ref, emit)
    for f in range(FIELDS):
        send_ref[:, f * LANES : (f + 1) * LANES] = out_ref[f, ROWS, EDGE : EDGE + COLS, :].astype(BF16)


def held_weights(weights):
    return tuple(in_vmem(w) if w.dtype == BF16 else w for w in weights)


def net_scratch(many, hidden):
    return [
        pltpu.VMEM((many, FEAT), BF16),
        pltpu.VMEM((many, FEAT), F32),
        pltpu.VMEM((many, hidden), BF16),
        pltpu.VMEM((many, hidden), BF16),
    ]


def rim(state, speeds, mask, halo, weights):
    near = (in_vmem(mask), *halo, *held_weights(weights))
    return pl.pallas_call(
        rim_kernel,
        in_specs=[VMEM] * (len(near) + 2),
        out_specs=[VMEM] * 4,
        out_shape=[
            vmem_out((FIELDS, *MARGIN), F32),
            vmem_out((2, *MARGIN), F32),
            vmem_out((FIELDS, *MARGIN), F32),
            jax.ShapeDtypeStruct((COLS, FEAT), BF16),
        ],
        input_output_aliases={len(near): 0, len(near) + 1: 1},
        scratch_shapes=net_scratch(RIM, weights[2].shape[0]),
        compiler_params=params(10),
        cost_estimate=cost(3_000_000_000, 4 << 20),
        name="rim",
    )(*near, in_vmem(state), in_vmem(speeds))


def piece_kernel(
    number, v_ref, c_ref, mask_ref, w1_ref, b1_ref, w2_ref, b2_ref, w3_ref, _, out_ref, *rest
):
    send, (x_ref, adv_ref, h1_ref, h2_ref) = rest[:-4], rest[-4:]
    first, count = PIECES[number]
    pick = [[at] for at in sides(2 * EDGE, INNER)]
    for j in range(count):
        here = slice(j * INNER, (j + 1) * INNER)
        advect_into(v_ref, c_ref, first + j + 1, pick, x_ref, adv_ref, here)

    def emit(n, heat):
        for j in range(count):
            here = slice(j * INNER, (j + 1) * INNER)
            lit = mask_ref[first + j, EDGE : EDGE + INNER, :]
            for m in range(0, heat.shape[1], LANES):
                out_ref[(n + m) // LANES, first + j + 1, 2 * EDGE : 2 * EDGE + INNER, :] = (
                    adv_ref[here, n + m : n + m + LANES] + lit * heat[here, m : m + LANES]
                )

    net(x_ref[...], h1_ref, h2_ref, w1_ref, b1_ref, w2_ref, b2_ref, w3_ref, emit)
    for f in range(FIELDS):
        at = slice(f * LANES, (f + 1) * LANES)
        if number == 0:
            send[0][:, at] = out_ref[f, 1, EDGE : EDGE + COLS, :].astype(BF16)
        if number == 1:
            send[0][:, at] = out_ref[f, 1 : ROWS + 1, EDGE + COLS - 1].astype(BF16)
        if number == 2:
            send[0][:, at] = out_ref[f, 1 : ROWS + 1, EDGE].astype(BF16)


def piece(number, state, speeds, mask, weights, target):
    near = (in_vmem(state), in_vmem(speeds), in_vmem(mask), *held_weights(weights), in_vmem(target))
    outs = [vmem_out((FIELDS, *MARGIN), F32)]
    if number < 3:
        outs += [jax.ShapeDtypeStruct((COLS if number == 0 else ROWS, FEAT), BF16)]
    return pl.pallas_call(
        lambda *refs: piece_kernel(number, *refs),
        in_specs=[VMEM] * len(near),
        out_specs=[VMEM] * len(outs),
        out_shape=outs,
        input_output_aliases={len(near) - 1: 0},
        scratch_shapes=net_scratch(PIECES[number][1] * INNER, weights[2].shape[0]),
        compiler_params=params(10),
        cost_estimate=cost(2_000_000_000, 1 << 20),
        name=f"piece_{number}",
    )(*near)


def final_kernel(
    c_ref, mask_ref, row_lo_ref, row_hi_ref, col_lo_ref, col_hi_ref,
    w1_ref, b1_ref, w2_ref, b2_ref, w3_ref, place_ref, tags_ref, _,
    v_ref, out_hbm, pack_hbm, out_ref, pack_ref, x_ref, adv_ref, h1_ref, h2_ref, out_sems, pack_sems,
):
    fill_halo(v_ref, row_lo_ref, row_hi_ref, col_lo_ref, col_hi_ref)
    pick = [[at] for at in sides(EDGE, COLS)]

    def store(g):
        rows = pl.ds(g * GROUP, GROUP)
        return pltpu.make_async_copy(out_ref.at[:, rows], out_hbm.at[:, rows], out_sems.at[g])

    def body(g, carry):
        for j in range(GROUP):
            here = slice(j * COLS, (j + 1) * COLS)
            advect_into(v_ref, c_ref, g * GROUP + j + 1, pick, x_ref, adv_ref, here)

        def emit(n, heat):
            for j in range(GROUP):
                r = g * GROUP + j
                here = slice(j * COLS, (j + 1) * COLS)
                for m in range(0, heat.shape[1], LANES):
                    out_ref[(n + m) // LANES, r] = (
                        adv_ref[here, n + m : n + m + LANES] + mask_ref[r] * heat[here, m : m + LANES]
                    )

        net(x_ref[...], h1_ref, h2_ref, w1_ref, b1_ref, w2_ref, b2_ref, w3_ref, emit)
        store(g).start()
        return carry

    lax.fori_loop(0, ROWS // GROUP, body, 0)
    stores = [store(g) for g in range(ROWS // GROUP)]
    flat = out_ref.reshape(FIELDS * CELLS, LANES)
    half = FEAT // 2
    columns = [
        jnp.concatenate(
            [flat[pl.ds(f * CELLS + c, SEGS, stride=2), :] for f in (2, 3)], axis=1
        ).astype(BF16)
        for c in range(2)
    ]
    pack_ref[:, 2 * FEAT :] = tags_ref[...]
    for i, b in enumerate(range(0, SEGS, 256)):
        for q in range(2):
            for c in range(2):
                pack_ref[b : b + 256, q * FEAT + c * half : q * FEAT + (c + 1) * half] = dot(
                    place_ref[q, b : b + 256, :], columns[c]
                ).astype(BF16)
        at = pl.ds(b, 256)
        stores.append(pltpu.make_async_copy(pack_ref.at[at], pack_hbm.at[at], pack_sems.at[i]))
        stores[-1].start()
    for copy in stores:
        copy.wait()


def final(state, speeds, mask, halo, weights, place, tags):
    near = (
        in_vmem(speeds), in_vmem(mask), *halo, *held_weights(weights), in_vmem(place), in_vmem(tags),
        in_vmem(state),
    )
    _, out, packed = pl.pallas_call(
        final_kernel,
        in_specs=[VMEM] * len(near),
        out_specs=[VMEM, HBM, HBM],
        out_shape=[
            vmem_out((FIELDS, *MARGIN), F32),
            hbm_out((FIELDS, ROWS, COLS, LANES), F32),
            hbm_out((SEGS, 2 * FEAT + LANES), BF16),
        ],
        input_output_aliases={len(near) - 1: 0},
        scratch_shapes=[
            pltpu.VMEM((FIELDS, ROWS, COLS, LANES), F32),
            pltpu.VMEM((SEGS, 2 * FEAT + LANES), BF16),
            *net_scratch(GROUP * COLS, weights[2].shape[0]),
            pltpu.SemaphoreType.DMA((ROWS // GROUP,)),
            pltpu.SemaphoreType.DMA((SEGS // 256,)),
        ],
        compiler_params=params(18),
        cost_estimate=cost(12_000_000_000, 4 << 20),
        name="final",
    )(*near)
    return out, packed


def unturn_kernel(t_hbm, out_ref, t_ref, stage_ref, in_sems, sems):
    size = LANES * ROWS
    loads = [pltpu.make_async_copy(t_hbm.at[f], t_ref.at[f], in_sems.at[f]) for f in range(FIELDS)]
    stores = [
        pltpu.make_async_copy(stage_ref.at[f], out_ref.at[pl.ds(f * size, size)], sems.at[f])
        for f in range(FIELDS)
    ]
    for load in loads:
        load.start()
    for f in range(FIELDS):
        loads[f].wait()
        for r in range(ROWS):
            stage_ref[f, pl.ds(r, LANES, stride=ROWS), :] = t_ref[f, r].T
        stores[f].start()
    for store in stores:
        store.wait()


def unturn(state):
    return pl.pallas_call(
        unturn_kernel,
        in_specs=[HBM],
        out_specs=HBM,
        out_shape=hbm_out((FIELDS * LANES * ROWS, COLS), F32),
        scratch_shapes=[
            pltpu.VMEM((FIELDS, ROWS, COLS, LANES), F32),
            pltpu.VMEM((FIELDS, LANES * ROWS, COLS), F32),
            pltpu.SemaphoreType.DMA((FIELDS,)),
            pltpu.SemaphoreType.DMA((FIELDS,)),
        ],
        compiler_params=params(12),
        cost_estimate=cost(1_000_000_000, 8 << 20),
        name="unturn",
    )(in_hbm(state))


def chem_kernel(
    arr_ref, regrid_ref, w1_ref, b1_ref, w2_hbm, out_hbm,
    want_ref, mix_ref, x_ref, h_ref, out_ref, w2_ref, sems, w_sem,
):
    w2_load = pltpu.make_async_copy(w2_hbm, w2_ref, w_sem.at[0])
    w2_load.start()
    from_cell = iota((LANES, LANES), 0)
    to_lane = iota((LANES, LANES), 1)
    source_cell = jnp.where(to_lane < 64, 2 * to_lane, 2 * (to_lane - 64) + 1)
    split = (from_cell == source_cell).astype(F32).astype(BF16)
    mix_ref[...] = dot(regrid_ref[...], split).astype(BF16)
    lane = iota((8, LANES), 1)
    which = iota((8, LANES), 0)
    pick = jnp.where(lane == 2 * which, 32.0, jnp.where(lane == 2 * which + 1, 1.0, 0.0))
    pick = jnp.where(which < 2, pick, 0.0).astype(BF16)
    want_ref[...] = dot_nt(pick, arr_ref[:, 2 * FEAT :]).astype(jnp.int32) - 1
    span = 256
    half = FEAT // 2
    stores = []
    for i in range(SEGS // span):
        start = i * span
        placed = []
        for q in range(2):
            chosen = (iota((span, SEGS), 0) + start == want_ref[q : q + 1, :]).astype(F32).astype(BF16)
            placed.append(dot(chosen, arr_ref[:, q * FEAT : (q + 1) * FEAT]))
        placed = (placed[0] + placed[1]).astype(BF16)
        for b in range(span // 64):
            cells = jnp.concatenate(
                [placed[b * 64 : (b + 1) * 64, :half], placed[b * 64 : (b + 1) * 64, half:]], axis=0
            )
            spot = 2 * start + b * LANES
            x_ref[i % 2, b * LANES : (b + 1) * LANES, :] = dot(
                mix_ref[spot : spot + LANES, :], cells
            ).astype(BF16)
        x = x_ref[i % 2]
        for n in range(0, w1_ref.shape[1], 256):
            u = dot(x, w1_ref[:, n : n + 256]) + b1_ref[:, n : n + 256]
            h_ref[i % 2, :, n : n + 256] = silu(u).astype(BF16)
        if i == 0:
            w2_load.wait()
        rows = slice(2 * start, 2 * (start + span))
        out_ref[rows, :] = dot(h_ref[i % 2], w2_ref[...]).astype(BF16)
        at = pl.ds(2 * start, 2 * span)
        stores.append(pltpu.make_async_copy(out_ref.at[at], out_hbm.at[at], sems.at[i]))
        stores[-1].start()
    for store in stores:
        store.wait()


def chem(arrived, regrid_weights, w1, b1, w2):
    return pl.pallas_call(
        chem_kernel,
        in_specs=[VMEM] * 4 + [HBM],
        out_specs=HBM,
        out_shape=hbm_out((CELLS, w2.shape[1]), BF16),
        scratch_shapes=[
            pltpu.VMEM((8, SEGS), jnp.int32),
            pltpu.VMEM((CELLS, LANES), BF16),
            pltpu.VMEM((2, 512, FEAT // 2), BF16),
            pltpu.VMEM((2, 512, w1.shape[1]), BF16),
            pltpu.VMEM((CELLS, w2.shape[1]), BF16),
            pltpu.VMEM(w2.shape, BF16),
            pltpu.SemaphoreType.DMA((SEGS // 256,)),
            pltpu.SemaphoreType.DMA((1,)),
        ],
        compiler_params=params(14),
        cost_estimate=cost(4_400_000_000, 4 << 20),
        name="chem",
    )(
        in_vmem(arrived),
        in_vmem(regrid_weights.reshape(CELLS, LANES)),
        in_vmem(w1),
        b1,
        in_hbm(w2),
    )


def rows_up(x):
    return lax.ppermute(x, "gx", [(i, i + 1) for i in range(lax.axis_size("gx") - 1)])


def rows_down(x):
    return lax.ppermute(x, "gx", [(i + 1, i) for i in range(lax.axis_size("gx") - 1)])


def columns_right(x):
    count = lax.axis_size("gy")
    return lax.ppermute(x, "gy", [(i, (i + 1) % count) for i in range(count)])


def columns_left(x):
    count = lax.axis_size("gy")
    return lax.ppermute(x, "gy", [((i + 1) % count, i) for i in range(count)])


def local(
    fields, courant, sun_columns, rad_w1, rad_b1, rad_w2, rad_b2, rad_w3,
    segment_route, regrid_weights, chem_w1, chem_b1, chem_w2,
):
    weights = (rad_w1, rad_b1.reshape(1, -1), rad_w2, rad_b2.reshape(1, -1), rad_w3)

    state, speeds, row_lo, row_hi, col_lo, col_hi = turn(fields, courant)
    halo = (rows_up(row_hi), rows_down(row_lo), columns_right(col_hi), columns_left(col_lo))
    mask, place, tags = plan(sun_columns, segment_route)
    state, speeds, target, row_hi = rim(state, speeds, mask, halo, weights)
    row_hi = rows_up(row_hi)
    target, row_lo = piece(0, state, speeds, mask, weights, target)
    row_lo = rows_down(row_lo)
    target, col_hi = piece(1, state, speeds, mask, weights, target)
    col_hi = columns_right(col_hi)
    target, col_lo = piece(2, state, speeds, mask, weights, target)
    col_lo = columns_left(col_lo)
    (target,) = piece(3, state, speeds, mask, weights, target)
    halo = (row_hi, row_lo, col_hi, col_lo)
    state, packed = final(target, speeds, mask, halo, weights, place, tags)
    tiles = lax.axis_size("gx") * lax.axis_size("gy")
    packed = packed.reshape(tiles, SEGS // tiles, packed.shape[1])
    arrived = lax.all_to_all(packed, ("gx", "gy"), split_axis=0, concat_axis=0, tiled=True)
    fields_out = unturn(state).reshape(fields.shape)
    output = chem(
        arrived.reshape(SEGS, arrived.shape[2]), regrid_weights, chem_w1, chem_b1.reshape(1, -1), chem_w2
    )
    return fields_out, output.reshape(1, 1, CELLS, -1)


def solution(mesh):
    return jax.shard_map(
        local,
        mesh=mesh,
        in_specs=(
            P(None, None, "gx", "gy"),
            P(None, None, "gx", "gy"),
            P("gx", "gy", None),
            P(),
            P(),
            P(),
            P(),
            P(),
            P(None, "gx", "gy", None),
            P("gx", "gy", None, None, None),
            P(),
            P(),
            P(),
        ),
        out_specs=(P(None, None, "gx", "gy"), P("gx", "gy", None, None)),
        check_vma=False,
    )
```

```python
import jax
import jax.numpy as jnp
from jax import lax
from jax.experimental import pallas as pl
from jax.experimental.pallas import tpu as pltpu
from jax.sharding import PartitionSpec as P

F32 = jnp.float32
BF16 = jnp.bfloat16
LANES = 128
FIELDS = 4
ROWS = 16
COLS = 128
FEAT = FIELDS * LANES
CELLS = ROWS * COLS
SEGS = CELLS // 2
EDGE = 8
GROUP = 8
SPAN = 512
PIECES = ((1, 5), (6, 9))
INNER = COLS - 2 * EDGE
RIM = 2 * COLS + (ROWS - 2) * 2 * EDGE
MARGIN = (ROWS + 2, COLS + 2 * EDGE, LANES)
MIB = 1024 * 1024

VMEM = pl.BlockSpec(memory_space=pltpu.VMEM)
SMEM = pl.BlockSpec(memory_space=pltpu.SMEM)
ANY = pl.BlockSpec(memory_space=pl.ANY)


HBM = pl.BlockSpec(memory_space=pltpu.HBM)


def vmem_out(shape, dtype):
    return pltpu.VMEM(shape, dtype)


def hbm_out(shape, dtype):
    return pltpu.HBM(shape, dtype)


def in_vmem(x):
    return pltpu.with_memory_space_constraint(x, pltpu.VMEM)


def in_hbm(x):
    return pltpu.with_memory_space_constraint(x, pltpu.HBM)


def params(mib):
    return pltpu.CompilerParams(vmem_limit_bytes=mib * MIB)


def cost(flops, bytes_accessed=0):
    return pl.CostEstimate(flops=flops, bytes_accessed=bytes_accessed, transcendentals=0)


def dot(a, b):
    return jnp.dot(a, b, preferred_element_type=F32)


def dot_nt(a, b):
    return lax.dot_general(a, b, (((1,), (1,)), ((), ())), preferred_element_type=F32)


def silu(u):
    half = 0.5 * u
    return half + half * jnp.tanh(half)


def iota(shape, dim):
    return lax.broadcasted_iota(jnp.int32, shape, dim)


def turn_kernel(f_hbm, c_hbm, t_ref, cc_ref, row_lo_ref, row_hi_ref, col_lo_ref, col_hi_ref, f_ref, c_ref, sems):
    size = LANES * ROWS
    inside = slice(EDGE, EDGE + COLS)
    loads = [
        pltpu.make_async_copy(f_hbm.at[pl.ds(i * size, size)], f_ref.at[i], sems.at[i])
        for i in range(FIELDS)
    ]
    loads += [
        pltpu.make_async_copy(c_hbm.at[pl.ds(i * size, size)], c_ref.at[i], sems.at[FIELDS + i])
        for i in range(2)
    ]
    for load in loads:
        load.start()

    def plane(source, i, target):
        for r in range(ROWS):
            target[i, r + 1, inside, :] = source[i, pl.ds(r, LANES, stride=ROWS), :].T

    for i in range(FIELDS):
        loads[i].wait()
        plane(f_ref, i, t_ref)
        at = slice(i * LANES, (i + 1) * LANES)
        row_lo_ref[:, at] = t_ref[i, 1, inside, :].astype(BF16)
        row_hi_ref[:, at] = t_ref[i, ROWS, inside, :].astype(BF16)
        col_lo_ref[:, at] = t_ref[i, 1 : ROWS + 1, EDGE].astype(BF16)
        col_hi_ref[:, at] = t_ref[i, 1 : ROWS + 1, EDGE + COLS - 1].astype(BF16)
    at = slice(FEAT, FEAT + LANES)
    for i in range(2):
        loads[FIELDS + i].wait()
        plane(c_ref, i, cc_ref)
    row_lo_ref[:, at] = cc_ref[0, 1, inside, :].astype(BF16)
    row_hi_ref[:, at] = cc_ref[0, ROWS, inside, :].astype(BF16)
    col_lo_ref[:, at] = cc_ref[1, 1 : ROWS + 1, EDGE].astype(BF16)
    col_hi_ref[:, at] = cc_ref[1, 1 : ROWS + 1, EDGE + COLS - 1].astype(BF16)


def turn(fields, courant):
    flat_f = in_hbm(fields.reshape(FIELDS * LANES * ROWS, COLS))
    flat_c = in_hbm(courant.reshape(2 * LANES * ROWS, COLS))
    return pl.pallas_call(
        turn_kernel,
        in_specs=[HBM] * 2,
        out_specs=[VMEM] * 6,
        out_shape=[
            vmem_out((FIELDS, *MARGIN), F32),
            vmem_out((2, *MARGIN), F32),
            jax.ShapeDtypeStruct((COLS, FEAT + LANES), BF16),
            jax.ShapeDtypeStruct((COLS, FEAT + LANES), BF16),
            jax.ShapeDtypeStruct((ROWS, FEAT + LANES), BF16),
            jax.ShapeDtypeStruct((ROWS, FEAT + LANES), BF16),
        ],
        scratch_shapes=[
            pltpu.VMEM((FIELDS, LANES * ROWS, COLS), F32),
            pltpu.VMEM((2, LANES * ROWS, COLS), F32),
            pltpu.SemaphoreType.DMA((FIELDS + 2,)),
        ],
        compiler_params=params(14),
        cost_estimate=cost(4_000_000_000, 12 << 20),
        name="turn",
    )(flat_f, flat_c)


def plan_kernel(sun_ref, route_ref, mask_ref, place_ref, tags_ref):
    slots = sun_ref[...]
    low = (iota((COLS, CELLS), 0) == (slots & (COLS - 1))).astype(F32).astype(BF16)
    high = (iota((LANES, CELLS), 0) == (slots >> 7)).astype(F32).astype(BF16)
    lit = dot_nt(low, high)
    for r in range(ROWS):
        mask_ref[r] = jnp.broadcast_to(lit[:, r : r + 1], (COLS, LANES))

    target = route_ref[0, 0]
    arrival = route_ref[1, 0] + 1
    before = (iota((LANES, LANES), 0) < iota((LANES, LANES), 1)).astype(F32).astype(BF16)
    ones = jnp.ones((LANES, LANES), BF16)
    carry = jnp.zeros((LANES, LANES), F32)
    ranks = []
    for b in range(SEGS // LANES):
        goes = (iota((LANES, LANES), 0) == target[:, b * LANES : (b + 1) * LANES]).astype(F32)
        goes16 = goes.astype(BF16)
        ranks.append(jnp.sum(goes * (dot(goes16, before) + carry), axis=0, keepdims=True))
        carry = carry + dot(goes16, ones)
    rank = jnp.concatenate(ranks, axis=1).astype(jnp.int32)
    row = target * 16 + rank
    index = iota((LANES, SEGS), 0)
    coarse = (arrival >> 5).astype(F32)
    fine = (arrival & 31).astype(F32)
    tag_rows = [
        jnp.where(index == 2 * q, coarse, jnp.where(index == 2 * q + 1, fine, 0.0)).astype(BF16)
        for q in range(2)
    ]
    for b in range(SEGS // LANES):
        tags = jnp.zeros((LANES, LANES), F32)
        for q in range(2):
            want = 2 * (iota((LANES, SEGS), 0) + b * LANES) + q
            chosen = (row == want).astype(F32).astype(BF16)
            place_ref[q, b * LANES : (b + 1) * LANES, :] = chosen
            tags = tags + dot_nt(chosen, tag_rows[q])
        tags_ref[b * LANES : (b + 1) * LANES, :] = tags.astype(BF16)


def plan(sun_columns, segment_route):
    return pl.pallas_call(
        plan_kernel,
        in_specs=[VMEM] * 2,
        out_specs=[VMEM] * 3,
        out_shape=[
            vmem_out((ROWS, COLS, LANES), F32),
            vmem_out((2, SEGS, SEGS), BF16),
            vmem_out((SEGS, LANES), BF16),
        ],
        compiler_params=params(10),
        cost_estimate=cost(3_000_000_000, 1 << 20),
        name="plan",
    )(sun_columns.reshape(1, CELLS), segment_route)


def weights_of(lo0, mid0, hi0, left1, mid1, right1):
    f_lo = 0.5 * (lo0 + mid0)
    f_hi = 0.5 * (mid0 + hi0)
    g_lo = 0.5 * (left1 + mid1)
    g_hi = 0.5 * (mid1 + right1)
    keep = (
        1.0
        - jnp.maximum(f_hi, 0.0)
        + jnp.minimum(f_lo, 0.0)
        - jnp.maximum(g_hi, 0.0)
        + jnp.minimum(g_lo, 0.0)
    )
    return (
        keep,
        jnp.maximum(f_lo, 0.0),
        -jnp.minimum(f_hi, 0.0),
        jnp.maximum(g_lo, 0.0),
        -jnp.minimum(g_hi, 0.0),
    )


def combine(k, mid, lo, hi, left, right):
    return k[0] * mid + k[1] * lo + k[2] * hi + k[3] * left + k[4] * right


def net(x, h1_ref, h2_ref, w1_ref, b1_ref, w2_ref, b2_ref, w3_ref, emit):
    hidden = w2_ref.shape[0]
    wide = 256
    for n in range(0, hidden, wide):
        u = dot(x, w1_ref[:, n : n + wide]) + b1_ref[:, n : n + wide]
        h1_ref[:, n : n + wide] = silu(u).astype(BF16)
    h1 = h1_ref[...]
    for n in range(0, hidden, wide):
        u = dot(h1, w2_ref[:, n : n + wide]) + b2_ref[:, n : n + wide]
        h2_ref[:, n : n + wide] = silu(u).astype(BF16)
    h2 = h2_ref[...]
    for n in range(0, FEAT, wide):
        emit(n, dot(h2, w3_ref[:, n : n + wide]))


def sides(first, count):
    return (
        slice(first, first + count), slice(first - 1, first + count - 1), slice(first + 1, first + count + 1)
    )


def fill_halo(v_ref, row_lo_ref, row_hi_ref, col_lo_ref, col_hi_ref):
    inside = slice(EDGE, EDGE + COLS)
    for f in range(FIELDS):
        at = slice(f * LANES, (f + 1) * LANES)
        v_ref[f, 0, inside, :] = row_lo_ref[:, at].astype(F32)
        v_ref[f, ROWS + 1, inside, :] = row_hi_ref[:, at].astype(F32)
        low = col_lo_ref[:, at].astype(F32)
        high = col_hi_ref[:, at].astype(F32)
        for r in range(ROWS):
            v_ref[f, r + 1, EDGE - 1 : EDGE, :] = low[r : r + 1, :]
            v_ref[f, r + 1, EDGE + COLS : EDGE + COLS + 1, :] = high[r : r + 1, :]


def fill_speed_halo(c_ref, row_lo_ref, row_hi_ref, col_lo_ref, col_hi_ref):
    inside = slice(EDGE, EDGE + COLS)
    at = slice(FEAT, FEAT + LANES)
    low = col_lo_ref[:, at].astype(F32)
    high = col_hi_ref[:, at].astype(F32)
    for r in range(ROWS):
        c_ref[1, r + 1, EDGE - 1 : EDGE, :] = low[r : r + 1, :]
        c_ref[1, r + 1, EDGE + COLS : EDGE + COLS + 1, :] = high[r : r + 1, :]
    for spot, held, halo_ref, flag in (
        (0, 1, row_lo_ref, lax.axis_index("gx") > 0),
        (ROWS + 1, ROWS, row_hi_ref, lax.axis_index("gx") < lax.axis_size("gx") - 1),
    ):
        halo = halo_ref[:, at].astype(F32)
        c_ref[0, spot, inside, :] = jnp.where(flag, halo, -c_ref[0, held, inside, :])


def advect_into(v_ref, c_ref, r, pick, x_ref, adv_ref, here):
    def read(ref, f, row, which):
        parts = [ref[f, row, at, :] for at in pick[which]]
        return parts[0] if len(parts) == 1 else jnp.concatenate(parts, axis=0)

    k = weights_of(
        read(c_ref, 0, r - 1, 0), read(c_ref, 0, r, 0), read(c_ref, 0, r + 1, 0),
        read(c_ref, 1, r, 1), read(c_ref, 1, r, 0), read(c_ref, 1, r, 2),
    )
    for f in range(FIELDS):
        at = slice(f * LANES, (f + 1) * LANES)
        moved = combine(
            k, read(v_ref, f, r, 0), read(v_ref, f, r - 1, 0), read(v_ref, f, r + 1, 0),
            read(v_ref, f, r, 1), read(v_ref, f, r, 2),
        )
        adv_ref[here, at] = moved
        x_ref[here, at] = moved.astype(BF16)


def rim_kernel(
    mask_ref, row_lo_ref, row_hi_ref, col_lo_ref, col_hi_ref,
    w1_ref, b1_ref, w2_ref, b2_ref, w3_ref, _v, _c, _out,
    v_ref, c_ref, out_ref, row_lo_out, row_hi_out, col_lo_out, col_hi_out,
    x_ref, adv_ref, h1_ref, h2_ref,
):
    halo = (row_lo_ref, row_hi_ref, col_lo_ref, col_hi_ref)
    fill_halo(v_ref, *halo)
    fill_speed_halo(c_ref, *halo)
    whole = [[at] for at in sides(EDGE, COLS)]
    edge = [list(pair) for pair in zip(sides(EDGE, EDGE), sides(COLS, EDGE))]
    places = []
    for r, spot in ((1, 0), (ROWS, COLS)):
        advect_into(v_ref, c_ref, r, whole, x_ref, adv_ref, slice(spot, spot + COLS))
        places.append((r, slice(EDGE, EDGE + COLS), slice(spot, spot + COLS)))

    def edge_row(i, carry):
        spot = pl.multiple_of(2 * COLS + i * 2 * EDGE, 2 * EDGE)
        advect_into(v_ref, c_ref, i + 2, edge, x_ref, adv_ref, pl.ds(spot, 2 * EDGE))
        return carry

    lax.fori_loop(0, ROWS - 2, edge_row, 0)
    for r in range(2, ROWS):
        spot = 2 * COLS + (r - 2) * 2 * EDGE
        places.append((r, slice(EDGE, 2 * EDGE), slice(spot, spot + EDGE)))
        places.append((r, slice(COLS, COLS + EDGE), slice(spot + EDGE, spot + 2 * EDGE)))

    def emit(n, heat):
        for m in range(0, heat.shape[1], LANES):
            at = slice(n + m, n + m + LANES)
            for r, columns, here in places:
                lit = mask_ref[r - 1, columns.start - EDGE : columns.stop - EDGE, :]
                out_ref[(n + m) // LANES, r, columns, :] = (
                    adv_ref[here, at] + lit * heat[here, m : m + LANES]
                )

    net(x_ref[...], h1_ref, h2_ref, w1_ref, b1_ref, w2_ref, b2_ref, w3_ref, emit)
    for f in range(FIELDS):
        at = slice(f * LANES, (f + 1) * LANES)
        row_lo_out[:, at] = out_ref[f, 1, EDGE : EDGE + COLS, :].astype(BF16)
        row_hi_out[:, at] = out_ref[f, ROWS, EDGE : EDGE + COLS, :].astype(BF16)
        col_lo_out[:, at] = out_ref[f, 1 : ROWS + 1, EDGE].astype(BF16)
        col_hi_out[:, at] = out_ref[f, 1 : ROWS + 1, EDGE + COLS - 1].astype(BF16)


def held_weights(weights):
    return tuple(in_vmem(w) if w.dtype == BF16 else w for w in weights)


def net_scratch(many, hidden):
    return [
        pltpu.VMEM((many, FEAT), BF16),
        pltpu.VMEM((many, FEAT), F32),
        pltpu.VMEM((many, hidden), BF16),
        pltpu.VMEM((many, hidden), BF16),
    ]


def rim(state, speeds, mask, halo, weights, target):
    near = (in_vmem(mask), *halo, *held_weights(weights))
    return pl.pallas_call(
        rim_kernel,
        in_specs=[VMEM] * (len(near) + 3),
        out_specs=[VMEM] * 7,
        out_shape=[
            vmem_out((FIELDS, *MARGIN), F32),
            vmem_out((2, *MARGIN), F32),
            vmem_out((FIELDS, *MARGIN), F32),
            *[jax.ShapeDtypeStruct((COLS, FEAT), BF16)] * 2,
            *[jax.ShapeDtypeStruct((ROWS, FEAT), BF16)] * 2,
        ],
        input_output_aliases={len(near) + i: i for i in range(3)},
        scratch_shapes=net_scratch(RIM, weights[2].shape[0]),
        compiler_params=params(10),
        cost_estimate=cost(3_000_000_000, 4 << 20),
        name="rim",
    )(*near, in_vmem(state), in_vmem(speeds), in_vmem(target))


def piece_kernel(
    number, v_ref, c_ref, mask_ref, w1_ref, b1_ref, w2_ref, b2_ref, w3_ref, *rest
):
    out_ref, x_ref, adv_ref, h1_ref, h2_ref = rest[-5:]
    first, count = PIECES[number]
    pick = [[at] for at in sides(2 * EDGE, INNER)]
    for j in range(count):
        here = slice(j * INNER, (j + 1) * INNER)
        advect_into(v_ref, c_ref, first + j + 1, pick, x_ref, adv_ref, here)

    def emit(n, heat):
        for j in range(count):
            here = slice(j * INNER, (j + 1) * INNER)
            lit = mask_ref[first + j, EDGE : EDGE + INNER, :]
            for m in range(0, heat.shape[1], LANES):
                out_ref[(n + m) // LANES, first + j + 1, 2 * EDGE : 2 * EDGE + INNER, :] = (
                    adv_ref[here, n + m : n + m + LANES] + lit * heat[here, m : m + LANES]
                )

    net(x_ref[...], h1_ref, h2_ref, w1_ref, b1_ref, w2_ref, b2_ref, w3_ref, emit)


def piece(number, state, speeds, mask, weights, target=None):
    near = (in_vmem(state), in_vmem(speeds), in_vmem(mask), *held_weights(weights))
    if target is not None:
        near += (in_vmem(target),)
    return pl.pallas_call(
        lambda *refs: piece_kernel(number, *refs),
        in_specs=[VMEM] * len(near),
        out_specs=VMEM,
        out_shape=vmem_out((FIELDS, *MARGIN), F32),
        input_output_aliases={} if target is None else {len(near) - 1: 0},
        scratch_shapes=net_scratch(PIECES[number][1] * INNER, weights[2].shape[0]),
        compiler_params=params(12),
        cost_estimate=cost(2_000_000_000 * (1 + 2 * number), 1 << 20),
        name=f"piece_{number}",
    )(*near)


def final_kernel(
    c_ref, mask_ref, row_lo_ref, row_hi_ref, col_lo_ref, col_hi_ref,
    w1_ref, b1_ref, w2_ref, b2_ref, w3_ref, place_ref, tags_ref, _,
    v_ref, out_hbm, pack_hbm, out_ref, pack_ref, x_ref, adv_ref, h1_ref, h2_ref, out_sems, pack_sems,
):
    fill_halo(v_ref, row_lo_ref, row_hi_ref, col_lo_ref, col_hi_ref)
    pick = [[at] for at in sides(EDGE, COLS)]

    def store(g):
        rows = pl.ds(g * GROUP, GROUP)
        return pltpu.make_async_copy(out_ref.at[:, rows], out_hbm.at[:, rows], out_sems.at[g])

    def body(g, carry):
        for j in range(GROUP):
            here = slice(j * COLS, (j + 1) * COLS)
            advect_into(v_ref, c_ref, g * GROUP + j + 1, pick, x_ref, adv_ref, here)

        def emit(n, heat):
            for j in range(GROUP):
                r = g * GROUP + j
                here = slice(j * COLS, (j + 1) * COLS)
                for m in range(0, heat.shape[1], LANES):
                    out_ref[(n + m) // LANES, r] = (
                        adv_ref[here, n + m : n + m + LANES] + mask_ref[r] * heat[here, m : m + LANES]
                    )

        net(x_ref[...], h1_ref, h2_ref, w1_ref, b1_ref, w2_ref, b2_ref, w3_ref, emit)
        store(g).start()
        return carry

    lax.fori_loop(0, ROWS // GROUP, body, 0)
    stores = [store(g) for g in range(ROWS // GROUP)]
    flat = out_ref.reshape(FIELDS * CELLS, LANES)
    half = FEAT // 2
    columns = [
        jnp.concatenate(
            [flat[pl.ds(f * CELLS + c, SEGS, stride=2), :] for f in (2, 3)], axis=1
        ).astype(BF16)
        for c in range(2)
    ]
    pack_ref[:, 2 * FEAT :] = tags_ref[...]
    for i, b in enumerate(range(0, SEGS, 256)):
        for q in range(2):
            for c in range(2):
                pack_ref[b : b + 256, q * FEAT + c * half : q * FEAT + (c + 1) * half] = dot(
                    place_ref[q, b : b + 256, :], columns[c]
                ).astype(BF16)
        at = pl.ds(b, 256)
        stores.append(pltpu.make_async_copy(pack_ref.at[at], pack_hbm.at[at], pack_sems.at[i]))
        stores[-1].start()
    for copy in stores:
        copy.wait()


def final(state, speeds, mask, halo, weights, place, tags):
    near = (
        in_vmem(speeds), in_vmem(mask), *halo, *held_weights(weights), in_vmem(place), in_vmem(tags),
        in_vmem(state),
    )
    _, out, packed = pl.pallas_call(
        final_kernel,
        in_specs=[VMEM] * len(near),
        out_specs=[VMEM, HBM, HBM],
        out_shape=[
            vmem_out((FIELDS, *MARGIN), F32),
            hbm_out((FIELDS, ROWS, COLS, LANES), F32),
            hbm_out((SEGS, 2 * FEAT + LANES), BF16),
        ],
        input_output_aliases={len(near) - 1: 0},
        scratch_shapes=[
            pltpu.VMEM((FIELDS, ROWS, COLS, LANES), F32),
            pltpu.VMEM((SEGS, 2 * FEAT + LANES), BF16),
            *net_scratch(GROUP * COLS, weights[2].shape[0]),
            pltpu.SemaphoreType.DMA((ROWS // GROUP,)),
            pltpu.SemaphoreType.DMA((SEGS // 256,)),
        ],
        compiler_params=params(24),
        cost_estimate=cost(12_000_000_000, 4 << 20),
        name="final",
    )(*near)
    return out, packed


def unturn_kernel(t_hbm, out_ref, t_ref, stage_ref, in_sems, sems):
    size = LANES * ROWS
    loads = [pltpu.make_async_copy(t_hbm.at[f], t_ref.at[f], in_sems.at[f]) for f in range(FIELDS)]
    stores = [
        pltpu.make_async_copy(stage_ref.at[f], out_ref.at[pl.ds(f * size, size)], sems.at[f])
        for f in range(FIELDS)
    ]
    for load in loads:
        load.start()
    for f in range(FIELDS):
        loads[f].wait()
        for r in range(ROWS):
            stage_ref[f, pl.ds(r, LANES, stride=ROWS), :] = t_ref[f, r].T
        stores[f].start()
    for store in stores:
        store.wait()


def unturn(state):
    return pl.pallas_call(
        unturn_kernel,
        in_specs=[HBM],
        out_specs=HBM,
        out_shape=hbm_out((FIELDS * LANES * ROWS, COLS), F32),
        scratch_shapes=[
            pltpu.VMEM((FIELDS, ROWS, COLS, LANES), F32),
            pltpu.VMEM((FIELDS, LANES * ROWS, COLS), F32),
            pltpu.SemaphoreType.DMA((FIELDS,)),
            pltpu.SemaphoreType.DMA((FIELDS,)),
        ],
        compiler_params=params(12),
        cost_estimate=cost(1_000_000_000, 8 << 20),
        name="unturn",
    )(in_hbm(state))


def chem_kernel(
    arr_ref, regrid_ref, w1_ref, b1_ref, w2_hbm, out_hbm,
    want_ref, mix_ref, x_ref, h_ref, out_ref, w2_ref, sems, w_sem,
):
    w2_load = pltpu.make_async_copy(w2_hbm, w2_ref, w_sem.at[0])
    w2_load.start()
    from_cell = iota((LANES, LANES), 0)
    to_lane = iota((LANES, LANES), 1)
    source_cell = jnp.where(to_lane < 64, 2 * to_lane, 2 * (to_lane - 64) + 1)
    split = (from_cell == source_cell).astype(F32).astype(BF16)
    mix_ref[...] = dot(regrid_ref[...], split).astype(BF16)
    lane = iota((8, LANES), 1)
    which = iota((8, LANES), 0)
    pick = jnp.where(lane == 2 * which, 32.0, jnp.where(lane == 2 * which + 1, 1.0, 0.0))
    pick = jnp.where(which < 2, pick, 0.0).astype(BF16)
    want_ref[...] = dot_nt(pick, arr_ref[:, 2 * FEAT :]).astype(jnp.int32) - 1
    span = SPAN
    half = FEAT // 2
    w2_load.wait()

    def store(i):
        at = pl.ds(pl.multiple_of(2 * span * i, 2 * span), 2 * span)
        return pltpu.make_async_copy(out_ref.at[at], out_hbm.at[at], sems.at[i])

    def body(i, carry):
        start = i * span
        placed = []
        for q in range(2):
            chosen = (iota((span, SEGS), 0) + start == want_ref[q : q + 1, :]).astype(F32).astype(BF16)
            placed.append(dot(chosen, arr_ref[:, q * FEAT : (q + 1) * FEAT]))
        placed = (placed[0] + placed[1]).astype(BF16)
        for b in range(span // 64):
            cells = jnp.concatenate(
                [placed[b * 64 : (b + 1) * 64, :half], placed[b * 64 : (b + 1) * 64, half:]], axis=0
            )
            spot = pl.multiple_of(2 * start + b * LANES, LANES)
            x_ref[b * LANES : (b + 1) * LANES, :] = dot(mix_ref[pl.ds(spot, LANES), :], cells).astype(BF16)
        x = x_ref[...]
        for n in range(0, w1_ref.shape[1], 256):
            u = dot(x, w1_ref[:, n : n + 256]) + b1_ref[:, n : n + 256]
            h_ref[:, n : n + 256] = silu(u).astype(BF16)
        rows = pl.ds(pl.multiple_of(2 * start, 2 * span), 2 * span)
        out_ref[rows, :] = dot(h_ref[...], w2_ref[...]).astype(BF16)
        store(i).start()
        return carry

    lax.fori_loop(0, SEGS // span, body, 0)
    for i in range(SEGS // span):
        store(i).wait()


def chem(arrived, regrid_weights, w1, b1, w2):
    return pl.pallas_call(
        chem_kernel,
        in_specs=[VMEM] * 4 + [HBM],
        out_specs=HBM,
        out_shape=hbm_out((CELLS, w2.shape[1]), BF16),
        scratch_shapes=[
            pltpu.VMEM((8, SEGS), jnp.int32),
            pltpu.VMEM((CELLS, LANES), BF16),
            pltpu.VMEM((2 * SPAN, FEAT // 2), BF16),
            pltpu.VMEM((2 * SPAN, w1.shape[1]), BF16),
            pltpu.VMEM((CELLS, w2.shape[1]), BF16),
            pltpu.VMEM(w2.shape, BF16),
            pltpu.SemaphoreType.DMA((SEGS // SPAN,)),
            pltpu.SemaphoreType.DMA((1,)),
        ],
        compiler_params=params(20),
        cost_estimate=cost(4_400_000_000, 4 << 20),
        name="chem",
    )(
        in_vmem(arrived),
        in_vmem(regrid_weights.reshape(CELLS, LANES)),
        in_vmem(w1),
        b1,
        in_hbm(w2),
    )


def rows_up(x):
    count = lax.axis_size("gx")
    return lax.ppermute(x, "gx", [(i, (i + 1) % count) for i in range(count)])


def rows_down(x):
    count = lax.axis_size("gx")
    return lax.ppermute(x, "gx", [((i + 1) % count, i) for i in range(count)])


def columns_right(x):
    count = lax.axis_size("gy")
    return lax.ppermute(x, "gy", [(i, (i + 1) % count) for i in range(count)])


def columns_left(x):
    count = lax.axis_size("gy")
    return lax.ppermute(x, "gy", [((i + 1) % count, i) for i in range(count)])


def local(
    fields, courant, sun_columns, rad_w1, rad_b1, rad_w2, rad_b2, rad_w3,
    segment_route, regrid_weights, chem_w1, chem_b1, chem_w2,
):
    weights = (rad_w1, rad_b1.reshape(1, -1), rad_w2, rad_b2.reshape(1, -1), rad_w3)

    state, speeds, row_lo, row_hi, col_lo, col_hi = turn(fields, courant)
    halo = (rows_up(row_hi), rows_down(row_lo), columns_right(col_hi), columns_left(col_lo))
    mask, place, tags = plan(sun_columns, segment_route)
    target = piece(0, state, speeds, mask, weights)
    state, speeds, target, row_lo, row_hi, col_lo, col_hi = rim(
        state, speeds, mask, halo, weights, target
    )
    halo = (rows_up(row_hi), rows_down(row_lo), columns_right(col_hi), columns_left(col_lo))
    target = piece(1, state, speeds, mask, weights, target)
    state, packed = final(target, speeds, mask, halo, weights, place, tags)
    tiles = lax.axis_size("gx") * lax.axis_size("gy")
    packed = packed.reshape(tiles, SEGS // tiles, packed.shape[1])
    arrived = lax.all_to_all(packed, ("gx", "gy"), split_axis=0, concat_axis=0, tiled=True)
    fields_out = unturn(state).reshape(fields.shape)
    output = chem(
        arrived.reshape(SEGS, arrived.shape[2]), regrid_weights, chem_w1, chem_b1.reshape(1, -1), chem_w2
    )
    return fields_out, output.reshape(1, 1, CELLS, -1)


def solution(mesh):
    return jax.shard_map(
        local,
        mesh=mesh,
        in_specs=(
            P(None, None, "gx", "gy"),
            P(None, None, "gx", "gy"),
            P("gx", "gy", None),
            P(),
            P(),
            P(),
            P(),
            P(),
            P(None, "gx", "gy", None),
            P("gx", "gy", None, None, None),
            P(),
            P(),
            P(),
        ),
        out_specs=(P(None, None, "gx", "gy"), P("gx", "gy", None, None)),
        check_vma=False,
    )
```

```python
import jax
import jax.numpy as jnp
from jax import lax
from jax.experimental import pallas as pl
from jax.experimental.pallas import tpu as pltpu
from jax.sharding import PartitionSpec as P

F32 = jnp.float32
BF16 = jnp.bfloat16
LANES = 128
FIELDS = 4
ROWS = 16
COLS = 128
FEAT = FIELDS * LANES
CELLS = ROWS * COLS
SEGS = CELLS // 2
EDGE = 8
GROUP = 8
SPAN = 512
PIECES = ((1, 6), (7, 8))
INNER = COLS - 2 * EDGE
RIM = 2 * COLS + (ROWS - 2) * 2 * EDGE
MARGIN = (ROWS + 2, COLS + 2 * EDGE, LANES)
MIB = 1024 * 1024

VMEM = pl.BlockSpec(memory_space=pltpu.VMEM)
SMEM = pl.BlockSpec(memory_space=pltpu.SMEM)
ANY = pl.BlockSpec(memory_space=pl.ANY)


HBM = pl.BlockSpec(memory_space=pltpu.HBM)


def vmem_out(shape, dtype):
    return pltpu.VMEM(shape, dtype)


def hbm_out(shape, dtype):
    return pltpu.HBM(shape, dtype)


def in_vmem(x):
    return pltpu.with_memory_space_constraint(x, pltpu.VMEM)


def in_hbm(x):
    return pltpu.with_memory_space_constraint(x, pltpu.HBM)


def params(mib):
    return pltpu.CompilerParams(vmem_limit_bytes=mib * MIB)


def cost(flops, bytes_accessed=0):
    return pl.CostEstimate(flops=flops, bytes_accessed=bytes_accessed, transcendentals=0)


def dot(a, b):
    return jnp.dot(a, b, preferred_element_type=F32)


def dot_nt(a, b):
    return lax.dot_general(a, b, (((1,), (1,)), ((), ())), preferred_element_type=F32)


def silu(u):
    half = 0.5 * u
    return half + half * jnp.tanh(half)


def iota(shape, dim):
    return lax.broadcasted_iota(jnp.int32, shape, dim)


def one_hot(rows, wanted):
    short = jnp.broadcast_to(wanted, (16, wanted.shape[1])).astype(jnp.int16)[0:1]
    match = lax.broadcasted_iota(jnp.int16, (rows, wanted.shape[1]), 0) == short
    return jnp.where(match, jnp.ones((), BF16), jnp.zeros((), BF16))


def turn_kernel(f_hbm, c_hbm, t_ref, cc_ref, row_lo_ref, row_hi_ref, col_lo_ref, col_hi_ref, f_ref, c_ref, sems):
    size = LANES * ROWS
    inside = slice(EDGE, EDGE + COLS)
    loads = [
        pltpu.make_async_copy(f_hbm.at[pl.ds(i * size, size)], f_ref.at[i], sems.at[i])
        for i in range(FIELDS)
    ]
    loads += [
        pltpu.make_async_copy(c_hbm.at[pl.ds(i * size, size)], c_ref.at[i], sems.at[FIELDS + i])
        for i in range(2)
    ]
    for load in loads:
        load.start()

    def plane(source, i, target):
        for r in range(ROWS):
            target[i, r + 1, inside, :] = source[i, pl.ds(r, LANES, stride=ROWS), :].T

    for i in range(FIELDS):
        loads[i].wait()
        plane(f_ref, i, t_ref)
        at = slice(i * LANES, (i + 1) * LANES)
        row_lo_ref[:, at] = t_ref[i, 1, inside, :].astype(BF16)
        row_hi_ref[:, at] = t_ref[i, ROWS, inside, :].astype(BF16)
        col_lo_ref[:, at] = t_ref[i, 1 : ROWS + 1, EDGE].astype(BF16)
        col_hi_ref[:, at] = t_ref[i, 1 : ROWS + 1, EDGE + COLS - 1].astype(BF16)
    at = slice(FEAT, FEAT + LANES)
    for i in range(2):
        loads[FIELDS + i].wait()
        plane(c_ref, i, cc_ref)
    row_lo_ref[:, at] = cc_ref[0, 1, inside, :].astype(BF16)
    row_hi_ref[:, at] = cc_ref[0, ROWS, inside, :].astype(BF16)
    col_lo_ref[:, at] = cc_ref[1, 1 : ROWS + 1, EDGE].astype(BF16)
    col_hi_ref[:, at] = cc_ref[1, 1 : ROWS + 1, EDGE + COLS - 1].astype(BF16)


def turn(fields, courant):
    flat_f = in_hbm(fields.reshape(FIELDS * LANES * ROWS, COLS))
    flat_c = in_hbm(courant.reshape(2 * LANES * ROWS, COLS))
    return pl.pallas_call(
        turn_kernel,
        in_specs=[HBM] * 2,
        out_specs=[VMEM] * 6,
        out_shape=[
            vmem_out((FIELDS, *MARGIN), F32),
            vmem_out((2, *MARGIN), F32),
            jax.ShapeDtypeStruct((COLS, FEAT + LANES), BF16),
            jax.ShapeDtypeStruct((COLS, FEAT + LANES), BF16),
            jax.ShapeDtypeStruct((ROWS, FEAT + LANES), BF16),
            jax.ShapeDtypeStruct((ROWS, FEAT + LANES), BF16),
        ],
        scratch_shapes=[
            pltpu.VMEM((FIELDS, LANES * ROWS, COLS), F32),
            pltpu.VMEM((2, LANES * ROWS, COLS), F32),
            pltpu.SemaphoreType.DMA((FIELDS + 2,)),
        ],
        compiler_params=params(14),
        cost_estimate=cost(4_000_000_000, 12 << 20),
        name="turn",
    )(flat_f, flat_c)


def plan_kernel(sun_ref, route_ref, mask_ref, place_ref, tags_ref):
    slots = sun_ref[...]
    low = one_hot(COLS, slots & (COLS - 1))
    high = one_hot(LANES, slots >> 7)
    lit = dot_nt(low, high)
    for r in range(ROWS):
        mask_ref[r] = jnp.broadcast_to(lit[:, r : r + 1], (COLS, LANES))

    target = route_ref[0, 0]
    arrival = route_ref[1, 0] + 1
    before = (iota((LANES, LANES), 0) < iota((LANES, LANES), 1)).astype(F32).astype(BF16)
    ones = jnp.ones((LANES, LANES), BF16)
    carry = jnp.zeros((LANES, LANES), F32)
    ranks = []
    for b in range(SEGS // LANES):
        goes = (iota((LANES, LANES), 0) == target[:, b * LANES : (b + 1) * LANES]).astype(F32)
        goes16 = goes.astype(BF16)
        ranks.append(jnp.sum(goes * (dot(goes16, before) + carry), axis=0, keepdims=True))
        carry = carry + dot(goes16, ones)
    rank = jnp.concatenate(ranks, axis=1).astype(jnp.int32)
    row = target * 16 + rank
    halves = [jnp.where((row & 1) == q, row >> 1, -1) for q in range(2)]
    index = iota((LANES, SEGS), 0)
    coarse = (arrival >> 5).astype(F32)
    fine = (arrival & 31).astype(F32)
    tag_rows = [
        jnp.where(index == 2 * q, coarse, jnp.where(index == 2 * q + 1, fine, 0.0)).astype(BF16)
        for q in range(2)
    ]
    for b in range(SEGS // LANES):
        tags = jnp.zeros((LANES, LANES), F32)
        for q in range(2):
            chosen = one_hot(LANES, halves[q] - b * LANES)
            place_ref[q, b * LANES : (b + 1) * LANES, :] = chosen
            tags = tags + dot_nt(chosen, tag_rows[q])
        tags_ref[b * LANES : (b + 1) * LANES, :] = tags.astype(BF16)


def plan(sun_columns, segment_route):
    return pl.pallas_call(
        plan_kernel,
        in_specs=[VMEM] * 2,
        out_specs=[VMEM] * 3,
        out_shape=[
            vmem_out((ROWS, COLS, LANES), F32),
            vmem_out((2, SEGS, SEGS), BF16),
            vmem_out((SEGS, LANES), BF16),
        ],
        compiler_params=params(10),
        cost_estimate=cost(3_000_000_000, 1 << 20),
        name="plan",
    )(sun_columns.reshape(1, CELLS), segment_route)


def weights_of(lo0, mid0, hi0, left1, mid1, right1):
    f_lo = 0.5 * (lo0 + mid0)
    f_hi = 0.5 * (mid0 + hi0)
    g_lo = 0.5 * (left1 + mid1)
    g_hi = 0.5 * (mid1 + right1)
    keep = (
        1.0
        - jnp.maximum(f_hi, 0.0)
        + jnp.minimum(f_lo, 0.0)
        - jnp.maximum(g_hi, 0.0)
        + jnp.minimum(g_lo, 0.0)
    )
    return (
        keep,
        jnp.maximum(f_lo, 0.0),
        -jnp.minimum(f_hi, 0.0),
        jnp.maximum(g_lo, 0.0),
        -jnp.minimum(g_hi, 0.0),
    )


def combine(k, mid, lo, hi, left, right):
    return k[0] * mid + k[1] * lo + k[2] * hi + k[3] * left + k[4] * right


def net(x, h1_ref, h2_ref, w1_ref, b1_ref, w2_ref, b2_ref, w3_ref, emit):
    hidden = w2_ref.shape[0]
    wide = 256
    for n in range(0, hidden, wide):
        u = dot(x, w1_ref[:, n : n + wide]) + b1_ref[:, n : n + wide]
        h1_ref[:, n : n + wide] = silu(u).astype(BF16)
    h1 = h1_ref[...]
    for n in range(0, hidden, wide):
        u = dot(h1, w2_ref[:, n : n + wide]) + b2_ref[:, n : n + wide]
        h2_ref[:, n : n + wide] = silu(u).astype(BF16)
    h2 = h2_ref[...]
    for n in range(0, FEAT, wide):
        emit(n, dot(h2, w3_ref[:, n : n + wide]))


def sides(first, count):
    return (
        slice(first, first + count), slice(first - 1, first + count - 1), slice(first + 1, first + count + 1)
    )


def fill_halo(v_ref, row_lo_ref, row_hi_ref, col_lo_ref, col_hi_ref):
    inside = slice(EDGE, EDGE + COLS)
    for f in range(FIELDS):
        at = slice(f * LANES, (f + 1) * LANES)
        v_ref[f, 0, inside, :] = row_lo_ref[:, at].astype(F32)
        v_ref[f, ROWS + 1, inside, :] = row_hi_ref[:, at].astype(F32)
        low = col_lo_ref[:, at].astype(F32)
        high = col_hi_ref[:, at].astype(F32)
        for r in range(ROWS):
            v_ref[f, r + 1, EDGE - 1 : EDGE, :] = low[r : r + 1, :]
            v_ref[f, r + 1, EDGE + COLS : EDGE + COLS + 1, :] = high[r : r + 1, :]


def fill_speed_halo(c_ref, row_lo_ref, row_hi_ref, col_lo_ref, col_hi_ref):
    inside = slice(EDGE, EDGE + COLS)
    at = slice(FEAT, FEAT + LANES)
    low = col_lo_ref[:, at].astype(F32)
    high = col_hi_ref[:, at].astype(F32)
    for r in range(ROWS):
        c_ref[1, r + 1, EDGE - 1 : EDGE, :] = low[r : r + 1, :]
        c_ref[1, r + 1, EDGE + COLS : EDGE + COLS + 1, :] = high[r : r + 1, :]
    for spot, held, halo_ref, flag in (
        (0, 1, row_lo_ref, lax.axis_index("gx") > 0),
        (ROWS + 1, ROWS, row_hi_ref, lax.axis_index("gx") < lax.axis_size("gx") - 1),
    ):
        halo = halo_ref[:, at].astype(F32)
        c_ref[0, spot, inside, :] = jnp.where(flag, halo, -c_ref[0, held, inside, :])


def advect_into(v_ref, c_ref, r, pick, x_ref, adv_ref, here):
    def read(ref, f, row, which):
        parts = [ref[f, row, at, :] for at in pick[which]]
        return parts[0] if len(parts) == 1 else jnp.concatenate(parts, axis=0)

    k = weights_of(
        read(c_ref, 0, r - 1, 0), read(c_ref, 0, r, 0), read(c_ref, 0, r + 1, 0),
        read(c_ref, 1, r, 1), read(c_ref, 1, r, 0), read(c_ref, 1, r, 2),
    )
    for f in range(FIELDS):
        at = slice(f * LANES, (f + 1) * LANES)
        moved = combine(
            k, read(v_ref, f, r, 0), read(v_ref, f, r - 1, 0), read(v_ref, f, r + 1, 0),
            read(v_ref, f, r, 1), read(v_ref, f, r, 2),
        )
        adv_ref[here, at] = moved
        x_ref[here, at] = moved.astype(BF16)


def rim_kernel(
    mask_ref, row_lo_ref, row_hi_ref, col_lo_ref, col_hi_ref,
    w1_ref, b1_ref, w2_ref, b2_ref, w3_ref, _v, _c, _out,
    v_ref, c_ref, out_ref, row_lo_out, row_hi_out, col_lo_out, col_hi_out,
    x_ref, adv_ref, h1_ref, h2_ref,
):
    halo = (row_lo_ref, row_hi_ref, col_lo_ref, col_hi_ref)
    fill_halo(v_ref, *halo)
    fill_speed_halo(c_ref, *halo)
    whole = [[at] for at in sides(EDGE, COLS)]
    edge = [list(pair) for pair in zip(sides(EDGE, EDGE), sides(COLS, EDGE))]
    places = []
    for r, spot in ((1, 0), (ROWS, COLS)):
        advect_into(v_ref, c_ref, r, whole, x_ref, adv_ref, slice(spot, spot + COLS))
        places.append((r, slice(EDGE, EDGE + COLS), slice(spot, spot + COLS)))

    def edge_row(i, carry):
        spot = pl.multiple_of(2 * COLS + i * 2 * EDGE, 2 * EDGE)
        advect_into(v_ref, c_ref, i + 2, edge, x_ref, adv_ref, pl.ds(spot, 2 * EDGE))
        return carry

    lax.fori_loop(0, ROWS - 2, edge_row, 0)
    for r in range(2, ROWS):
        spot = 2 * COLS + (r - 2) * 2 * EDGE
        places.append((r, slice(EDGE, 2 * EDGE), slice(spot, spot + EDGE)))
        places.append((r, slice(COLS, COLS + EDGE), slice(spot + EDGE, spot + 2 * EDGE)))

    def emit(n, heat):
        for m in range(0, heat.shape[1], LANES):
            at = slice(n + m, n + m + LANES)
            for r, columns, here in places:
                lit = mask_ref[r - 1, columns.start - EDGE : columns.stop - EDGE, :]
                out_ref[(n + m) // LANES, r, columns, :] = (
                    adv_ref[here, at] + lit * heat[here, m : m + LANES]
                )

    net(x_ref[...], h1_ref, h2_ref, w1_ref, b1_ref, w2_ref, b2_ref, w3_ref, emit)
    for f in range(FIELDS):
        at = slice(f * LANES, (f + 1) * LANES)
        row_lo_out[:, at] = out_ref[f, 1, EDGE : EDGE + COLS, :].astype(BF16)
        row_hi_out[:, at] = out_ref[f, ROWS, EDGE : EDGE + COLS, :].astype(BF16)
        col_lo_out[:, at] = out_ref[f, 1 : ROWS + 1, EDGE].astype(BF16)
        col_hi_out[:, at] = out_ref[f, 1 : ROWS + 1, EDGE + COLS - 1].astype(BF16)


def held_weights(weights):
    return tuple(in_vmem(w) if w.dtype == BF16 else w for w in weights)


def net_scratch(many, hidden):
    return [
        pltpu.VMEM((many, FEAT), BF16),
        pltpu.VMEM((many, FEAT), F32),
        pltpu.VMEM((many, hidden), BF16),
        pltpu.VMEM((many, hidden), BF16),
    ]


def rim(state, speeds, mask, halo, weights, target):
    near = (in_vmem(mask), *halo, *held_weights(weights))
    return pl.pallas_call(
        rim_kernel,
        in_specs=[VMEM] * (len(near) + 3),
        out_specs=[VMEM] * 7,
        out_shape=[
            vmem_out((FIELDS, *MARGIN), F32),
            vmem_out((2, *MARGIN), F32),
            vmem_out((FIELDS, *MARGIN), F32),
            *[jax.ShapeDtypeStruct((COLS, FEAT), BF16)] * 2,
            *[jax.ShapeDtypeStruct((ROWS, FEAT), BF16)] * 2,
        ],
        input_output_aliases={len(near) + i: i for i in range(3)},
        scratch_shapes=net_scratch(RIM, weights[2].shape[0]),
        compiler_params=params(10),
        cost_estimate=cost(3_000_000_000, 4 << 20),
        name="rim",
    )(*near, in_vmem(state), in_vmem(speeds), in_vmem(target))


def piece_kernel(
    number, v_ref, c_ref, mask_ref, w1_ref, b1_ref, w2_ref, b2_ref, w3_ref, *rest
):
    out_ref, x_ref, adv_ref, h1_ref, h2_ref = rest[-5:]
    first, count = PIECES[number]
    pick = [[at] for at in sides(2 * EDGE, INNER)]
    for j in range(count):
        here = slice(j * INNER, (j + 1) * INNER)
        advect_into(v_ref, c_ref, first + j + 1, pick, x_ref, adv_ref, here)

    def emit(n, heat):
        for j in range(count):
            here = slice(j * INNER, (j + 1) * INNER)
            lit = mask_ref[first + j, EDGE : EDGE + INNER, :]
            for m in range(0, heat.shape[1], LANES):
                out_ref[(n + m) // LANES, first + j + 1, 2 * EDGE : 2 * EDGE + INNER, :] = (
                    adv_ref[here, n + m : n + m + LANES] + lit * heat[here, m : m + LANES]
                )

    net(x_ref[...], h1_ref, h2_ref, w1_ref, b1_ref, w2_ref, b2_ref, w3_ref, emit)


def piece(number, state, speeds, mask, weights, target=None):
    near = (in_vmem(state), in_vmem(speeds), in_vmem(mask), *held_weights(weights))
    if target is not None:
        near += (in_vmem(target),)
    return pl.pallas_call(
        lambda *refs: piece_kernel(number, *refs),
        in_specs=[VMEM] * len(near),
        out_specs=VMEM,
        out_shape=vmem_out((FIELDS, *MARGIN), F32),
        input_output_aliases={} if target is None else {len(near) - 1: 0},
        scratch_shapes=net_scratch(PIECES[number][1] * INNER, weights[2].shape[0]),
        compiler_params=params(12),
        cost_estimate=cost(2_000_000_000 * (1 + 2 * number), 1 << 20),
        name=f"piece_{number}",
    )(*near)


def final_kernel(
    c_ref, mask_ref, row_lo_ref, row_hi_ref, col_lo_ref, col_hi_ref,
    w1_ref, b1_ref, w2_ref, b2_ref, w3_ref, place_ref, tags_ref, _,
    v_ref, out_hbm, pack_hbm, out_ref, pack_ref, x_ref, adv_ref, h1_ref, h2_ref, out_sems, pack_sems,
):
    fill_halo(v_ref, row_lo_ref, row_hi_ref, col_lo_ref, col_hi_ref)
    pick = [[at] for at in sides(EDGE, COLS)]

    def store(g):
        rows = pl.ds(g * GROUP, GROUP)
        return pltpu.make_async_copy(out_ref.at[:, rows], out_hbm.at[:, rows], out_sems.at[g])

    def body(g, carry):
        for j in range(GROUP):
            here = slice(j * COLS, (j + 1) * COLS)
            advect_into(v_ref, c_ref, g * GROUP + j + 1, pick, x_ref, adv_ref, here)

        def emit(n, heat):
            for j in range(GROUP):
                r = g * GROUP + j
                here = slice(j * COLS, (j + 1) * COLS)
                for m in range(0, heat.shape[1], LANES):
                    out_ref[(n + m) // LANES, r] = (
                        adv_ref[here, n + m : n + m + LANES] + mask_ref[r] * heat[here, m : m + LANES]
                    )

        net(x_ref[...], h1_ref, h2_ref, w1_ref, b1_ref, w2_ref, b2_ref, w3_ref, emit)
        store(g).start()
        return carry

    lax.fori_loop(0, ROWS // GROUP, body, 0)
    stores = [store(g) for g in range(ROWS // GROUP)]
    flat = out_ref.reshape(FIELDS * CELLS, LANES)
    half = FEAT // 2
    columns = [
        jnp.concatenate(
            [flat[pl.ds(f * CELLS + c, SEGS, stride=2), :] for f in (2, 3)], axis=1
        ).astype(BF16)
        for c in range(2)
    ]
    pack_ref[:, 2 * FEAT :] = tags_ref[...]
    for i, b in enumerate(range(0, SEGS, 256)):
        for q in range(2):
            for c in range(2):
                pack_ref[b : b + 256, q * FEAT + c * half : q * FEAT + (c + 1) * half] = dot(
                    place_ref[q, b : b + 256, :], columns[c]
                ).astype(BF16)
        at = pl.ds(b, 256)
        stores.append(pltpu.make_async_copy(pack_ref.at[at], pack_hbm.at[at], pack_sems.at[i]))
        stores[-1].start()
    for copy in stores:
        copy.wait()


def final(state, speeds, mask, halo, weights, place, tags):
    near = (
        in_vmem(speeds), in_vmem(mask), *halo, *held_weights(weights), in_vmem(place), in_vmem(tags),
        in_vmem(state),
    )
    _, out, packed = pl.pallas_call(
        final_kernel,
        in_specs=[VMEM] * len(near),
        out_specs=[VMEM, HBM, HBM],
        out_shape=[
            vmem_out((FIELDS, *MARGIN), F32),
            hbm_out((FIELDS, ROWS, COLS, LANES), F32),
            hbm_out((SEGS, 2 * FEAT + LANES), BF16),
        ],
        input_output_aliases={len(near) - 1: 0},
        scratch_shapes=[
            pltpu.VMEM((FIELDS, ROWS, COLS, LANES), F32),
            pltpu.VMEM((SEGS, 2 * FEAT + LANES), BF16),
            *net_scratch(GROUP * COLS, weights[2].shape[0]),
            pltpu.SemaphoreType.DMA((ROWS // GROUP,)),
            pltpu.SemaphoreType.DMA((SEGS // 256,)),
        ],
        compiler_params=params(24),
        cost_estimate=cost(12_000_000_000, 4 << 20),
        name="final",
    )(*near)
    return out, packed


def unturn_kernel(t_hbm, out_ref, t_ref, stage_ref, in_sems, sems):
    size = LANES * ROWS
    loads = [pltpu.make_async_copy(t_hbm.at[f], t_ref.at[f], in_sems.at[f]) for f in range(FIELDS)]
    stores = [
        pltpu.make_async_copy(stage_ref.at[f], out_ref.at[pl.ds(f * size, size)], sems.at[f])
        for f in range(FIELDS)
    ]
    for load in loads:
        load.start()
    for f in range(FIELDS):
        loads[f].wait()
        for r in range(ROWS):
            stage_ref[f, pl.ds(r, LANES, stride=ROWS), :] = t_ref[f, r].T
        stores[f].start()
    for store in stores:
        store.wait()


def unturn(state):
    return pl.pallas_call(
        unturn_kernel,
        in_specs=[HBM],
        out_specs=HBM,
        out_shape=hbm_out((FIELDS * LANES * ROWS, COLS), F32),
        scratch_shapes=[
            pltpu.VMEM((FIELDS, ROWS, COLS, LANES), F32),
            pltpu.VMEM((FIELDS, LANES * ROWS, COLS), F32),
            pltpu.SemaphoreType.DMA((FIELDS,)),
            pltpu.SemaphoreType.DMA((FIELDS,)),
        ],
        compiler_params=params(12),
        cost_estimate=cost(1_000_000_000, 8 << 20),
        name="unturn",
    )(in_hbm(state))


def chem_kernel(
    arr_ref, regrid_ref, w1_ref, b1_ref, w2_hbm, out_hbm,
    want_ref, mix_ref, x_ref, h_ref, out_ref, w2_ref, sems, w_sem,
):
    w2_load = pltpu.make_async_copy(w2_hbm, w2_ref, w_sem.at[0])
    w2_load.start()
    from_cell = iota((LANES, LANES), 0)
    to_lane = iota((LANES, LANES), 1)
    source_cell = jnp.where(to_lane < 64, 2 * to_lane, 2 * (to_lane - 64) + 1)
    split = (from_cell == source_cell).astype(F32).astype(BF16)
    mix_ref[...] = dot(regrid_ref[...], split).astype(BF16)
    lane = iota((8, LANES), 1)
    which = iota((8, LANES), 0)
    pick = jnp.where(lane == 2 * which, 32.0, jnp.where(lane == 2 * which + 1, 1.0, 0.0))
    pick = jnp.where(which < 2, pick, 0.0).astype(BF16)
    want_ref[...] = dot_nt(pick, arr_ref[:, 2 * FEAT :]).astype(jnp.int32) - 1
    span = SPAN
    half = FEAT // 2
    w2_load.wait()

    def store(i):
        at = pl.ds(pl.multiple_of(2 * span * i, 2 * span), 2 * span)
        return pltpu.make_async_copy(out_ref.at[at], out_hbm.at[at], sems.at[i])

    def body(i, carry):
        start = i * span
        placed = []
        for q in range(2):
            chosen = (iota((span, SEGS), 0) + start == want_ref[q : q + 1, :]).astype(F32).astype(BF16)
            placed.append(dot(chosen, arr_ref[:, q * FEAT : (q + 1) * FEAT]))
        placed = (placed[0] + placed[1]).astype(BF16)
        for b in range(span // 64):
            cells = jnp.concatenate(
                [placed[b * 64 : (b + 1) * 64, :half], placed[b * 64 : (b + 1) * 64, half:]], axis=0
            )
            spot = pl.multiple_of(2 * start + b * LANES, LANES)
            x_ref[b * LANES : (b + 1) * LANES, :] = dot(mix_ref[pl.ds(spot, LANES), :], cells).astype(BF16)
        x = x_ref[...]
        for n in range(0, w1_ref.shape[1], 256):
            u = dot(x, w1_ref[:, n : n + 256]) + b1_ref[:, n : n + 256]
            h_ref[:, n : n + 256] = silu(u).astype(BF16)
        rows = pl.ds(pl.multiple_of(2 * start, 2 * span), 2 * span)
        out_ref[rows, :] = dot(h_ref[...], w2_ref[...]).astype(BF16)
        store(i).start()
        return carry

    lax.fori_loop(0, SEGS // span, body, 0)
    for i in range(SEGS // span):
        store(i).wait()


def chem(arrived, regrid_weights, w1, b1, w2):
    return pl.pallas_call(
        chem_kernel,
        in_specs=[VMEM] * 4 + [HBM],
        out_specs=HBM,
        out_shape=hbm_out((CELLS, w2.shape[1]), BF16),
        scratch_shapes=[
            pltpu.VMEM((8, SEGS), jnp.int32),
            pltpu.VMEM((CELLS, LANES), BF16),
            pltpu.VMEM((2 * SPAN, FEAT // 2), BF16),
            pltpu.VMEM((2 * SPAN, w1.shape[1]), BF16),
            pltpu.VMEM((CELLS, w2.shape[1]), BF16),
            pltpu.VMEM(w2.shape, BF16),
            pltpu.SemaphoreType.DMA((SEGS // SPAN,)),
            pltpu.SemaphoreType.DMA((1,)),
        ],
        compiler_params=params(20),
        cost_estimate=cost(4_400_000_000, 4 << 20),
        name="chem",
    )(
        in_vmem(arrived),
        in_vmem(regrid_weights.reshape(CELLS, LANES)),
        in_vmem(w1),
        b1,
        in_hbm(w2),
    )


def rows_up(x):
    count = lax.axis_size("gx")
    return lax.ppermute(x, "gx", [(i, (i + 1) % count) for i in range(count)])


def rows_down(x):
    count = lax.axis_size("gx")
    return lax.ppermute(x, "gx", [((i + 1) % count, i) for i in range(count)])


def columns_right(x):
    count = lax.axis_size("gy")
    return lax.ppermute(x, "gy", [(i, (i + 1) % count) for i in range(count)])


def columns_left(x):
    count = lax.axis_size("gy")
    return lax.ppermute(x, "gy", [((i + 1) % count, i) for i in range(count)])


def local(
    fields, courant, sun_columns, rad_w1, rad_b1, rad_w2, rad_b2, rad_w3,
    segment_route, regrid_weights, chem_w1, chem_b1, chem_w2,
):
    weights = (rad_w1, rad_b1.reshape(1, -1), rad_w2, rad_b2.reshape(1, -1), rad_w3)

    state, speeds, row_lo, row_hi, col_lo, col_hi = turn(fields, courant)
    halo = (rows_up(row_hi), rows_down(row_lo), columns_right(col_hi), columns_left(col_lo))
    mask, place, tags = plan(sun_columns, segment_route)
    target = piece(0, state, speeds, mask, weights)
    state, speeds, target, row_lo, row_hi, col_lo, col_hi = rim(
        state, speeds, mask, halo, weights, target
    )
    halo = (rows_up(row_hi), rows_down(row_lo), columns_right(col_hi), columns_left(col_lo))
    target = piece(1, state, speeds, mask, weights, target)
    state, packed = final(target, speeds, mask, halo, weights, place, tags)
    tiles = lax.axis_size("gx") * lax.axis_size("gy")
    packed = packed.reshape(tiles, SEGS // tiles, packed.shape[1])
    arrived = lax.all_to_all(packed, ("gx", "gy"), split_axis=0, concat_axis=0, tiled=True)
    fields_out = unturn(state).reshape(fields.shape)
    output = chem(
        arrived.reshape(SEGS, arrived.shape[2]), regrid_weights, chem_w1, chem_b1.reshape(1, -1), chem_w2
    )
    return fields_out, output.reshape(1, 1, CELLS, -1)


def solution(mesh):
    return jax.shard_map(
        local,
        mesh=mesh,
        in_specs=(
            P(None, None, "gx", "gy"),
            P(None, None, "gx", "gy"),
            P("gx", "gy", None),
            P(),
            P(),
            P(),
            P(),
            P(),
            P(None, "gx", "gy", None),
            P("gx", "gy", None, None, None),
            P(),
            P(),
            P(),
        ),
        out_specs=(P(None, None, "gx", "gy"), P("gx", "gy", None, None)),
        check_vma=False,
    )
```

```python
import jax
import jax.numpy as jnp
from jax import lax
from jax.experimental import pallas as pl
from jax.experimental.pallas import tpu as pltpu
from jax.sharding import PartitionSpec as P

F32 = jnp.float32
BF16 = jnp.bfloat16
LANES = 128
FIELDS = 4
ROWS = 16
COLS = 128
FEAT = FIELDS * LANES
CELLS = ROWS * COLS
SEGS = CELLS // 2
EDGE = 8
GROUP = 8
SPAN = 512
PIECES = ((1, 6), (7, 8))
INNER = COLS - 2 * EDGE
RIM = 2 * COLS + (ROWS - 2) * 2 * EDGE
MARGIN = (ROWS + 2, COLS + 2 * EDGE, LANES)
MIB = 1024 * 1024

VMEM = pl.BlockSpec(memory_space=pltpu.VMEM)
SMEM = pl.BlockSpec(memory_space=pltpu.SMEM)
ANY = pl.BlockSpec(memory_space=pl.ANY)


HBM = pl.BlockSpec(memory_space=pltpu.HBM)


def vmem_out(shape, dtype):
    return pltpu.VMEM(shape, dtype)


def hbm_out(shape, dtype):
    return pltpu.HBM(shape, dtype)


def in_vmem(x):
    return pltpu.with_memory_space_constraint(x, pltpu.VMEM)


def in_hbm(x):
    return pltpu.with_memory_space_constraint(x, pltpu.HBM)


def params(mib):
    return pltpu.CompilerParams(vmem_limit_bytes=mib * MIB)


def cost(flops, bytes_accessed=0):
    return pl.CostEstimate(flops=flops, bytes_accessed=bytes_accessed, transcendentals=0)


def dot(a, b):
    return jnp.dot(a, b, preferred_element_type=F32)


def dot_nt(a, b):
    return lax.dot_general(a, b, (((1,), (1,)), ((), ())), preferred_element_type=F32)


def silu(u):
    half = 0.5 * u
    return half + half * jnp.tanh(half)


def iota(shape, dim):
    return lax.broadcasted_iota(jnp.int32, shape, dim)


def one_hot(rows, wanted):
    short = jnp.broadcast_to(wanted, (16, wanted.shape[1])).astype(jnp.int16)[0:1]
    match = lax.broadcasted_iota(jnp.int16, (rows, wanted.shape[1]), 0) == short
    return jnp.where(match, jnp.ones((), BF16), jnp.zeros((), BF16))


def turn_kernel(f_hbm, c_hbm, t_ref, cc_ref, row_lo_ref, row_hi_ref, col_lo_ref, col_hi_ref, f_ref, c_ref, sems):
    size = LANES * ROWS
    inside = slice(EDGE, EDGE + COLS)
    loads = [
        pltpu.make_async_copy(f_hbm.at[pl.ds(i * size, size)], f_ref.at[i], sems.at[i])
        for i in range(FIELDS)
    ]
    loads += [
        pltpu.make_async_copy(c_hbm.at[pl.ds(i * size, size)], c_ref.at[i], sems.at[FIELDS + i])
        for i in range(2)
    ]
    for load in loads:
        load.start()

    def plane(source, i, target):
        for r in range(ROWS):
            target[i, r + 1, inside, :] = source[i, pl.ds(r, LANES, stride=ROWS), :].T

    for i in range(FIELDS):
        loads[i].wait()
        plane(f_ref, i, t_ref)
        at = slice(i * LANES, (i + 1) * LANES)
        row_lo_ref[:, at] = t_ref[i, 1, inside, :].astype(BF16)
        row_hi_ref[:, at] = t_ref[i, ROWS, inside, :].astype(BF16)
        col_lo_ref[:, at] = t_ref[i, 1 : ROWS + 1, EDGE].astype(BF16)
        col_hi_ref[:, at] = t_ref[i, 1 : ROWS + 1, EDGE + COLS - 1].astype(BF16)
    at = slice(FEAT, FEAT + LANES)
    for i in range(2):
        loads[FIELDS + i].wait()
        plane(c_ref, i, cc_ref)
    row_lo_ref[:, at] = cc_ref[0, 1, inside, :].astype(BF16)
    row_hi_ref[:, at] = cc_ref[0, ROWS, inside, :].astype(BF16)
    col_lo_ref[:, at] = cc_ref[1, 1 : ROWS + 1, EDGE].astype(BF16)
    col_hi_ref[:, at] = cc_ref[1, 1 : ROWS + 1, EDGE + COLS - 1].astype(BF16)


def turn(fields, courant):
    flat_f = in_hbm(fields.reshape(FIELDS * LANES * ROWS, COLS))
    flat_c = in_hbm(courant.reshape(2 * LANES * ROWS, COLS))
    return pl.pallas_call(
        turn_kernel,
        in_specs=[HBM] * 2,
        out_specs=[VMEM] * 6,
        out_shape=[
            vmem_out((FIELDS, *MARGIN), F32),
            vmem_out((2, *MARGIN), F32),
            jax.ShapeDtypeStruct((COLS, FEAT + LANES), BF16),
            jax.ShapeDtypeStruct((COLS, FEAT + LANES), BF16),
            jax.ShapeDtypeStruct((ROWS, FEAT + LANES), BF16),
            jax.ShapeDtypeStruct((ROWS, FEAT + LANES), BF16),
        ],
        scratch_shapes=[
            pltpu.VMEM((FIELDS, LANES * ROWS, COLS), F32),
            pltpu.VMEM((2, LANES * ROWS, COLS), F32),
            pltpu.SemaphoreType.DMA((FIELDS + 2,)),
        ],
        compiler_params=params(14),
        cost_estimate=cost(4_000_000_000, 12 << 20),
        name="turn",
    )(flat_f, flat_c)


def plan_kernel(sun_ref, route_ref, mask_ref, place_ref, tags_ref):
    slots = sun_ref[...]
    low = one_hot(COLS, slots & (COLS - 1))
    high = one_hot(LANES, slots >> 7)
    lit = dot_nt(low, high)
    for r in range(ROWS):
        mask_ref[r] = jnp.broadcast_to(lit[:, r : r + 1], (COLS, LANES))

    target = route_ref[0, 0]
    arrival = route_ref[1, 0] + 1
    before = (iota((LANES, LANES), 0) < iota((LANES, LANES), 1)).astype(F32).astype(BF16)
    ones = jnp.ones((LANES, LANES), BF16)
    carry = jnp.zeros((LANES, LANES), F32)
    ranks = []
    for b in range(SEGS // LANES):
        goes = (iota((LANES, LANES), 0) == target[:, b * LANES : (b + 1) * LANES]).astype(F32)
        goes16 = goes.astype(BF16)
        ranks.append(jnp.sum(goes * (dot(goes16, before) + carry), axis=0, keepdims=True))
        carry = carry + dot(goes16, ones)
    rank = jnp.concatenate(ranks, axis=1).astype(jnp.int32)
    row = target * 16 + rank
    halves = [jnp.where((row & 1) == q, row >> 1, -1) for q in range(2)]
    index = iota((LANES, SEGS), 0)
    coarse = (arrival >> 5).astype(F32)
    fine = (arrival & 31).astype(F32)
    tag_rows = [
        jnp.where(index == 2 * q, coarse, jnp.where(index == 2 * q + 1, fine, 0.0)).astype(BF16)
        for q in range(2)
    ]
    for b in range(SEGS // LANES):
        tags = jnp.zeros((LANES, LANES), F32)
        for q in range(2):
            chosen = one_hot(LANES, halves[q] - b * LANES)
            place_ref[q, b * LANES : (b + 1) * LANES, :] = chosen
            tags = tags + dot_nt(chosen, tag_rows[q])
        tags_ref[b * LANES : (b + 1) * LANES, :] = tags.astype(BF16)


def plan(sun_columns, segment_route):
    return pl.pallas_call(
        plan_kernel,
        in_specs=[VMEM] * 2,
        out_specs=[VMEM] * 3,
        out_shape=[
            vmem_out((ROWS, COLS, LANES), F32),
            vmem_out((2, SEGS, SEGS), BF16),
            vmem_out((SEGS, LANES), BF16),
        ],
        compiler_params=params(10),
        cost_estimate=cost(300_000_000, 1 << 20),
        name="plan",
    )(sun_columns.reshape(1, CELLS), segment_route)


def weights_of(lo0, mid0, hi0, left1, mid1, right1):
    f_lo = 0.5 * (lo0 + mid0)
    f_hi = 0.5 * (mid0 + hi0)
    g_lo = 0.5 * (left1 + mid1)
    g_hi = 0.5 * (mid1 + right1)
    keep = (
        1.0
        - jnp.maximum(f_hi, 0.0)
        + jnp.minimum(f_lo, 0.0)
        - jnp.maximum(g_hi, 0.0)
        + jnp.minimum(g_lo, 0.0)
    )
    return (
        keep,
        jnp.maximum(f_lo, 0.0),
        -jnp.minimum(f_hi, 0.0),
        jnp.maximum(g_lo, 0.0),
        -jnp.minimum(g_hi, 0.0),
    )


def combine(k, mid, lo, hi, left, right):
    return k[0] * mid + k[1] * lo + k[2] * hi + k[3] * left + k[4] * right


def net(x, h1_ref, h2_ref, w1_ref, b1_ref, w2_ref, b2_ref, w3_ref, emit):
    hidden = w2_ref.shape[0]
    wide = 256
    for n in range(0, hidden, wide):
        u = dot(x, w1_ref[:, n : n + wide]) + b1_ref[:, n : n + wide]
        h1_ref[:, n : n + wide] = silu(u).astype(BF16)
    h1 = h1_ref[...]
    for n in range(0, hidden, wide):
        u = dot(h1, w2_ref[:, n : n + wide]) + b2_ref[:, n : n + wide]
        h2_ref[:, n : n + wide] = silu(u).astype(BF16)
    h2 = h2_ref[...]
    for n in range(0, FEAT, wide):
        emit(n, dot(h2, w3_ref[:, n : n + wide]))


def sides(first, count):
    return (
        slice(first, first + count), slice(first - 1, first + count - 1), slice(first + 1, first + count + 1)
    )


def fill_halo(v_ref, row_lo_ref, row_hi_ref, col_lo_ref, col_hi_ref):
    inside = slice(EDGE, EDGE + COLS)
    for f in range(FIELDS):
        at = slice(f * LANES, (f + 1) * LANES)
        v_ref[f, 0, inside, :] = row_lo_ref[:, at].astype(F32)
        v_ref[f, ROWS + 1, inside, :] = row_hi_ref[:, at].astype(F32)
        low = col_lo_ref[:, at].astype(F32)
        high = col_hi_ref[:, at].astype(F32)
        for r in range(ROWS):
            v_ref[f, r + 1, EDGE - 1 : EDGE, :] = low[r : r + 1, :]
            v_ref[f, r + 1, EDGE + COLS : EDGE + COLS + 1, :] = high[r : r + 1, :]


def fill_speed_halo(c_ref, row_lo_ref, row_hi_ref, col_lo_ref, col_hi_ref):
    inside = slice(EDGE, EDGE + COLS)
    at = slice(FEAT, FEAT + LANES)
    low = col_lo_ref[:, at].astype(F32)
    high = col_hi_ref[:, at].astype(F32)
    for r in range(ROWS):
        c_ref[1, r + 1, EDGE - 1 : EDGE, :] = low[r : r + 1, :]
        c_ref[1, r + 1, EDGE + COLS : EDGE + COLS + 1, :] = high[r : r + 1, :]
    for spot, held, halo_ref, flag in (
        (0, 1, row_lo_ref, lax.axis_index("gx") > 0),
        (ROWS + 1, ROWS, row_hi_ref, lax.axis_index("gx") < lax.axis_size("gx") - 1),
    ):
        halo = halo_ref[:, at].astype(F32)
        c_ref[0, spot, inside, :] = jnp.where(flag, halo, -c_ref[0, held, inside, :])


def advect_into(v_ref, c_ref, r, pick, x_ref, adv_ref, here):
    def read(ref, f, row, which):
        parts = [ref[f, row, at, :] for at in pick[which]]
        return parts[0] if len(parts) == 1 else jnp.concatenate(parts, axis=0)

    k = weights_of(
        read(c_ref, 0, r - 1, 0), read(c_ref, 0, r, 0), read(c_ref, 0, r + 1, 0),
        read(c_ref, 1, r, 1), read(c_ref, 1, r, 0), read(c_ref, 1, r, 2),
    )
    for f in range(FIELDS):
        at = slice(f * LANES, (f + 1) * LANES)
        moved = combine(
            k, read(v_ref, f, r, 0), read(v_ref, f, r - 1, 0), read(v_ref, f, r + 1, 0),
            read(v_ref, f, r, 1), read(v_ref, f, r, 2),
        )
        adv_ref[here, at] = moved
        x_ref[here, at] = moved.astype(BF16)


def rim_kernel(
    mask_ref, row_lo_ref, row_hi_ref, col_lo_ref, col_hi_ref,
    w1_ref, b1_ref, w2_ref, b2_ref, w3_ref, _v, _c, _out,
    v_ref, c_ref, out_ref, row_lo_out, row_hi_out, col_lo_out, col_hi_out,
    x_ref, adv_ref, h1_ref, h2_ref,
):
    halo = (row_lo_ref, row_hi_ref, col_lo_ref, col_hi_ref)
    fill_halo(v_ref, *halo)
    fill_speed_halo(c_ref, *halo)
    whole = [[at] for at in sides(EDGE, COLS)]
    edge = [list(pair) for pair in zip(sides(EDGE, EDGE), sides(COLS, EDGE))]
    places = []
    for r, spot in ((1, 0), (ROWS, COLS)):
        advect_into(v_ref, c_ref, r, whole, x_ref, adv_ref, slice(spot, spot + COLS))
        places.append((r, slice(EDGE, EDGE + COLS), slice(spot, spot + COLS)))

    def edge_row(i, carry):
        spot = pl.multiple_of(2 * COLS + i * 2 * EDGE, 2 * EDGE)
        advect_into(v_ref, c_ref, i + 2, edge, x_ref, adv_ref, pl.ds(spot, 2 * EDGE))
        return carry

    lax.fori_loop(0, ROWS - 2, edge_row, 0)
    for r in range(2, ROWS):
        spot = 2 * COLS + (r - 2) * 2 * EDGE
        places.append((r, slice(EDGE, 2 * EDGE), slice(spot, spot + EDGE)))
        places.append((r, slice(COLS, COLS + EDGE), slice(spot + EDGE, spot + 2 * EDGE)))

    def emit(n, heat):
        for m in range(0, heat.shape[1], LANES):
            at = slice(n + m, n + m + LANES)
            for r, columns, here in places:
                lit = mask_ref[r - 1, columns.start - EDGE : columns.stop - EDGE, :]
                out_ref[(n + m) // LANES, r, columns, :] = (
                    adv_ref[here, at] + lit * heat[here, m : m + LANES]
                )

    net(x_ref[...], h1_ref, h2_ref, w1_ref, b1_ref, w2_ref, b2_ref, w3_ref, emit)
    for f in range(FIELDS):
        at = slice(f * LANES, (f + 1) * LANES)
        row_lo_out[:, at] = out_ref[f, 1, EDGE : EDGE + COLS, :].astype(BF16)
        row_hi_out[:, at] = out_ref[f, ROWS, EDGE : EDGE + COLS, :].astype(BF16)
        col_lo_out[:, at] = out_ref[f, 1 : ROWS + 1, EDGE].astype(BF16)
        col_hi_out[:, at] = out_ref[f, 1 : ROWS + 1, EDGE + COLS - 1].astype(BF16)


def held_weights(weights):
    return tuple(in_vmem(w) if w.dtype == BF16 else w for w in weights)


def net_scratch(many, hidden):
    return [
        pltpu.VMEM((many, FEAT), BF16),
        pltpu.VMEM((many, FEAT), F32),
        pltpu.VMEM((many, hidden), BF16),
        pltpu.VMEM((many, hidden), BF16),
    ]


def rim(state, speeds, mask, halo, weights, target):
    near = (in_vmem(mask), *halo, *held_weights(weights))
    return pl.pallas_call(
        rim_kernel,
        in_specs=[VMEM] * (len(near) + 3),
        out_specs=[VMEM] * 7,
        out_shape=[
            vmem_out((FIELDS, *MARGIN), F32),
            vmem_out((2, *MARGIN), F32),
            vmem_out((FIELDS, *MARGIN), F32),
            *[jax.ShapeDtypeStruct((COLS, FEAT), BF16)] * 2,
            *[jax.ShapeDtypeStruct((ROWS, FEAT), BF16)] * 2,
        ],
        input_output_aliases={len(near) + i: i for i in range(3)},
        scratch_shapes=net_scratch(RIM, weights[2].shape[0]),
        compiler_params=params(10),
        cost_estimate=cost(3_000_000_000, 4 << 20),
        name="rim",
    )(*near, in_vmem(state), in_vmem(speeds), in_vmem(target))


def piece_kernel(
    number, v_ref, c_ref, mask_ref, w1_ref, b1_ref, w2_ref, b2_ref, w3_ref, *rest
):
    out_ref, x_ref, adv_ref, h1_ref, h2_ref = rest[-5:]
    first, count = PIECES[number]
    pick = [[at] for at in sides(2 * EDGE, INNER)]
    for j in range(count):
        here = slice(j * INNER, (j + 1) * INNER)
        advect_into(v_ref, c_ref, first + j + 1, pick, x_ref, adv_ref, here)

    def emit(n, heat):
        for j in range(count):
            here = slice(j * INNER, (j + 1) * INNER)
            lit = mask_ref[first + j, EDGE : EDGE + INNER, :]
            for m in range(0, heat.shape[1], LANES):
                out_ref[(n + m) // LANES, first + j + 1, 2 * EDGE : 2 * EDGE + INNER, :] = (
                    adv_ref[here, n + m : n + m + LANES] + lit * heat[here, m : m + LANES]
                )

    net(x_ref[...], h1_ref, h2_ref, w1_ref, b1_ref, w2_ref, b2_ref, w3_ref, emit)


def piece(number, state, speeds, mask, weights, target=None):
    near = (in_vmem(state), in_vmem(speeds), in_vmem(mask), *held_weights(weights))
    if target is not None:
        near += (in_vmem(target),)
    return pl.pallas_call(
        lambda *refs: piece_kernel(number, *refs),
        in_specs=[VMEM] * len(near),
        out_specs=VMEM,
        out_shape=vmem_out((FIELDS, *MARGIN), F32),
        input_output_aliases={} if target is None else {len(near) - 1: 0},
        scratch_shapes=net_scratch(PIECES[number][1] * INNER, weights[2].shape[0]),
        compiler_params=params(12),
        cost_estimate=cost(2_000_000_000 * (1 + 2 * number), 1 << 20),
        name=f"piece_{number}",
    )(*near)


def final_kernel(
    c_ref, mask_ref, row_lo_ref, row_hi_ref, col_lo_ref, col_hi_ref,
    w1_ref, b1_ref, w2_ref, b2_ref, w3_ref, place_ref, tags_ref, _,
    v_ref, out_hbm, pack_hbm, out_ref, pack_ref, x_ref, adv_ref, h1_ref, h2_ref, out_sems, pack_sems,
):
    fill_halo(v_ref, row_lo_ref, row_hi_ref, col_lo_ref, col_hi_ref)
    pick = [[at] for at in sides(EDGE, COLS)]

    def store(g):
        rows = pl.ds(g * GROUP, GROUP)
        return pltpu.make_async_copy(out_ref.at[:, rows], out_hbm.at[:, rows], out_sems.at[g])

    def body(g, carry):
        for j in range(GROUP):
            here = slice(j * COLS, (j + 1) * COLS)
            advect_into(v_ref, c_ref, g * GROUP + j + 1, pick, x_ref, adv_ref, here)

        def emit(n, heat):
            for j in range(GROUP):
                r = g * GROUP + j
                here = slice(j * COLS, (j + 1) * COLS)
                for m in range(0, heat.shape[1], LANES):
                    out_ref[(n + m) // LANES, r] = (
                        adv_ref[here, n + m : n + m + LANES] + mask_ref[r] * heat[here, m : m + LANES]
                    )

        net(x_ref[...], h1_ref, h2_ref, w1_ref, b1_ref, w2_ref, b2_ref, w3_ref, emit)
        store(g).start()
        return carry

    lax.fori_loop(0, ROWS // GROUP, body, 0)
    stores = [store(g) for g in range(ROWS // GROUP)]
    flat = out_ref.reshape(FIELDS * CELLS, LANES)
    half = FEAT // 2
    columns = [
        jnp.concatenate(
            [flat[pl.ds(f * CELLS + c, SEGS, stride=2), :] for f in (2, 3)], axis=1
        ).astype(BF16)
        for c in range(2)
    ]
    pack_ref[:, 2 * FEAT :] = tags_ref[...]
    for i, b in enumerate(range(0, SEGS, 256)):
        for q in range(2):
            for c in range(2):
                pack_ref[b : b + 256, q * FEAT + c * half : q * FEAT + (c + 1) * half] = dot(
                    place_ref[q, b : b + 256, :], columns[c]
                ).astype(BF16)
        at = pl.ds(b, 256)
        stores.append(pltpu.make_async_copy(pack_ref.at[at], pack_hbm.at[at], pack_sems.at[i]))
        stores[-1].start()
    for copy in stores:
        copy.wait()


def final(state, speeds, mask, halo, weights, place, tags):
    near = (
        in_vmem(speeds), in_vmem(mask), *halo, *held_weights(weights), in_vmem(place), in_vmem(tags),
        in_vmem(state),
    )
    _, out, packed = pl.pallas_call(
        final_kernel,
        in_specs=[VMEM] * len(near),
        out_specs=[VMEM, HBM, HBM],
        out_shape=[
            vmem_out((FIELDS, *MARGIN), F32),
            hbm_out((FIELDS, ROWS, COLS, LANES), F32),
            hbm_out((SEGS, 2 * FEAT + LANES), BF16),
        ],
        input_output_aliases={len(near) - 1: 0},
        scratch_shapes=[
            pltpu.VMEM((FIELDS, ROWS, COLS, LANES), F32),
            pltpu.VMEM((SEGS, 2 * FEAT + LANES), BF16),
            *net_scratch(GROUP * COLS, weights[2].shape[0]),
            pltpu.SemaphoreType.DMA((ROWS // GROUP,)),
            pltpu.SemaphoreType.DMA((SEGS // 256,)),
        ],
        compiler_params=params(24),
        cost_estimate=cost(12_000_000_000, 4 << 20),
        name="final",
    )(*near)
    return out, packed


def unturn_kernel(t_hbm, out_ref, t_ref, stage_ref, in_sems, sems):
    size = LANES * ROWS
    loads = [pltpu.make_async_copy(t_hbm.at[f], t_ref.at[f], in_sems.at[f]) for f in range(FIELDS)]
    stores = [
        pltpu.make_async_copy(stage_ref.at[f], out_ref.at[pl.ds(f * size, size)], sems.at[f])
        for f in range(FIELDS)
    ]
    for load in loads:
        load.start()
    for f in range(FIELDS):
        loads[f].wait()
        for r in range(ROWS):
            stage_ref[f, pl.ds(r, LANES, stride=ROWS), :] = t_ref[f, r].T
        stores[f].start()
    for store in stores:
        store.wait()


def unturn(state):
    return pl.pallas_call(
        unturn_kernel,
        in_specs=[HBM],
        out_specs=HBM,
        out_shape=hbm_out((FIELDS * LANES * ROWS, COLS), F32),
        scratch_shapes=[
            pltpu.VMEM((FIELDS, ROWS, COLS, LANES), F32),
            pltpu.VMEM((FIELDS, LANES * ROWS, COLS), F32),
            pltpu.SemaphoreType.DMA((FIELDS,)),
            pltpu.SemaphoreType.DMA((FIELDS,)),
        ],
        compiler_params=params(12),
        cost_estimate=cost(1_000_000_000, 8 << 20),
        name="unturn",
    )(in_hbm(state))


def chem_kernel(
    arr_ref, regrid_ref, w1_ref, b1_ref, w2_hbm, out_hbm,
    want_ref, mix_ref, x_ref, h_ref, out_ref, w2_ref, sems, w_sem,
):
    w2_load = pltpu.make_async_copy(w2_hbm, w2_ref, w_sem.at[0])
    w2_load.start()
    from_cell = iota((LANES, LANES), 0)
    to_lane = iota((LANES, LANES), 1)
    source_cell = jnp.where(to_lane < 64, 2 * to_lane, 2 * (to_lane - 64) + 1)
    split = (from_cell == source_cell).astype(F32).astype(BF16)
    mix_ref[...] = dot(regrid_ref[...], split).astype(BF16)
    lane = iota((8, LANES), 1)
    which = iota((8, LANES), 0)
    pick = jnp.where(lane == 2 * which, 32.0, jnp.where(lane == 2 * which + 1, 1.0, 0.0))
    pick = jnp.where(which < 2, pick, 0.0).astype(BF16)
    want_ref[...] = dot_nt(pick, arr_ref[:, 2 * FEAT :]).astype(jnp.int32) - 1
    span = SPAN
    half = FEAT // 2
    w2_load.wait()

    def store(i):
        at = pl.ds(pl.multiple_of(2 * span * i, 2 * span), 2 * span)
        return pltpu.make_async_copy(out_ref.at[at], out_hbm.at[at], sems.at[i])

    def body(i, carry):
        start = i * span
        placed = []
        for q in range(2):
            chosen = (iota((span, SEGS), 0) + start == want_ref[q : q + 1, :]).astype(F32).astype(BF16)
            placed.append(dot(chosen, arr_ref[:, q * FEAT : (q + 1) * FEAT]))
        placed = (placed[0] + placed[1]).astype(BF16)
        for b in range(span // 64):
            cells = jnp.concatenate(
                [placed[b * 64 : (b + 1) * 64, :half], placed[b * 64 : (b + 1) * 64, half:]], axis=0
            )
            spot = pl.multiple_of(2 * start + b * LANES, LANES)
            x_ref[b * LANES : (b + 1) * LANES, :] = dot(mix_ref[pl.ds(spot, LANES), :], cells).astype(BF16)
        x = x_ref[...]
        for n in range(0, w1_ref.shape[1], 256):
            u = dot(x, w1_ref[:, n : n + 256]) + b1_ref[:, n : n + 256]
            h_ref[:, n : n + 256] = silu(u).astype(BF16)
        rows = pl.ds(pl.multiple_of(2 * start, 2 * span), 2 * span)
        out_ref[rows, :] = dot(h_ref[...], w2_ref[...]).astype(BF16)
        store(i).start()
        return carry

    lax.fori_loop(0, SEGS // span, body, 0)
    for i in range(SEGS // span):
        store(i).wait()


def chem(arrived, regrid_weights, w1, b1, w2):
    return pl.pallas_call(
        chem_kernel,
        in_specs=[VMEM] * 4 + [HBM],
        out_specs=HBM,
        out_shape=hbm_out((CELLS, w2.shape[1]), BF16),
        scratch_shapes=[
            pltpu.VMEM((8, SEGS), jnp.int32),
            pltpu.VMEM((CELLS, LANES), BF16),
            pltpu.VMEM((2 * SPAN, FEAT // 2), BF16),
            pltpu.VMEM((2 * SPAN, w1.shape[1]), BF16),
            pltpu.VMEM((CELLS, w2.shape[1]), BF16),
            pltpu.VMEM(w2.shape, BF16),
            pltpu.SemaphoreType.DMA((SEGS // SPAN,)),
            pltpu.SemaphoreType.DMA((1,)),
        ],
        compiler_params=params(20),
        cost_estimate=cost(4_400_000_000, 4 << 20),
        name="chem",
    )(
        in_vmem(arrived),
        in_vmem(regrid_weights.reshape(CELLS, LANES)),
        in_vmem(w1),
        b1,
        in_hbm(w2),
    )


def rows_up(x):
    count = lax.axis_size("gx")
    return lax.ppermute(x, "gx", [(i, (i + 1) % count) for i in range(count)])


def rows_down(x):
    count = lax.axis_size("gx")
    return lax.ppermute(x, "gx", [((i + 1) % count, i) for i in range(count)])


def columns_right(x):
    count = lax.axis_size("gy")
    return lax.ppermute(x, "gy", [(i, (i + 1) % count) for i in range(count)])


def columns_left(x):
    count = lax.axis_size("gy")
    return lax.ppermute(x, "gy", [((i + 1) % count, i) for i in range(count)])


def local(
    fields, courant, sun_columns, rad_w1, rad_b1, rad_w2, rad_b2, rad_w3,
    segment_route, regrid_weights, chem_w1, chem_b1, chem_w2,
):
    weights = (rad_w1, rad_b1.reshape(1, -1), rad_w2, rad_b2.reshape(1, -1), rad_w3)

    state, speeds, row_lo, row_hi, col_lo, col_hi = turn(fields, courant)
    halo = (rows_up(row_hi), rows_down(row_lo), columns_right(col_hi), columns_left(col_lo))
    mask, place, tags = plan(sun_columns, segment_route)
    target = piece(0, state, speeds, mask, weights)
    state, speeds, target, row_lo, row_hi, col_lo, col_hi = rim(
        state, speeds, mask, halo, weights, target
    )
    halo = (rows_up(row_hi), rows_down(row_lo), columns_right(col_hi), columns_left(col_lo))
    target = piece(1, state, speeds, mask, weights, target)
    state, packed = final(target, speeds, mask, halo, weights, place, tags)
    tiles = lax.axis_size("gx") * lax.axis_size("gy")
    packed = packed.reshape(tiles, SEGS // tiles, packed.shape[1])
    arrived = lax.all_to_all(packed, ("gx", "gy"), split_axis=0, concat_axis=0, tiled=True)
    fields_out = unturn(state).reshape(fields.shape)
    output = chem(
        arrived.reshape(SEGS, arrived.shape[2]), regrid_weights, chem_w1, chem_b1.reshape(1, -1), chem_w2
    )
    return fields_out, output.reshape(1, 1, CELLS, -1)


def solution(mesh):
    return jax.shard_map(
        local,
        mesh=mesh,
        in_specs=(
            P(None, None, "gx", "gy"),
            P(None, None, "gx", "gy"),
            P("gx", "gy", None),
            P(),
            P(),
            P(),
            P(),
            P(),
            P(None, "gx", "gy", None),
            P("gx", "gy", None, None, None),
            P(),
            P(),
            P(),
        ),
        out_specs=(P(None, None, "gx", "gy"), P("gx", "gy", None, None)),
        check_vma=False,
    )
```
